512 devices in a mesh: state: 64 (over z, y), seq: 8 (over x, core).
Axes of the slice: x: 4, y: 8, z: 8, core: 2. Of those that a mesh axis runs over, the one named last changes fastest.
Arguments:
- emit_states: bfloat16 [32768, 512], P('state'), may hold values from -7 to 7
- trans_out: bfloat16 [32768, 512], P('state'), may hold values from -7 to 7
- trans_in: bfloat16 [32768, 512], P('state'), may hold values from -0.25 to 0.25
- word_emb: bfloat16 [131072, 512], P('state'), may hold values from -0.25 to 0.25
- word_cluster: int32 [131072], replicated, may hold values from 0 to 127, as said below
- cluster_block: int32 [128], replicated, may hold values from 0 to 127, as said below
- kept_parts: int32 [128, 2], replicated, may hold values from 0 to 7, as said below
- tokens: int32 [512, 128], P(('state', 'seq')), may hold values from 0 to 131071, as said below
Outputs:
- token_loglik: float32 [512], P(('state', 'seq'))
- trans_norm: float32 [8192], P('state')
- emit_norm: float32 [8192], P('state')
The draws below stay inside these ranges and needn't reach their ends.
Inputs may be any that keep to these rules, and one draw needn't show every extreme that they name: `word_cluster`: within each shard of 2048 consecutive words every cluster holds at least 2 and at most 24 words, and some cluster holds exactly 24. `cluster_block`: A permutation of the blocks. `kept_parts`: each row holds 2 different parts in increasing order. Of the 128 tokens of one device, at most 2 have their word in the clusters of one block, and some block has exactly 2.
All inputs are finite; a program needn't handle non-finite values.
Results may differ from the reference program's by a relative error of at most 0.0003.
Values may be sent and summed in bfloat16 or wider, within the bound.
No kernel may reach another device: no remote copies, remote signals or barrier semaphores. Data moves between devices by JAX's collectives and lax.ppermute only.
A program may use at most 64 MiB of HBM per device.

```python
import jax
import jax.numpy as jnp
import numpy as np
from jax import lax

E = 512
BS = 256
PART = 32
KP = 2
V_DEV = 2048
LEN = 128
SUB_DEV = 1
NB = 128
STATES = 32768
VOCAB = 131072
NSUB = 512
CAP_W = 24
CAP_T = 2
N_STATE = 64
N_SEQ = 8


def ramp_counts(mean_count, most_count, kinds):
    half_kinds = kinds // 2
    lower = np.arange(half_kinds)
    shift = (kinds - 1 - 2 * lower) * (most_count - mean_count) // (kinds - 1)
    return np.concatenate([mean_count + shift, mean_count - shift[::-1]]).astype(np.int32)


def spread_labels(key, counts, total, kinds):
    first_key, second_key = jax.random.split(key)
    labels = jnp.repeat(jax.random.permutation(first_key, kinds).astype(jnp.int32), jnp.asarray(counts), total_repeat_length=total)
    return jax.random.permutation(second_key, labels)


def shared_clusters(key):
    key = jax.random.fold_in(key, 501)
    counts = ramp_counts(V_DEV // NB, CAP_W, NB)
    keys = jax.random.split(key, N_STATE)
    return jax.vmap(lambda one_key: spread_labels(one_key, counts, V_DEV, NB))(keys).reshape(-1).astype(jnp.int32)


def shared_blocks(key):
    return jax.random.permutation(jax.random.fold_in(key, 502), NB).astype(jnp.int32)


def draw_emit_states(key, part):
    key = jax.random.fold_in(key, 7)
    base_key = jax.random.fold_in(key, 0)
    values = jnp.clip(jax.random.normal(base_key, (STATES, E), jnp.float32), -6.0, 6.0)
    return values.astype(jnp.bfloat16)


def draw_trans_out(key, part):
    key = jax.random.fold_in(key, 8)
    base_key = jax.random.fold_in(key, 0)
    values = jnp.clip(jax.random.normal(base_key, (STATES, E), jnp.float32), -6.0, 6.0)
    return values.astype(jnp.bfloat16)


def draw_word_cluster(key, part):
    return shared_clusters(key)


def draw_cluster_block(key, part):
    return shared_blocks(key)


def draw_kept_parts(key, part):
    key = jax.random.fold_in(key, 9)
    keys = jax.random.split(key, NB)
    chosen = jax.vmap(lambda one_key: jax.random.permutation(one_key, BS // PART)[:KP])(keys)
    return jnp.sort(chosen, axis=1).astype(jnp.int32)


def draw_tokens(key, part):
    clusters = shared_clusters(key)
    blocks = shared_blocks(key)
    key = jax.random.fold_in(key, 13)
    label_key, word_key = jax.random.split(key)
    per_device = SUB_DEV * LEN
    counts = ramp_counts(per_device // NB, CAP_T, NB)
    keys = jax.random.split(label_key, N_STATE * N_SEQ)
    token_blocks = jax.vmap(lambda one_key: spread_labels(one_key, counts, per_device, NB))(keys).reshape(-1)
    cluster_of_block = jnp.zeros((NB,), jnp.int32).at[blocks].set(jnp.arange(NB, dtype=jnp.int32))
    token_clusters = cluster_of_block[token_blocks]
    sorted_words = jnp.argsort(clusters, stable=True).astype(jnp.int32)
    sizes = jnp.bincount(clusters, length=NB).astype(jnp.int32)
    starts_of = jnp.cumsum(sizes) - sizes
    offsets = jax.random.randint(word_key, token_clusters.shape, 0, sizes[token_clusters])
    return sorted_words[starts_of[token_clusters] + offsets].reshape(NSUB, LEN).astype(jnp.int32)


def levels(key, extent, cuts, least, top_value):
    loudness, own = 1.0, jax.random.fold_in(key, 6)
    for dim, blocks in cuts:
        draws = jnp.exp(jax.random.uniform(jax.random.fold_in(own, dim), (blocks,), jnp.float32, least / len(cuts), top_value / len(cuts)))
        loudness = loudness * jnp.repeat(draws, extent[dim] // blocks).reshape([-1 if axis == dim else 1 for axis in range(len(extent))])
    return loudness


def gaussian(rng, extent, width, most, shards=(), kind=jnp.bfloat16):
    loudness = levels(rng, extent, shards, -0.22, 0.18) if shards else 1.0
    drawn = jax.random.normal(rng, extent, jnp.float32) * width * loudness
    return jnp.minimum(jnp.maximum(drawn, -most), most).astype(kind)


def setup_inputs(seed: int = 0) -> dict:
    seeds = jax.random.split(jax.random.key(seed), 9)
    return {
        "emit_states": draw_emit_states(jax.random.fold_in(seeds[8], 71), 0),
        "trans_out": draw_trans_out(jax.random.fold_in(seeds[8], 71), 0),
        "trans_in": gaussian(seeds[2], (STATES, E), E ** -0.5, 0.25, ((0, 64),)),
        "word_emb": gaussian(seeds[3], (VOCAB, E), E ** -0.5, 0.25, ((0, 64),)),
        "word_cluster": draw_word_cluster(jax.random.fold_in(seeds[8], 71), 0),
        "cluster_block": draw_cluster_block(jax.random.fold_in(seeds[8], 71), 0),
        "kept_parts": draw_kept_parts(jax.random.fold_in(seeds[8], 71), 0),
        "tokens": draw_tokens(jax.random.fold_in(seeds[8], 71), 0),
    }


def kept_states(kept_parts):
    block_total = kept_parts.shape[0]
    starts_of = jnp.arange(block_total, dtype=jnp.int32)[:, None, None] * BS
    within = kept_parts[:, :, None] * PART + jnp.arange(PART, dtype=jnp.int32)[None, None, :]
    return (starts_of + within).reshape(-1).astype(jnp.int32)


def reference(emit_states, trans_out, trans_in, word_emb, word_cluster, cluster_block, kept_parts, tokens):
    kept_width = KP * PART
    kept_rows = kept_states(kept_parts)
    emit_kept = emit_states[kept_rows]
    out_kept = trans_out[kept_rows]
    in_kept = trans_in[kept_rows]

    def row_block(block_rows):
        scores = jnp.exp(jnp.dot(block_rows, in_kept.T, preferred_element_type=jnp.float32))
        totals = jnp.sum(scores, axis=1)
        probs = (scores / totals[:, None]).astype(jnp.bfloat16)
        return probs.reshape(kept_width, NB, kept_width).transpose(1, 0, 2), jnp.log(totals)

    panels, trans_norm = lax.map(row_block, out_kept.reshape(NB, kept_width, E))

    word_block = cluster_block[word_cluster]
    emit_blocks = emit_kept.reshape(NB, kept_width, E)

    def word_span(span_args):
        span_rows, span_blocks = span_args
        states_of = emit_blocks[span_blocks].astype(jnp.float32)
        return jnp.einsum('we,wke->wk', span_rows.astype(jnp.float32), states_of)

    word_scores = lax.map(word_span, (word_emb.reshape(-1, V_DEV, E), word_block.reshape(-1, V_DEV))).reshape(-1, kept_width)
    emit_totals = jax.ops.segment_sum(jnp.exp(word_scores), word_block, NB)
    emit_norm = jnp.log(emit_totals)

    def chain(chain_tokens):
        blocks_of = word_block[chain_tokens]
        emission = jnp.exp(word_scores[chain_tokens] - emit_norm[blocks_of]).astype(jnp.bfloat16)
        emission = lax.optimization_barrier(emission).astype(jnp.float32)
        moves = panels[blocks_of[:-1], blocks_of[1:]].astype(jnp.float32)

        def advance(carry, inputs):
            prior, acc = carry
            move, emit_row = inputs
            after = jnp.dot(prior * emit_row, move, precision=lax.Precision.HIGHEST)
            total = jnp.sum(after)
            return (after / total, acc + jnp.log(total)), None

        start = jnp.ones((kept_width,), jnp.float32)
        (prior, acc), _ = lax.scan(advance, (start, jnp.zeros((), jnp.float32)), (moves, emission[:-1]))
        final = jnp.log(jnp.sum(prior * emission[-1]))
        return (acc + final - jnp.log(jnp.asarray(NB * kept_width, jnp.float32))) / LEN

    token_loglik = lax.map(chain, tokens)
    return token_loglik, trans_norm.reshape(-1), emit_norm.reshape(-1)
```

```python
import jax
import jax.numpy as jnp
from jax import lax
from jax.experimental import pallas as pl
from jax.experimental.pallas import tpu as pltpu
from jax.sharding import PartitionSpec as P

BS = 256
PART = 32
KP = 2
KW = KP * PART
LANES = 128
RANKS = 3
f32 = jnp.float32
bf16 = jnp.bfloat16


def iota(shape, axis):
    return lax.broadcasted_iota(jnp.int32, shape, axis)


def one_hot(mask):
    return jnp.where(mask, 1.0, 0.0).astype(bf16)


def prep_kernel(
    scal_ref, emit_ref, out_ref, in_ref, word_ref, cluster_ref, table_ref,
    msg_ref, out_kept_ref, emit_kept_ref, in_kept, slot_of,
):
    share = scal_ref[4]
    for blk in range(2):
        for part in range(2):
            src = pl.ds(pl.multiple_of(blk * BS + scal_ref[blk * 2 + part] * PART, PART), PART)
            dst = pl.ds((blk * 2 + part) * PART, PART)
            emit_kept_ref[dst, :] = emit_ref[src, :]
            out_kept_ref[dst, :] = out_ref[src, :]
            in_kept[dst, :] = in_ref[src, :]
    row = iota((16, LANES), 0)
    want = ((row >> 2) & 1) * KW + (row & 3) * 16 + (row >> 3) * 8 + share
    targets = jnp.dot(
        one_hot(iota((16, LANES), 1) == want), in_kept[...], preferred_element_type=f32
    )
    sub = iota((LANES, LANES), 0)
    lane = iota((LANES, LANES), 1)
    sums = jnp.concatenate([one_hot(sub < lane), jnp.ones((LANES, LANES), bf16)], axis=1)
    table = table_ref[...].astype(f32)
    carry = jnp.zeros((LANES, LANES), f32)
    chunks = cluster_ref.shape[0]
    for c in range(chunks):
        hit = sub == cluster_ref[c : c + 1, :]
        counts = jnp.dot(one_hot(hit), sums, preferred_element_type=f32)
        before = counts[:, :LANES] + carry
        carry = carry + counts[:, LANES:]
        rank = jnp.sum(jnp.where(hit, before, 0.0), axis=0, keepdims=True).astype(jnp.int32)
        block = jnp.sum(jnp.where(hit, table, 0.0), axis=0, keepdims=True).astype(jnp.int32)
        x = rank - RANKS * share
        slot = (block >> 1) * 8 + x * 2 + (block & 1)
        slot_of[c : c + 1, :] = jnp.where((x >= 0) & (x < RANKS), slot, -1)
    for tile in range(4):
        rows = sub + tile * LANES
        chosen = jnp.concatenate(
            [one_hot(rows == slot_of[c : c + 1, :]) for c in range(chunks)], axis=1
        )
        words = jnp.dot(chosen, word_ref[...], preferred_element_type=f32)
        for d in range(16):
            both = jnp.concatenate(
                [targets[(d & 1) * 8 : (d & 1) * 8 + 8, :], words[d * 8 : d * 8 + 8, :]], axis=0
            )
            msg_ref[tile * 16 + d] = both.astype(bf16)


def prep(scal, emit_states, trans_out, trans_in, word_emb, clusters, table):
    width = emit_states.shape[1]
    vmem = pl.BlockSpec(memory_space=pltpu.VMEM)
    return pl.pallas_call(
        prep_kernel,
        out_shape=(
            jax.ShapeDtypeStruct((64, 16, width), bf16),
            jax.ShapeDtypeStruct((2 * KW, width), bf16),
            jax.ShapeDtypeStruct((2 * KW, width), bf16),
        ),
        in_specs=[pl.BlockSpec(memory_space=pltpu.SMEM)] + [vmem] * 6,
        out_specs=(vmem, vmem, vmem),
        scratch_shapes=[pltpu.VMEM((2 * KW, width), bf16), pltpu.VMEM((16, LANES), jnp.int32)],
        compiler_params=pltpu.CompilerParams(vmem_limit_bytes=40 * 1024 * 1024),
        name="prep",
    )(scal, emit_states, trans_out, trans_in, word_emb, clusters, table)


def pick_kernel(msg_ref, mat_ref, next_ref, panel_ref, z_ref, ws_ref, sa, sb, words, table):
    for tile in range(4):
        got = msg_ref[tile * 16 : tile * 16 + 16].reshape(256, msg_ref.shape[2])
        res = lax.dot_general(
            got, mat_ref[...], (((1,), (1,)), ((), ())), preferred_element_type=f32
        ).reshape(16, 16, 3 * LANES)
        rows = pl.ds(tile * LANES, LANES)
        sa[rows, :] = jnp.exp(res[:, :8, :LANES]).reshape(LANES, LANES)
        sb[rows, :] = jnp.exp(res[:, :8, LANES : 2 * LANES]).reshape(LANES, LANES)
        words[rows, :] = res[:, 8:, 2 * LANES :].reshape(LANES, LANES)
    low = iota((LANES, LANES), 1) < KW
    for part, ref in enumerate((sa, sb)):
        cols = [ref[pl.ds(j, LANES, stride=4), :] for j in range(4)]
        total = jnp.sum(cols[0] + cols[1] + cols[2] + cols[3], axis=0, keepdims=True)
        z_ref[:, part * LANES : (part + 1) * LANES] = jnp.broadcast_to(total, (8, LANES))
        for pair in range(2):
            first, second = cols[2 * pair], cols[2 * pair + 1]
            left = jnp.where(low, first, pltpu.roll(second, KW, 1))
            right = jnp.where(low, pltpu.roll(first, KW, 1), second)
            lanes = slice(pair * LANES, (pair + 1) * LANES)
            table[(2 * part) * LANES : (2 * part + 1) * LANES, lanes] = left.astype(bf16)
            table[(2 * part + 1) * LANES : (2 * part + 2) * LANES, lanes] = right.astype(bf16)
    ws_ref[...] = jnp.where(
        iota((256, LANES), 1) < KW,
        words[pl.ds(0, 256, stride=2), :],
        words[pl.ds(1, 256, stride=2), :],
    )
    eye = iota((64, 64), 0) == iota((64, 64), 1)
    ones = jnp.ones((64, LANES), bf16)
    lane = iota((512, LANES), 1).astype(f32)
    block_of = (iota((512, LANES), 0) & 7) >> 1

    def step(tile, _):
        asked = next_ref[pl.ds(pl.multiple_of(tile * 8, 8), 8), :]
        spread = jnp.concatenate(
            [jnp.where(eye, asked[d : d + 1, :64], 0.0) for d in range(8)], axis=0
        )
        wanted = jnp.dot(spread.astype(bf16), ones, preferred_element_type=f32)
        hit = wanted == lane
        chosen = jnp.concatenate([one_hot(hit & (block_of == b)) for b in range(4)], axis=1)
        got = jnp.dot(chosen, table[...], preferred_element_type=f32)
        panel_ref[pl.ds(pl.multiple_of(tile * 512, 512), 512), :] = got.astype(bf16)
        return 0

    lax.fori_loop(0, 8, step, 0)


def pick(msg, mat, next_blocks):
    vmem = pl.BlockSpec(memory_space=pltpu.VMEM)
    return pl.pallas_call(
        pick_kernel,
        out_shape=(
            jax.ShapeDtypeStruct((4096, 256), bf16),
            jax.ShapeDtypeStruct((8, 256), f32),
            jax.ShapeDtypeStruct((256, LANES), f32),
        ),
        in_specs=[vmem] * 3,
        out_specs=(vmem, vmem, vmem),
        scratch_shapes=[
            pltpu.VMEM((512, LANES), f32),
            pltpu.VMEM((512, LANES), f32),
            pltpu.VMEM((512, LANES), f32),
            pltpu.VMEM((512, 256), bf16),
        ],
        compiler_params=pltpu.CompilerParams(vmem_limit_bytes=40 * 1024 * 1024),
        name="pick",
    )(msg, mat, next_blocks)


def chain_kernel(slot_ref, panel_ref, ez_ref, out_ref, ya, yb, ge, ga, ping, pong, logs):
    length = slot_ref.shape[0]

    def widen(i, _):
        rows = pl.ds(pl.multiple_of(i * 256, 256), 256)
        got = panel_ref[rows, :].astype(f32)
        ya[rows, :] = got[:, :LANES]
        yb[rows, :] = got[:, LANES:]
        return 0

    lax.fori_loop(0, panel_ref.shape[0] // 256, widen, 0)

    def pull(i, _):
        for u in range(8):
            t = i * 8 + u
            ge[pl.ds(t, 1), :] = ez_ref[pl.ds(slot_ref[t], 1), :]
        return 0

    lax.fori_loop(0, length // 8, pull, 0)
    low = iota((length, LANES), 1) < KW
    raw = ge[...]
    peak = jnp.max(jnp.where(low, raw, -jnp.inf), axis=1, keepdims=True)
    ga[...] = jnp.exp(-0.5 * pltpu.roll(raw, KW, 1))
    ge[...] = jnp.where(low, jnp.exp(jnp.where(low, raw - peak, 0.0)), 0.0)
    shift = jnp.sum(peak, axis=0, keepdims=True)

    def build(i, _):
        for u in range(4):
            t = i * 4 + u
            slot = slot_ref[t]
            rows = pl.ds((slot >> 3) * LANES + (slot & 7), 16, stride=8)
            a, b = ya[rows, :], yb[rows, :]
            norm, emit = ga[pl.ds(t, 1), :], ge[pl.ds(t, 1), :]
            move = jnp.concatenate([a, pltpu.roll(a, KW, 1), b, pltpu.roll(b, KW, 1)], axis=0)
            ping[t] = (((move * norm) * norm) * emit).astype(bf16)
        return 0

    lax.fori_loop(0, length // 4, build, 0)
    last = ge[length - 1 : length, :]
    ping[length - 1] = jnp.where(
        iota((KW, LANES), 0) == iota((KW, LANES), 1), last, 0.0
    ).astype(bf16)

    logs[...] = jnp.ones_like(logs)
    src, dst, count, base = ping, pong, length // 2, 0
    while count >= 1:
        unroll = min(count, 8)

        def level(i, _, src=src, dst=dst, unroll=unroll, base=base):
            for u in range(unroll):
                n = i * unroll + u
                prod = jnp.dot(src[2 * n + 1][:, :KW], src[2 * n], preferred_element_type=f32)
                top = jnp.max(jnp.max(prod, axis=0, keepdims=True), axis=1, keepdims=True)
                dst[n] = (prod * (1.0 / top)).astype(bf16)
                logs[pl.ds(base + n, 1), :] = jnp.broadcast_to(top, (1, LANES))
            return 0

        lax.fori_loop(0, count // unroll, level, 0)
        src, dst, count, base = dst, src, count // 2, base + count
    final = jnp.sum(jnp.sum(src[0].astype(f32), axis=0, keepdims=True), axis=1, keepdims=True)
    scale = jnp.sum(jnp.log(logs[...]), axis=0, keepdims=True)
    out_ref[...] = jnp.broadcast_to(jnp.log(final) + shift + scale, (8, LANES))


def chain(slots, panels, ez):
    length = slots.shape[0]
    vmem = pl.BlockSpec(memory_space=pltpu.VMEM)
    return pl.pallas_call(
        chain_kernel,
        out_shape=jax.ShapeDtypeStruct((8, LANES), f32),
        in_specs=[pl.BlockSpec(memory_space=pltpu.SMEM), vmem, vmem],
        out_specs=vmem,
        scratch_shapes=[
            pltpu.VMEM((4096, LANES), f32),
            pltpu.VMEM((4096, LANES), f32),
            pltpu.VMEM((length, LANES), f32),
            pltpu.VMEM((length, LANES), f32),
            pltpu.VMEM((length, KW, LANES), bf16),
            pltpu.VMEM((length // 2, KW, LANES), bf16),
            pltpu.VMEM((length, LANES), f32),
        ],
        compiler_params=pltpu.CompilerParams(vmem_limit_bytes=40 * 1024 * 1024),
        name="chain",
    )(slots, panels, ez)


def local(
    emit_states, trans_out, trans_in, word_emb, word_cluster, cluster_block, kept_parts, tokens
):
    states = lax.axis_size("state")
    me = lax.axis_index("state")
    share = lax.axis_index("seq")
    odd = me % 2
    blocks = cluster_block.shape[0]
    all_clusters = word_cluster.reshape(states, -1)
    vocab_local = all_clusters.shape[1]
    my_parts = lax.dynamic_slice_in_dim(kept_parts, me * 2, 2, 0).reshape(-1)
    scal = jnp.concatenate([my_parts, share[None].astype(jnp.int32), jnp.zeros((3,), jnp.int32)])
    own_clusters = lax.dynamic_slice_in_dim(word_cluster, me * vocab_local, vocab_local, 0)
    msg, out_kept, emit_kept = prep(
        scal, emit_states, trans_out, trans_in, word_emb,
        own_clusters.reshape(-1, LANES), cluster_block[:, None],
    )
    arrived = lax.all_to_all(msg, "state", split_axis=0, concat_axis=0, tiled=True)
    swap = [(i, i ^ 1) for i in range(states)]
    out_other = lax.ppermute(out_kept, "state", swap)
    mat = jnp.concatenate(
        [
            jnp.where(odd == 0, out_kept, out_other),
            jnp.where(odd == 0, out_other, out_kept),
            emit_kept,
        ],
        axis=0,
    )

    flat = tokens.reshape(-1)
    length = flat.shape[0]
    shard = flat // vocab_local
    cluster = jnp.take(word_cluster, flat)
    shard_rows = jnp.take(all_clusters, shard, axis=0)
    within = flat - shard * vocab_local
    earlier = (shard_rows == cluster[:, None]) & (
        jnp.arange(vocab_local, dtype=jnp.int32)[None, :] < within[:, None]
    )
    rank = jnp.sum(earlier.astype(jnp.int32), axis=1)
    hit = cluster[:, None] == jnp.arange(blocks, dtype=jnp.int32)[None, :]
    block = jnp.sum(jnp.where(hit, cluster_block[None, :], 0), axis=1)
    times = jnp.arange(length, dtype=jnp.int32)
    same = (block[:, None] == block[None, :]) & (times[None, :] < times[:, None])
    slots = block * 2 + jnp.sum(same.astype(jnp.int32), axis=1)
    following = jnp.concatenate([block[1:], block[-1:]])
    key = (rank // RANKS) * 256 + shard * 4 + rank % RANKS
    code = following * 2048 + key
    at = slots[:, None] == jnp.arange(2 * blocks, dtype=jnp.int32)[None, :]
    request = jnp.sum(jnp.where(at, code[:, None], 0), axis=0)
    group = lax.all_gather(request, "seq", axis=0, tiled=False)
    by_pair = group.reshape(8, states // 2, 8).transpose(1, 0, 2).reshape(states // 2, 1, 64)
    asked = lax.all_to_all(
        jnp.repeat(by_pair, 2, axis=0), "state", split_axis=0, concat_axis=0, tiled=True
    )[:, 0, :]

    panels, z_part, ws = pick(arrived, mat, (asked >> 11).astype(f32))
    got = lax.all_to_all(
        panels.reshape(512, 8, 256), ("state", "seq"), split_axis=0, concat_axis=0, tiled=True
    ).reshape(4096, 256)

    z_half = lax.psum(z_part[0], "seq")
    z_all = z_half + lax.ppermute(z_half, "state", swap)
    trans_norm = jnp.log(lax.dynamic_slice_in_dim(z_all, odd * 128, 128, 0))
    my_blocks = me * 2 + jnp.arange(2, dtype=jnp.int32)
    mine = (cluster_block[None, :] == my_blocks[:, None]).astype(jnp.int32)
    my_clusters = jnp.sum(mine * jnp.arange(blocks, dtype=jnp.int32)[None, :], axis=1)
    present = jnp.sum(
        (all_clusters[None, :, :] == my_clusters[:, None, None]).astype(jnp.int32), axis=2
    )
    x = jnp.arange(4, dtype=jnp.int32)
    valid = (x[None, None, :] < RANKS) & (x[None, None, :] + RANKS * share < present[:, :, None])
    valid = jnp.broadcast_to(
        valid.reshape(2, 256).T[:, :, None], (256, 2, KW)
    ).reshape(256, LANES)
    ws = jnp.where(valid, ws, -1e30)
    ws_all = lax.all_gather(ws, "seq", axis=0, tiled=True)
    emit_norm = jnp.log(jnp.sum(jnp.exp(ws_all), axis=0))
    mine_asked = lax.dynamic_slice_in_dim(asked, share * 8 + odd * 4, 4, 1) & 2047
    rows = jnp.take(ws_all, mine_asked.reshape(-1), axis=0) - emit_norm[None, :]
    rows = rows.reshape(states, 2, 2, 2, KW)
    log_emit = jnp.stack([rows[:, 0, :, 0, :], rows[:, 1, :, 1, :]], axis=1)
    norms = jnp.broadcast_to(trans_norm.reshape(1, 2, 1, KW), log_emit.shape)
    ez = lax.all_to_all(
        jnp.concatenate([log_emit, norms], axis=3).reshape(states, 4, LANES),
        "state", split_axis=0, concat_axis=0, tiled=True,
    ).reshape(4 * states, LANES)

    total = chain(slots, got, ez)[0, :1]
    token_loglik = (total - jnp.log(jnp.asarray(KW * blocks, f32))) / length
    return (token_loglik, trans_norm, emit_norm)


def solution(mesh):
    placed = (
        P("state", None),
        P("state", None),
        P("state", None),
        P("state", None),
        P(),
        P(),
        P(),
        P(("state", "seq"), None),
    )
    return jax.shard_map(
        local,
        mesh=mesh,
        in_specs=placed,
        out_specs=(P(("state", "seq")), P("state"), P("state")),
        check_vma=False,
    )
```

```python
import jax
import jax.numpy as jnp
from jax import lax
from jax.experimental import pallas as pl
from jax.experimental.pallas import tpu as pltpu
from jax.sharding import PartitionSpec as P

BS = 256
PART = 32
KW = 64
LANES = 128
RANKS = 3
SHARDS = 64
ROWS = 24
XROWS = 208
f32 = jnp.float32
bf16 = jnp.bfloat16
i32 = jnp.int32


def iota(shape, axis):
    return lax.broadcasted_iota(i32, shape, axis)


def one_hot(mask):
    return jnp.where(mask, 1.0, 0.0).astype(bf16)


def ints(mask, value):
    return jnp.where(mask, value, 0)


def prep_kernel(
    parts_ref, token_ref, tokens_ref, cluster_ref, table_ref, emit_ref, out_ref, in_ref, word_ref,
    msg_ref, mat_ref, slot_ref, in_kept, slot_of, near, wide, counts_of,
):
    me = lax.axis_index("state")
    share = lax.axis_index("seq")
    sub = iota((LANES, LANES), 0)
    lane = iota((LANES, LANES), 1)
    eye = sub == lane

    def column(row):
        return jnp.sum(ints(eye, row), axis=1, keepdims=True)

    def line(col):
        return jnp.sum(ints(eye, col), axis=0, keepdims=True)

    for blk in range(2):
        for part in range(2):
            start = blk * BS + parts_ref[me * 2 + blk, part] * PART
            src = pl.ds(pl.multiple_of(start, PART), PART)
            at = (blk * 2 + part) * PART
            mat_ref[at : at + PART, :] = out_ref[src, :]
            mat_ref[2 * KW + at : 2 * KW + at + PART, :] = emit_ref[src, :]
            in_kept[at : at + PART, :] = in_ref[src, :]
    row = iota((16, LANES), 0)
    want = (row >> 3) * KW + (row & 3) * 16 + share * 2 + ((row >> 2) & 1)
    targets = jnp.dot(
        one_hot(iota((16, LANES), 1) == want), in_kept[...], preferred_element_type=f32
    ).astype(bf16)

    sums = jnp.concatenate([one_hot(sub < lane), jnp.ones((LANES, LANES), bf16)], axis=1)
    block_row = table_ref[...]
    block_col = column(block_row)
    block_col_f = block_col.astype(f32)
    carry = jnp.zeros((LANES, LANES), f32)
    chunks = 2048 // LANES
    own = pl.multiple_of(me * chunks, chunks)
    own_rows = cluster_ref[pl.ds(own, chunks), :]
    for c in range(chunks):
        hit = sub == own_rows[c : c + 1, :]
        found = jnp.dot(one_hot(hit), sums, preferred_element_type=f32)
        before = found[:, :LANES] + carry
        carry = carry + found[:, LANES:]
        rank = jnp.sum(jnp.where(hit, before, 0.0), axis=0, keepdims=True).astype(i32)
        block = jnp.sum(jnp.where(hit, block_col_f, 0.0), axis=0, keepdims=True).astype(i32)
        x = rank - RANKS * share
        slot = (block >> 1) * 8 + x * 2 + (block & 1)
        slot_of[c : c + 1, :] = jnp.where((x >= 0) & (x < RANKS), slot, -1)
    counts_of[...] = carry

    length = token_ref.shape[1]

    def pull(i, _):
        for u in range(8):
            t = i * 8 + u
            near[pl.ds(t, 1), :] = cluster_ref[pl.ds(token_ref[0, t] >> 7, 1), :]
        return 0

    lax.fori_loop(0, length // 8, pull, 0)
    token_col = column(tokens_ref[...])
    cluster_col = jnp.sum(ints(lane == (token_col & 127), near[...]), axis=1, keepdims=True)
    near[...] = jnp.broadcast_to(cluster_col, (LANES, LANES))
    place = iota((chunks, LANES), 0) * LANES + iota((chunks, LANES), 1)

    def tally(i, _):
        for u in range(8):
            t = i * 8 + u
            token = token_ref[0, t]
            shard_rows = cluster_ref[pl.ds(pl.multiple_of((token >> 11) * chunks, chunks), chunks), :]
            earlier = (shard_rows == near[pl.ds(t, 1), :]) & (place < (token & 2047))
            wide[pl.ds(t, 1), :] = jnp.sum(ints(earlier, 1), axis=0, keepdims=True)
        return 0

    lax.fori_loop(0, length // 8, tally, 0)
    rank_col = jnp.sum(wide[...], axis=1, keepdims=True)
    own_block_col = jnp.sum(ints(lane == cluster_col, block_row), axis=1, keepdims=True)
    own_block_row = line(own_block_col)
    same = own_block_col == own_block_row
    times_col = jnp.sum(ints(same & (lane < sub), 1), axis=1, keepdims=True)
    times_row = jnp.sum(ints(same & (sub < lane), 1), axis=0, keepdims=True)
    slot_ref[...] = (own_block_row >> 1) * 64 + (own_block_row & 1) * 2 + times_row
    following = jnp.sum(ints(lane == sub + 1, own_block_row), axis=1, keepdims=True)
    following = jnp.where(iota((LANES, 1), 0) == length - 1, LANES, following)
    slots_col = own_block_col * 2 + times_col
    asked = jnp.zeros((SHARDS, LANES), f32)
    slot_line = iota((LANES, 2 * LANES), 1)
    at_slot = slot_line == slots_col
    owner = (iota((SHARDS, 2 * LANES), 1) >> 2) == iota((SHARDS, 2 * LANES), 0)
    slot_sub = iota((2 * LANES, LANES), 0) & 3
    slot_lane = iota((2 * LANES, LANES), 1)
    for field, values in enumerate((following, token_col >> 11, rank_col)):
        value_row = jnp.sum(ints(at_slot, values), axis=0, keepdims=True)
        spread = jnp.where(owner, value_row.astype(f32), 0.0).astype(bf16)
        asked += jnp.dot(
            spread, one_hot(slot_lane == field * 4 + slot_sub), preferred_element_type=f32
        )
    count_lane = jnp.where(lane == 12 + (block_col & 1), counts_of[...], 0.0).astype(bf16)
    count_owner = one_hot((block_row >> 1) == iota((SHARDS, LANES), 0))
    asked += jnp.dot(count_owner, count_lane, preferred_element_type=f32)

    request_row = iota((8, LANES), 0) == 6
    for tile in range(4):
        rows = sub + tile * LANES
        chosen = jnp.concatenate(
            [one_hot(rows == slot_of[c : c + 1, :]) for c in range(chunks)], axis=1
        )
        words = jnp.dot(chosen, word_ref[...], preferred_element_type=f32)
        for d in range(16):
            to = tile * 16 + d
            mine = words[d * 8 : d * 8 + 8, :]
            head = jnp.where(request_row, asked[to : to + 1, :], mine[:, :LANES])
            msg_ref[to, 0:16, :] = targets
            msg_ref[to, 16:24, :] = jnp.concatenate([head, mine[:, LANES:]], axis=1).astype(bf16)


def prep(kept_parts, tokens, word_cluster, cluster_block, emit_states, trans_out, trans_in, word_emb):
    width = emit_states.shape[1]
    vmem = pl.BlockSpec(memory_space=pltpu.VMEM)
    smem = pl.BlockSpec(memory_space=pltpu.SMEM)
    return pl.pallas_call(
        prep_kernel,
        out_shape=(
            jax.ShapeDtypeStruct((SHARDS, ROWS, width), bf16),
            jax.ShapeDtypeStruct((4 * KW, width), bf16),
            jax.ShapeDtypeStruct((1, LANES), i32),
        ),
        in_specs=[smem, smem] + [vmem] * 7,
        out_specs=(vmem, vmem, vmem),
        scratch_shapes=[
            pltpu.VMEM((2 * KW, width), bf16),
            pltpu.VMEM((16, LANES), i32),
            pltpu.VMEM((LANES, LANES), i32),
            pltpu.VMEM((LANES, LANES), i32),
            pltpu.VMEM((LANES, LANES), f32),
        ],
        compiler_params=pltpu.CompilerParams(vmem_limit_bytes=40 * 1024 * 1024),
        name="prep",
    )(
        kept_parts, tokens, tokens, word_cluster.reshape(-1, LANES), cluster_block[None, :],
        emit_states, trans_out, trans_in, word_emb,
    )


def score_kernel(msg_ref, mat_ref, exps_ref, out_ref, words, raw):
    share = lax.axis_index("seq")
    total = jnp.zeros((1, LANES), f32)
    for tile in range(8):
        got = msg_ref[tile * 8 : tile * 8 + 8].reshape(8 * ROWS, msg_ref.shape[2])
        res = lax.dot_general(
            got, mat_ref[...], (((1,), (1,)), ((), ())), preferred_element_type=f32
        ).reshape(8, ROWS, 2 * LANES)
        exps = jnp.exp(res[:, :16, :LANES]).reshape(LANES, LANES)
        exps_ref[tile * LANES : (tile + 1) * LANES, :] = exps
        total = total + jnp.sum(exps, axis=0, keepdims=True)
        words[tile * 64 : (tile + 1) * 64, :] = res[:, 16:, LANES:].reshape(64, LANES)
        raw[tile * 64 : (tile + 1) * 64, :] = (
            msg_ref[tile * 8 : tile * 8 + 8, 16:24, :LANES].astype(f32).reshape(64, LANES)
        )
    asked = raw[pl.ds(6, SHARDS, stride=8), :]
    spread = one_hot(iota((LANES, LANES), 0) == 12 + (iota((LANES, LANES), 1) >> 6))
    counts = jnp.dot(asked.astype(bf16), spread, preferred_element_type=f32)
    low = iota((SHARDS, LANES), 1) < KW
    for x in range(RANKS):
        scores = jnp.where(
            low,
            words[pl.ds(2 * x, SHARDS, stride=8), :],
            words[pl.ds(2 * x + 1, SHARDS, stride=8), :],
        )
        valid = (RANKS * share + x).astype(f32) < counts
        out_ref[x * SHARDS : (x + 1) * SHARDS, :] = jnp.where(valid, scores, -1e30)
    lane16 = iota((8, LANES), 1) >> 4
    packed = jnp.zeros((8, LANES), f32)
    for m in range(8):
        some = raw[pl.ds(m * 8 + 6, 8, stride=64), :]
        some = pltpu.roll(some, m * 16, 1) if m else some
        packed = jnp.where(lane16 == m, some, packed)
    out_ref[192:200, :] = packed
    out_ref[200:208, :] = jnp.broadcast_to(total, (8, LANES))


def score(msg, mat):
    vmem = pl.BlockSpec(memory_space=pltpu.VMEM)
    return pl.pallas_call(
        score_kernel,
        out_shape=(
            jax.ShapeDtypeStruct((1024, LANES), f32),
            jax.ShapeDtypeStruct((XROWS, LANES), f32),
        ),
        in_specs=[vmem] * 2,
        out_specs=(vmem, vmem),
        scratch_shapes=[pltpu.VMEM((512, LANES), f32), pltpu.VMEM((512, LANES), f32)],
        compiler_params=pltpu.CompilerParams(vmem_limit_bytes=40 * 1024 * 1024),
        name="score",
    )(msg, mat)


def pick_kernel(exps_ref, all_ref, panel_ref, trans_ref, emit_ref, table, emits):
    share = lax.axis_index("seq")
    total = jnp.zeros((1, LANES), f32)
    heap = jnp.zeros((SHARDS, LANES), f32)
    for g in range(8):
        total = total + all_ref[g, 200:201, :]
        for x in range(RANKS):
            heap = heap + jnp.exp(all_ref[g, x * SHARDS : (x + 1) * SHARDS, :])
    trans_ref[...] = jnp.broadcast_to(jnp.log(total), (8, LANES))
    emit_norm = jnp.log(jnp.sum(heap, axis=0, keepdims=True))
    emit_ref[...] = jnp.broadcast_to(emit_norm, (8, LANES))
    for g in range(8):
        rows = slice(g * 192, (g + 1) * 192)
        emits[rows, :] = jnp.exp(all_ref[g, 0:192, :] - emit_norm).astype(bf16)
    low = iota((LANES, LANES), 1) < KW
    for half in range(2):
        cols = [exps_ref[pl.ds(half * 4 + j, LANES, stride=8), :] / total for j in range(4)]
        for pair in range(2):
            first, second = cols[2 * pair], cols[2 * pair + 1]
            lanes = slice(pair * LANES, (pair + 1) * LANES)
            at = 2 * half * LANES
            table[at : at + LANES, lanes] = jnp.where(
                low, first, pltpu.roll(second, KW, 1)
            ).astype(bf16)
            table[at + LANES : at + 2 * LANES, lanes] = jnp.where(
                low, pltpu.roll(first, KW, 1), second
            ).astype(bf16)
    row8, lane8 = iota((512, LANES), 0), iota((512, LANES), 1)
    row4, lane4 = iota((256, LANES), 0), iota((256, LANES), 1)
    from8 = one_hot(((iota((512, 8), 0) >> 3) & 7) == iota((512, 8), 1))
    from4 = one_hot(((iota((256, 8), 0) >> 2) & 7) == iota((256, 8), 1))
    next_at = lane8 == (row8 >> 6) * 16 + (row8 & 3)
    key_at = ((lane4 >> 4) == (row4 >> 5)) & ((lane4 & 3) == (row4 & 3))
    key_at = key_at & ((lane4 & 15) >= 4) & ((lane4 & 15) < 12)
    ones = jnp.ones((LANES, LANES), bf16)
    weights = jnp.where((iota((LANES, LANES), 0) & 15) >= 8, 64.0, 1.0).astype(bf16)
    code = (row8 & 7) >> 1
    lane_f = lane8.astype(f32)
    key_lane = lane4.astype(f32)
    wide = iota((512, 2 * LANES), 1)
    half_of = (iota((512, 2 * LANES), 0) >> 2) & 1
    diagonal = (wide & (KW - 1)) == (wide >> 6) * 16 + share * 2 + half_of
    keep = (lane4 < KW) == ((row4 & 2) == 0)
    upper = (iota((32, 8, LANES), 1)) < 4

    def step(tile, _):
        asked = jnp.concatenate(
            [all_ref[g, pl.ds(192 + tile, 1), :] for g in range(8)], axis=0
        ).astype(bf16)
        spread = jnp.dot(from8, asked, preferred_element_type=f32)
        wanted = jnp.dot(
            jnp.where(next_at, spread, 0.0).astype(bf16), ones, preferred_element_type=f32
        )
        hit = wanted == lane_f
        chosen = jnp.concatenate([one_hot(hit & (code == b)) for b in range(4)], axis=1)
        panels = jnp.dot(chosen, table[...], preferred_element_type=f32)
        last = wanted == float(LANES)
        last = jnp.concatenate([last, last], axis=1)
        panels = jnp.where(last & diagonal, 1.0, panels)
        spread = jnp.dot(from4, asked, preferred_element_type=f32)
        keys = jnp.dot(
            jnp.where(key_at, spread, 0.0).astype(bf16), weights, preferred_element_type=f32
        )
        chosen = jnp.concatenate(
            [one_hot(keys == key_lane + float(n * LANES)) for n in range(12)], axis=1
        )
        got = jnp.dot(chosen, emits[...], preferred_element_type=f32)
        got = jnp.where(keep, got, pltpu.roll(got, KW, 1)).reshape(32, 8, LANES)
        other = pltpu.roll(got, 4, 1)
        even = jnp.where(upper, got, other)
        odd = jnp.where(upper, other, got)
        both = jnp.stack([even, odd], axis=1).reshape(512, LANES)
        panels = panels * jnp.concatenate([both, both], axis=1)
        panel_ref[pl.ds(pl.multiple_of(tile * 512, 512), 512), :] = panels.astype(bf16)
        return 0

    lax.fori_loop(0, 8, step, 0)


def pick(exps, everything):
    vmem = pl.BlockSpec(memory_space=pltpu.VMEM)
    return pl.pallas_call(
        pick_kernel,
        out_shape=(
            jax.ShapeDtypeStruct((4096, 2 * LANES), bf16),
            jax.ShapeDtypeStruct((8, LANES), f32),
            jax.ShapeDtypeStruct((8, LANES), f32),
        ),
        in_specs=[vmem] * 2,
        out_specs=(vmem, vmem, vmem),
        scratch_shapes=[pltpu.VMEM((512, 2 * LANES), bf16), pltpu.VMEM((1536, LANES), bf16)],
        compiler_params=pltpu.CompilerParams(vmem_limit_bytes=40 * 1024 * 1024),
        name="pick",
    )(exps, everything)


def chain_kernel(slot_ref, panel_ref, out_ref, ya, yb, ping, pong, logs):
    length = slot_ref.shape[1]

    def widen(i, _):
        rows = pl.ds(pl.multiple_of(i * 256, 256), 256)
        got = panel_ref[rows, :].astype(f32)
        ya[rows, :] = got[:, :LANES]
        yb[rows, :] = got[:, LANES:]
        return 0

    lax.fori_loop(0, panel_ref.shape[0] // 256, widen, 0)
    low = iota((KW, LANES), 1) < KW
    logs[...] = jnp.ones_like(logs)

    def scaled(value, at):
        top = jnp.max(jnp.max(value, axis=0, keepdims=True), axis=1, keepdims=True)
        logs[pl.ds(at, 1), :] = jnp.broadcast_to(top, (1, LANES))
        return (value * (1.0 / top)).astype(bf16)

    def build(i, _):
        for u in range(8):
            t = i * 8 + u
            rows = pl.ds(slot_ref[0, t], 16, stride=4)
            a, b = ya[rows, :], yb[rows, :]
            move = jnp.concatenate([a, pltpu.roll(a, KW, 1), b, pltpu.roll(b, KW, 1)], axis=0)
            ping[t] = scaled(jnp.where(low, move, 0.0), t)
        return 0

    lax.fori_loop(0, length // 8, build, 0)
    src, dst, count, base = ping, pong, length // 2, length
    while count >= 1:
        unroll = min(count, 8)

        def level(i, _, src=src, dst=dst, unroll=unroll, base=base):
            for u in range(unroll):
                n = i * unroll + u
                prod = jnp.dot(src[2 * n + 1][:, :KW], src[2 * n], preferred_element_type=f32)
                dst[n] = scaled(prod, base + n)
            return 0

        lax.fori_loop(0, count // unroll, level, 0)
        src, dst, count, base = dst, src, count // 2, base + count
    final = jnp.sum(jnp.sum(src[0].astype(f32), axis=0, keepdims=True), axis=1, keepdims=True)
    scale = jnp.sum(jnp.log(logs[...]), axis=0, keepdims=True)
    total = jnp.log(final) + scale - jnp.log(jnp.full((1, LANES), 8192.0, f32))
    out_ref[...] = jnp.broadcast_to(total / length, (8, LANES))


def chain(slots, panels):
    length = slots.shape[1]
    vmem = pl.BlockSpec(memory_space=pltpu.VMEM)
    return pl.pallas_call(
        chain_kernel,
        out_shape=jax.ShapeDtypeStruct((8, LANES), f32),
        in_specs=[pl.BlockSpec(memory_space=pltpu.SMEM), vmem],
        out_specs=vmem,
        scratch_shapes=[
            pltpu.VMEM((4096, LANES), f32),
            pltpu.VMEM((4096, LANES), f32),
            pltpu.VMEM((length, KW, LANES), bf16),
            pltpu.VMEM((length // 2, KW, LANES), bf16),
            pltpu.VMEM((2 * length, LANES), f32),
        ],
        compiler_params=pltpu.CompilerParams(vmem_limit_bytes=40 * 1024 * 1024),
        name="chain",
    )(slots, panels)


def local(
    emit_states, trans_out, trans_in, word_emb, word_cluster, cluster_block, kept_parts, tokens
):
    msg, mat, slots = prep(
        kept_parts, tokens, word_cluster, cluster_block, emit_states, trans_out, trans_in, word_emb
    )
    arrived = lax.all_to_all(msg, "state", split_axis=0, concat_axis=0, tiled=True)
    exps, mine = score(arrived, mat)
    everything = lax.all_gather(mine, "seq", axis=0, tiled=False)
    panels, trans_norm, emit_norm = pick(exps, everything)
    got = lax.all_to_all(
        panels.reshape(512, 8, 2 * LANES),
        ("state", "seq"),
        split_axis=0,
        concat_axis=0,
        tiled=True,
    ).reshape(4096, 2 * LANES)
    token_loglik = chain(slots, got)
    return (token_loglik[0, :1], trans_norm[0], emit_norm[0])


def solution(mesh):
    placed = (
        P("state", None),
        P("state", None),
        P("state", None),
        P("state", None),
        P(),
        P(),
        P(),
        P(("state", "seq"), None),
    )
    return jax.shard_map(
        local,
        mesh=mesh,
        in_specs=placed,
        out_specs=(P(("state", "seq")), P("state"), P("state")),
        check_vma=False,
    )
```

```python
import jax
import jax.numpy as jnp
from jax import lax
from jax.experimental import pallas as pl
from jax.experimental.pallas import tpu as pltpu
from jax.sharding import PartitionSpec as P

BS = 256
PART = 32
KW = 64
LANES = 128
RANKS = 3
SHARDS = 64
ROWS = 24
XROWS = 208
f32 = jnp.float32
bf16 = jnp.bfloat16
i32 = jnp.int32


def iota(shape, axis):
    return lax.broadcasted_iota(i32, shape, axis)


def one_hot(mask):
    return jnp.where(mask, 1.0, 0.0).astype(bf16)


def ints(mask, value):
    return jnp.where(mask, value, 0)


def prep_kernel(
    parts_ref, token_ref, tokens_hbm, cluster_hbm, table_hbm, emit_hbm, out_hbm, in_hbm, word_hbm,
    msg_ref, mat_ref, slot_ref,
    in_kept, slot_of, near, wide, counts_of, tokens_ref, cluster_ref, table_ref, word_ref, chosen, sems,
):
    me = lax.axis_index("state")
    share = lax.axis_index("seq")
    head = []
    for n, (src, dst) in enumerate(
        ((cluster_hbm, cluster_ref), (table_hbm, table_ref), (tokens_hbm, tokens_ref))
    ):
        head.append(pltpu.make_async_copy(src, dst, sems.at[n]))
        head[-1].start()
    word_copy = pltpu.make_async_copy(word_hbm, word_ref, sems.at[3])
    word_copy.start()
    kept = []
    for blk in range(2):
        for part in range(2):
            start = blk * BS + parts_ref[part, me * 2 + blk] * PART
            src = pl.ds(pl.multiple_of(start, PART), PART)
            at = (blk * 2 + part) * PART
            for which, (hbm, ref, to) in enumerate(
                ((in_hbm, in_kept, at), (out_hbm, mat_ref, at), (emit_hbm, mat_ref, 2 * KW + at))
            ):
                sem = sems.at[4 + (blk * 2 + part) * 3 + which]
                kept.append(pltpu.make_async_copy(hbm.at[src, :], ref.at[pl.ds(to, PART), :], sem))
                kept[-1].start()
    for copy in head:
        copy.wait()
    sub = iota((LANES, LANES), 0)
    lane = iota((LANES, LANES), 1)
    eye = sub == lane

    def column(row):
        return jnp.sum(ints(eye, row), axis=1, keepdims=True)

    def line(col):
        return jnp.sum(ints(eye, col), axis=0, keepdims=True)

    sums = jnp.concatenate([one_hot(sub < lane), jnp.ones((LANES, LANES), bf16)], axis=1)
    block_row = table_ref[...]
    block_col = column(block_row)
    block_col_f = block_col.astype(f32)
    carry = jnp.zeros((LANES, LANES), f32)
    chunks = 2048 // LANES
    own = pl.multiple_of(me * chunks, chunks)
    own_rows = cluster_ref[pl.ds(own, chunks), :]
    for c in range(chunks):
        hit = sub == own_rows[c : c + 1, :]
        found = jnp.dot(one_hot(hit), sums, preferred_element_type=f32)
        before = found[:, :LANES] + carry
        carry = carry + found[:, LANES:]
        rank = jnp.sum(jnp.where(hit, before, 0.0), axis=0, keepdims=True).astype(i32)
        block = jnp.sum(jnp.where(hit, block_col_f, 0.0), axis=0, keepdims=True).astype(i32)
        x = rank - RANKS * share
        slot = (block >> 1) * 8 + x * 2 + (block & 1)
        slot_of[c : c + 1, :] = jnp.where((x >= 0) & (x < RANKS), slot, -1)
    counts_of[...] = carry

    length = token_ref.shape[1]

    def pull(i, _):
        for u in range(8):
            t = i * 8 + u
            near[pl.ds(t, 1), :] = cluster_ref[pl.ds(token_ref[0, t] >> 7, 1), :]
        return 0

    lax.fori_loop(0, length // 8, pull, 0)
    token_col = column(tokens_ref[...])
    cluster_col = jnp.sum(ints(lane == (token_col & 127), near[...]), axis=1, keepdims=True)
    near[...] = jnp.broadcast_to(cluster_col, (LANES, LANES))
    place = iota((chunks, LANES), 0) * LANES + iota((chunks, LANES), 1)

    def tally(i, _):
        for u in range(8):
            t = i * 8 + u
            token = token_ref[0, t]
            shard_rows = cluster_ref[pl.ds(pl.multiple_of((token >> 11) * chunks, chunks), chunks), :]
            earlier = (shard_rows == near[pl.ds(t, 1), :]) & (place < (token & 2047))
            wide[pl.ds(t, 1), :] = jnp.sum(ints(earlier, 1), axis=0, keepdims=True)
        return 0

    lax.fori_loop(0, length // 8, tally, 0)
    rank_col = jnp.sum(wide[...], axis=1, keepdims=True)
    own_block_col = jnp.sum(ints(lane == cluster_col, block_row), axis=1, keepdims=True)
    own_block_row = line(own_block_col)
    same = own_block_col == own_block_row
    times_col = jnp.sum(ints(same & (lane < sub), 1), axis=1, keepdims=True)
    times_row = jnp.sum(ints(same & (sub < lane), 1), axis=0, keepdims=True)
    slot_ref[...] = (own_block_row >> 1) * 64 + (own_block_row & 1) * 2 + times_row
    following = jnp.sum(ints(lane == sub + 1, own_block_row), axis=1, keepdims=True)
    following = jnp.where(iota((LANES, 1), 0) == length - 1, LANES, following)
    slots_col = own_block_col * 2 + times_col
    asked = jnp.zeros((SHARDS, LANES), f32)
    slot_line = iota((LANES, 2 * LANES), 1)
    at_slot = slot_line == slots_col
    owner = (iota((SHARDS, 2 * LANES), 1) >> 2) == iota((SHARDS, 2 * LANES), 0)
    slot_sub = iota((2 * LANES, LANES), 0) & 3
    slot_lane = iota((2 * LANES, LANES), 1)
    for field, values in enumerate((following, token_col >> 11, rank_col)):
        value_row = jnp.sum(ints(at_slot, values), axis=0, keepdims=True)
        spread = jnp.where(owner, value_row.astype(f32), 0.0).astype(bf16)
        asked += jnp.dot(
            spread, one_hot(slot_lane == field * 4 + slot_sub), preferred_element_type=f32
        )
    count_lane = jnp.where(lane == 12 + (block_col & 1), counts_of[...], 0.0).astype(bf16)
    count_owner = one_hot((block_row >> 1) == iota((SHARDS, LANES), 0))
    asked += jnp.dot(count_owner, count_lane, preferred_element_type=f32)

    for copy in kept:
        copy.wait()
    row = iota((16, LANES), 0)
    want = (row >> 3) * KW + (row & 3) * 16 + share * 2 + ((row >> 2) & 1)
    targets = jnp.dot(
        one_hot(iota((16, LANES), 1) == want), in_kept[...], preferred_element_type=f32
    ).astype(bf16)
    for to in range(SHARDS):
        msg_ref[to, 0:16, :] = targets
    for tile in range(4):
        for c in range(chunks):
            chosen[tile * LANES : (tile + 1) * LANES, c * LANES : (c + 1) * LANES] = one_hot(
                sub + tile * LANES == slot_of[c : c + 1, :]
            )
    word_copy.wait()
    request_row = iota((8, LANES), 0) == 6
    words = jnp.dot(chosen[...], word_ref[...], preferred_element_type=f32)
    for to in range(SHARDS):
        mine = words[to * 8 : to * 8 + 8, :]
        first = jnp.where(request_row, asked[to : to + 1, :], mine[:, :LANES])
        msg_ref[to, 16:24, :] = jnp.concatenate([first, mine[:, LANES:]], axis=1).astype(bf16)


def prep(kept_parts, tokens, word_cluster, cluster_block, emit_states, trans_out, trans_in, word_emb):
    width = emit_states.shape[1]
    vmem = pl.BlockSpec(memory_space=pltpu.VMEM)
    smem = pl.BlockSpec(memory_space=pltpu.SMEM)
    clusters = word_cluster.reshape(-1, LANES)
    return pl.pallas_call(
        prep_kernel,
        out_shape=(
            jax.ShapeDtypeStruct((SHARDS, ROWS, width), bf16),
            jax.ShapeDtypeStruct((4 * KW, width), bf16),
            jax.ShapeDtypeStruct((1, LANES), i32),
        ),
        in_specs=[smem, smem] + [pl.BlockSpec(memory_space=pltpu.HBM)] * 7,
        out_specs=(vmem, vmem, vmem),
        scratch_shapes=[
            pltpu.VMEM((2 * KW, width), bf16),
            pltpu.VMEM((16, LANES), i32),
            pltpu.VMEM((LANES, LANES), i32),
            pltpu.VMEM((LANES, LANES), i32),
            pltpu.VMEM((LANES, LANES), f32),
            pltpu.VMEM((1, LANES), i32),
            pltpu.VMEM(clusters.shape, i32),
            pltpu.VMEM((1, LANES), i32),
            pltpu.VMEM(word_emb.shape, bf16),
            pltpu.VMEM((8 * SHARDS, word_emb.shape[0]), bf16),
            pltpu.SemaphoreType.DMA((16,)),
        ],
        compiler_params=pltpu.CompilerParams(vmem_limit_bytes=60 * 1024 * 1024),
        name="prep",
    )(
        kept_parts.T, tokens, tokens, clusters, cluster_block[None, :],
        emit_states, trans_out, trans_in, word_emb,
    )


def score_kernel(msg_ref, mat_ref, exps_ref, out_ref, words, raw):
    share = lax.axis_index("seq")
    total = jnp.zeros((1, LANES), f32)
    for tile in range(8):
        got = msg_ref[tile * 8 : tile * 8 + 8].reshape(8 * ROWS, msg_ref.shape[2])
        res = lax.dot_general(
            got, mat_ref[...], (((1,), (1,)), ((), ())), preferred_element_type=f32
        ).reshape(8, ROWS, 2 * LANES)
        exps = jnp.exp(res[:, :16, :LANES]).reshape(LANES, LANES)
        exps_ref[tile * LANES : (tile + 1) * LANES, :] = exps
        total = total + jnp.sum(exps, axis=0, keepdims=True)
        words[tile * 64 : (tile + 1) * 64, :] = res[:, 16:, LANES:].reshape(64, LANES)
        raw[tile * 64 : (tile + 1) * 64, :] = (
            msg_ref[tile * 8 : tile * 8 + 8, 16:24, :LANES].astype(f32).reshape(64, LANES)
        )
    asked = raw[pl.ds(6, SHARDS, stride=8), :]
    spread = one_hot(iota((LANES, LANES), 0) == 12 + (iota((LANES, LANES), 1) >> 6))
    counts = jnp.dot(asked.astype(bf16), spread, preferred_element_type=f32)
    low = iota((SHARDS, LANES), 1) < KW
    for x in range(RANKS):
        scores = jnp.where(
            low,
            words[pl.ds(2 * x, SHARDS, stride=8), :],
            words[pl.ds(2 * x + 1, SHARDS, stride=8), :],
        )
        valid = (RANKS * share + x).astype(f32) < counts
        out_ref[x * SHARDS : (x + 1) * SHARDS, :] = jnp.where(valid, scores, -1e30)
    lane16 = iota((8, LANES), 1) >> 4
    packed = jnp.zeros((8, LANES), f32)
    for m in range(8):
        some = raw[pl.ds(m * 8 + 6, 8, stride=64), :]
        some = pltpu.roll(some, m * 16, 1) if m else some
        packed = jnp.where(lane16 == m, some, packed)
    out_ref[192:200, :] = packed
    out_ref[200:208, :] = jnp.broadcast_to(total, (8, LANES))


def score(msg, mat):
    vmem = pl.BlockSpec(memory_space=pltpu.VMEM)
    return pl.pallas_call(
        score_kernel,
        out_shape=(
            jax.ShapeDtypeStruct((1024, LANES), f32),
            jax.ShapeDtypeStruct((XROWS, LANES), f32),
        ),
        in_specs=[vmem] * 2,
        out_specs=(vmem, vmem),
        scratch_shapes=[pltpu.VMEM((512, LANES), f32), pltpu.VMEM((512, LANES), f32)],
        compiler_params=pltpu.CompilerParams(vmem_limit_bytes=40 * 1024 * 1024),
        name="score",
    )(msg, mat)


def pick_kernel(
    exps_ref, all_ref, panel_ref, trans_ref, emit_ref, table, emits, next_rows, word_rows
):
    share = lax.axis_index("seq")
    step = pl.program_id(0)

    @pl.when(step == 0)
    def _():
        total = jnp.zeros((1, LANES), f32)
        heap = jnp.zeros((SHARDS, LANES), f32)
        for g in range(8):
            total = total + all_ref[g, 200:201, :]
            for x in range(RANKS):
                heap = heap + jnp.exp(all_ref[g, x * SHARDS : (x + 1) * SHARDS, :])
        trans_ref[...] = jnp.broadcast_to(jnp.log(total), (8, LANES))
        emit_norm = jnp.log(jnp.sum(heap, axis=0, keepdims=True))
        emit_ref[...] = jnp.broadcast_to(emit_norm, (8, LANES))
        for g in range(8):
            rows = slice((g & 3) * 192, (g & 3) * 192 + 192)
            lanes = slice((g >> 2) * LANES, (g >> 2) * LANES + LANES)
            emits[rows, lanes] = jnp.exp(all_ref[g, 0:192, :] - emit_norm).astype(bf16)
        low = iota((LANES, LANES), 1) < KW
        for half in range(2):
            cols = [exps_ref[pl.ds(half * 4 + j, LANES, stride=8), :] / total for j in range(4)]
            for pair in range(2):
                first, second = cols[2 * pair], cols[2 * pair + 1]
                lanes = slice(pair * LANES, (pair + 1) * LANES)
                at = 2 * half * LANES
                table[at : at + LANES, lanes] = jnp.where(
                    low, first, pltpu.roll(second, KW, 1)
                ).astype(bf16)
                table[at + LANES : at + 2 * LANES, lanes] = jnp.where(
                    low, pltpu.roll(first, KW, 1), second
                ).astype(bf16)

    row8, lane8 = iota((512, LANES), 0), iota((512, LANES), 1)
    row4, lane4 = iota((256, LANES), 0), iota((256, LANES), 1)
    from8 = one_hot(((iota((512, 8), 0) >> 3) & 7) == iota((512, 8), 1))
    from4 = one_hot(((iota((256, 8), 0) >> 2) & 7) == iota((256, 8), 1))
    next_at = lane8 == (row8 >> 6) * 16 + (row8 & 3)
    key_at = ((lane4 >> 4) == (row4 >> 5)) & ((lane4 & 3) == (row4 & 3))
    key_at = key_at & ((lane4 & 15) >= 4) & ((lane4 & 15) < 12)
    ones = jnp.ones((LANES, LANES), bf16)
    weights = jnp.where((iota((LANES, LANES), 0) & 15) >= 8, 64.0, 1.0).astype(bf16)
    code = (row8 & 7) >> 1
    lane_f = lane8.astype(f32)
    key_lane = lane4.astype(f32)
    wanted, late = [], []
    for part in range(2):
        asked = jnp.concatenate(
            [all_ref[g, pl.ds(192 + step * 2 + part, 1), :] for g in range(8)], axis=0
        ).astype(bf16)
        spread = jnp.dot(from8, asked, preferred_element_type=f32)
        block = jnp.dot(
            jnp.where(next_at, spread, 0.0).astype(bf16), ones, preferred_element_type=f32
        )
        hit = block == lane_f
        for b in range(4):
            next_rows[part * 512 : part * 512 + 512, b * LANES : (b + 1) * LANES] = one_hot(
                hit & (code == b)
            )
        wanted.append(block == float(LANES))
        spread = jnp.dot(from4, asked, preferred_element_type=f32)
        keys = jnp.dot(
            jnp.where(key_at, spread, 0.0).astype(bf16), weights, preferred_element_type=f32
        )
        late.append(keys >= 768.0)
        keys = jnp.where(late[-1], keys - 768.0, keys)
        for n in range(6):
            word_rows[part * 256 : part * 256 + 256, n * LANES : (n + 1) * LANES] = one_hot(
                keys == key_lane + float(n * LANES)
            )
    panels = jnp.dot(next_rows[...], table[...], preferred_element_type=f32)
    got = jnp.dot(word_rows[...], emits[...], preferred_element_type=f32)
    wide = iota((512, 2 * LANES), 1)
    half_of = (iota((512, 2 * LANES), 0) >> 2) & 1
    diagonal = (wide & (KW - 1)) == (wide >> 6) * 16 + share * 2 + half_of
    keep = (lane4 < KW) == ((row4 & 2) == 0)
    upper = (iota((32, 8, LANES), 1)) < 4
    for part in range(2):
        rows = slice(part * 256, part * 256 + 256)
        mine = jnp.where(late[part], got[rows, LANES:], got[rows, :LANES])
        mine = jnp.where(keep, mine, pltpu.roll(mine, KW, 1)).reshape(32, 8, LANES)
        other = pltpu.roll(mine, 4, 1)
        even = jnp.where(upper, mine, other)
        odd = jnp.where(upper, other, mine)
        both = jnp.stack([even, odd], axis=1).reshape(512, LANES)
        rows = slice(part * 512, part * 512 + 512)
        last = jnp.concatenate([wanted[part], wanted[part]], axis=1)
        panel = jnp.where(last & diagonal, 1.0, panels[rows, :])
        panel_ref[rows, :] = (panel * jnp.concatenate([both, both], axis=1)).astype(bf16)


def pick(exps, everything):
    vmem = pl.BlockSpec(memory_space=pltpu.VMEM)
    small = pl.BlockSpec((8, LANES), lambda i: (0, 0))
    return pl.pallas_call(
        pick_kernel,
        grid=(4,),
        out_shape=(
            jax.ShapeDtypeStruct((4096, 2 * LANES), bf16),
            jax.ShapeDtypeStruct((8, LANES), f32),
            jax.ShapeDtypeStruct((8, LANES), f32),
        ),
        in_specs=[vmem] * 2,
        out_specs=(pl.BlockSpec((1024, 2 * LANES), lambda i: (i, 0)), small, small),
        scratch_shapes=[
            pltpu.VMEM((512, 2 * LANES), bf16),
            pltpu.VMEM((768, 2 * LANES), bf16),
            pltpu.VMEM((1024, 512), bf16),
            pltpu.VMEM((512, 768), bf16),
        ],
        compiler_params=pltpu.CompilerParams(vmem_limit_bytes=60 * 1024 * 1024),
        name="pick",
    )(exps, everything)


def chain_kernel(slot_ref, panel_ref, out_ref, ya, yb, ping, pong, logs, tops):
    length = slot_ref.shape[1]

    def widen(i, _):
        rows = pl.ds(pl.multiple_of(i * 256, 256), 256)
        got = panel_ref[rows, :].astype(f32)
        ya[rows, :] = got[:, :LANES]
        yb[rows, :] = got[:, LANES:]
        return 0

    lax.fori_loop(0, panel_ref.shape[0] // 256, widen, 0)
    low = iota((16, LANES), 1) < KW

    def build(i, _):
        for u in range(8):
            t = i * 8 + u
            rows = pl.ds(slot_ref[0, t], 16, stride=4)
            a, b = ya[rows, :], yb[rows, :]
            logs[pl.ds(t, 1), :] = jnp.max(jnp.maximum(a, b), axis=0, keepdims=True)
            move = [a, pltpu.roll(a, KW, 1), b, pltpu.roll(b, KW, 1)]
            move = [jnp.where(low, part, 0.0) for part in move]
            ping[t] = jnp.concatenate(move, axis=0).astype(bf16)
        return 0

    lax.fori_loop(0, length // 8, build, 0)
    peak = jnp.max(logs[0:length, :], axis=1, keepdims=True)
    tops[...] = jnp.broadcast_to((1.0 / peak).astype(bf16).astype(f32), (length, LANES))
    logs[0:length, :] = 1.0 / tops[...]
    logs[length:, :] = jnp.ones((length, LANES), f32)
    src, dst, count, base = ping, pong, length // 2, length
    while count > 1:
        unroll = min(count, 16)

        def level(i, _, src=src, dst=dst, unroll=unroll, base=base, first=src is ping and base == length):
            for u in range(unroll):
                n = i * unroll + u
                left, right = src[2 * n + 1][:, :KW], src[2 * n]
                if first:
                    left = left * tops[pl.ds(2 * n + 1, 1), :KW].astype(bf16)
                    right = right * tops[pl.ds(2 * n, 1), :].astype(bf16)
                prod = jnp.dot(left, right, preferred_element_type=f32)
                top = jnp.max(jnp.max(prod, axis=0, keepdims=True), axis=1, keepdims=True)
                logs[pl.ds(base + n, 1), :] = jnp.broadcast_to(top, (1, LANES))
                dst[n] = (prod * (1.0 / top)).astype(bf16)
            return 0

        lax.fori_loop(0, count // unroll, level, 0)
        src, dst, count, base = dst, src, count // 2, base + count
    prod = jnp.dot(src[1][:, :KW], src[0], preferred_element_type=f32)
    final = jnp.sum(jnp.sum(prod, axis=0, keepdims=True), axis=1, keepdims=True)
    scale = jnp.sum(jnp.log(logs[...]), axis=0, keepdims=True)
    total = jnp.log(final) + scale - jnp.log(jnp.full((1, LANES), 8192.0, f32))
    out_ref[...] = jnp.broadcast_to(total / length, (8, LANES))


def chain(slots, panels):
    length = slots.shape[1]
    vmem = pl.BlockSpec(memory_space=pltpu.VMEM)
    return pl.pallas_call(
        chain_kernel,
        out_shape=jax.ShapeDtypeStruct((8, LANES), f32),
        in_specs=[pl.BlockSpec(memory_space=pltpu.SMEM), vmem],
        out_specs=vmem,
        scratch_shapes=[
            pltpu.VMEM((4096, LANES), f32),
            pltpu.VMEM((4096, LANES), f32),
            pltpu.VMEM((length, KW, LANES), bf16),
            pltpu.VMEM((length // 2, KW, LANES), bf16),
            pltpu.VMEM((2 * length, LANES), f32),
            pltpu.VMEM((length, LANES), f32),
        ],
        compiler_params=pltpu.CompilerParams(vmem_limit_bytes=40 * 1024 * 1024),
        name="chain",
    )(slots, panels)


def local(
    emit_states, trans_out, trans_in, word_emb, word_cluster, cluster_block, kept_parts, tokens
):
    msg, mat, slots = prep(
        kept_parts, tokens, word_cluster, cluster_block, emit_states, trans_out, trans_in, word_emb
    )
    arrived = lax.all_to_all(msg, "state", split_axis=0, concat_axis=0, tiled=True)
    exps, mine = score(arrived, mat)
    everything = lax.all_gather(mine, "seq", axis=0, tiled=False)
    panels, trans_norm, emit_norm = pick(exps, everything)
    got = lax.all_to_all(
        panels.reshape(512, 8, 2 * LANES),
        ("state", "seq"),
        split_axis=0,
        concat_axis=0,
        tiled=True,
    ).reshape(4096, 2 * LANES)
    token_loglik = chain(slots, got)
    return (token_loglik[0, :1], trans_norm[0], emit_norm[0])


def solution(mesh):
    placed = (
        P("state", None),
        P("state", None),
        P("state", None),
        P("state", None),
        P(),
        P(),
        P(),
        P(("state", "seq"), None),
    )
    return jax.shard_map(
        local,
        mesh=mesh,
        in_specs=placed,
        out_specs=(P(("state", "seq")), P("state"), P("state")),
        check_vma=False,
    )
```

```python
import jax
import jax.numpy as jnp
from jax import lax
from jax.experimental import pallas as pl
from jax.experimental.pallas import tpu as pltpu
from jax.sharding import PartitionSpec as P

BS = 256
PART = 32
KW = 64
LANES = 128
RANKS = 3
SHARDS = 64
SLOTS = 4
SENT = 3
ROWS = 24
XROWS = 208
f32 = jnp.float32
bf16 = jnp.bfloat16
i32 = jnp.int32


def iota(shape, axis):
    return lax.broadcasted_iota(i32, shape, axis)


def one_hot(mask):
    return jnp.where(mask, 1.0, 0.0).astype(bf16)


def ints(mask, value):
    return jnp.where(mask, value, 0)


def prep_kernel(
    parts_ref, token_ref, tokens_hbm, cluster_hbm, table_hbm, emit_hbm, out_hbm, in_hbm, word_hbm,
    msg_ref, mat_ref, slot_ref,
    in_kept, slot_of, near, wide, counts_of, tokens_ref, cluster_ref, table_ref, word_ref, chosen, sems,
):
    me = lax.axis_index("state")
    share = lax.axis_index("seq")
    head = []
    for n, (src, dst) in enumerate(
        ((cluster_hbm, cluster_ref), (table_hbm, table_ref), (tokens_hbm, tokens_ref))
    ):
        head.append(pltpu.make_async_copy(src, dst, sems.at[n]))
        head[-1].start()
    word_copy = pltpu.make_async_copy(word_hbm, word_ref, sems.at[3])
    word_copy.start()
    kept = []
    for blk in range(2):
        for part in range(2):
            start = blk * BS + parts_ref[part, me * 2 + blk] * PART
            src = pl.ds(pl.multiple_of(start, PART), PART)
            at = (blk * 2 + part) * PART
            for which, (hbm, ref, to) in enumerate(
                ((in_hbm, in_kept, at), (out_hbm, mat_ref, at), (emit_hbm, mat_ref, 2 * KW + at))
            ):
                sem = sems.at[4 + (blk * 2 + part) * 3 + which]
                kept.append(pltpu.make_async_copy(hbm.at[src, :], ref.at[pl.ds(to, PART), :], sem))
                kept[-1].start()
    for copy in head:
        copy.wait()
    sub = iota((LANES, LANES), 0)
    lane = iota((LANES, LANES), 1)
    eye = sub == lane

    def column(row):
        return jnp.sum(ints(eye, row), axis=1, keepdims=True)

    def line(col):
        return jnp.sum(ints(eye, col), axis=0, keepdims=True)

    sums = jnp.concatenate([one_hot(sub < lane), jnp.ones((LANES, LANES), bf16)], axis=1)
    block_row = table_ref[...]
    block_col = column(block_row)
    block_col_f = block_col.astype(f32)
    carry = jnp.zeros((LANES, LANES), f32)
    chunks = 2048 // LANES
    own = pl.multiple_of(me * chunks, chunks)
    own_rows = cluster_ref[pl.ds(own, chunks), :]
    for c in range(chunks):
        hit = sub == own_rows[c : c + 1, :]
        found = jnp.dot(one_hot(hit), sums, preferred_element_type=f32)
        before = found[:, :LANES] + carry
        carry = carry + found[:, LANES:]
        rank = jnp.sum(jnp.where(hit, before, 0.0), axis=0, keepdims=True).astype(i32)
        block = jnp.sum(jnp.where(hit, block_col_f, 0.0), axis=0, keepdims=True).astype(i32)
        x = rank - RANKS * share
        slot = (block >> 1) * 8 + x * 2 + (block & 1)
        slot_of[c : c + 1, :] = jnp.where((x >= 0) & (x < RANKS), slot, -1)
    counts_of[...] = carry

    length = token_ref.shape[1]

    def pull(i, _):
        for u in range(8):
            t = i * 8 + u
            near[pl.ds(t, 1), :] = cluster_ref[pl.ds(token_ref[0, t] >> 7, 1), :]
        return 0

    lax.fori_loop(0, length // 8, pull, 0)
    token_col = column(tokens_ref[...])
    cluster_col = jnp.sum(ints(lane == (token_col & 127), near[...]), axis=1, keepdims=True)
    near[...] = jnp.broadcast_to(cluster_col, (LANES, LANES))
    place = iota((chunks, LANES), 0) * LANES + iota((chunks, LANES), 1)

    def tally(i, _):
        for u in range(8):
            t = i * 8 + u
            token = token_ref[0, t]
            shard_rows = cluster_ref[pl.ds(pl.multiple_of((token >> 11) * chunks, chunks), chunks), :]
            earlier = (shard_rows == near[pl.ds(t, 1), :]) & (place < (token & 2047))
            wide[pl.ds(t, 1), :] = jnp.sum(ints(earlier, 1), axis=0, keepdims=True)
        return 0

    lax.fori_loop(0, length // 8, tally, 0)
    rank_col = jnp.sum(wide[...], axis=1, keepdims=True)
    own_block_col = jnp.sum(ints(lane == cluster_col, block_row), axis=1, keepdims=True)
    own_block_row = line(own_block_col)
    same = (own_block_col >> 1) == (own_block_row >> 1)
    times_col = jnp.sum(ints(same & (lane < sub), 1), axis=1, keepdims=True)
    times_row = jnp.sum(ints(same & (sub < lane), 1), axis=0, keepdims=True)
    slot_ref[...] = times_row * 4096 + (own_block_row >> 1) * 64
    following = jnp.sum(ints(lane == sub + 1, own_block_row), axis=1, keepdims=True)
    following = jnp.where(iota((LANES, 1), 0) == length - 1, LANES, following)
    slots_col = (own_block_col >> 1) * SLOTS + times_col
    asked = jnp.zeros((SHARDS, LANES), f32)
    slot_line = iota((LANES, 2 * LANES), 1)
    at_slot = slot_line == slots_col
    owner = (iota((SHARDS, 2 * LANES), 1) >> 2) == iota((SHARDS, 2 * LANES), 0)
    slot_sub = iota((2 * LANES, LANES), 0) & 3
    slot_lane = iota((2 * LANES, LANES), 1)
    for field, values in enumerate((following, token_col >> 11, rank_col + 32 * (own_block_col & 1))):
        value_row = jnp.sum(ints(at_slot, values), axis=0, keepdims=True)
        spread = jnp.where(owner, value_row.astype(f32), 0.0).astype(bf16)
        asked += jnp.dot(
            spread, one_hot(slot_lane == field * 4 + slot_sub), preferred_element_type=f32
        )
    count_lane = jnp.where(lane == 12 + (block_col & 1), counts_of[...], 0.0).astype(bf16)
    count_owner = one_hot((block_row >> 1) == iota((SHARDS, LANES), 0))
    asked += jnp.dot(count_owner, count_lane, preferred_element_type=f32)
    full = jnp.max(times_row, axis=1, keepdims=True) >= SENT
    asked += jnp.where(full & (iota((SHARDS, LANES), 1) == 14), 1.0, 0.0)

    for copy in kept:
        copy.wait()
    row = iota((16, LANES), 0)
    want = (row >> 3) * KW + (row & 7) * 8 + share
    targets = jnp.dot(
        one_hot(iota((16, LANES), 1) == want), in_kept[...], preferred_element_type=f32
    ).astype(bf16)
    for to in range(SHARDS):
        msg_ref[to, 0:16, :] = targets
    for tile in range(4):
        for c in range(chunks):
            chosen[tile * LANES : (tile + 1) * LANES, c * LANES : (c + 1) * LANES] = one_hot(
                sub + tile * LANES == slot_of[c : c + 1, :]
            )
    word_copy.wait()
    request_row = iota((8, LANES), 0) == 6
    words = jnp.dot(chosen[...], word_ref[...], preferred_element_type=f32)
    for to in range(SHARDS):
        mine = words[to * 8 : to * 8 + 8, :]
        first = jnp.where(request_row, asked[to : to + 1, :], mine[:, :LANES])
        msg_ref[to, 16:24, :] = jnp.concatenate([first, mine[:, LANES:]], axis=1).astype(bf16)


def prep(kept_parts, tokens, word_cluster, cluster_block, emit_states, trans_out, trans_in, word_emb):
    width = emit_states.shape[1]
    vmem = pl.BlockSpec(memory_space=pltpu.VMEM)
    smem = pl.BlockSpec(memory_space=pltpu.SMEM)
    clusters = word_cluster.reshape(-1, LANES)
    return pl.pallas_call(
        prep_kernel,
        out_shape=(
            jax.ShapeDtypeStruct((SHARDS, ROWS, width), bf16),
            jax.ShapeDtypeStruct((4 * KW, width), bf16),
            jax.ShapeDtypeStruct((1, LANES), i32),
        ),
        in_specs=[smem, smem] + [pl.BlockSpec(memory_space=pltpu.HBM)] * 7,
        out_specs=(vmem, vmem, vmem),
        scratch_shapes=[
            pltpu.VMEM((2 * KW, width), bf16),
            pltpu.VMEM((16, LANES), i32),
            pltpu.VMEM((LANES, LANES), i32),
            pltpu.VMEM((LANES, LANES), i32),
            pltpu.VMEM((LANES, LANES), f32),
            pltpu.VMEM((1, LANES), i32),
            pltpu.VMEM(clusters.shape, i32),
            pltpu.VMEM((1, LANES), i32),
            pltpu.VMEM(word_emb.shape, bf16),
            pltpu.VMEM((8 * SHARDS, word_emb.shape[0]), bf16),
            pltpu.SemaphoreType.DMA((16,)),
        ],
        compiler_params=pltpu.CompilerParams(vmem_limit_bytes=60 * 1024 * 1024),
        name="prep",
    )(
        kept_parts.T, tokens, tokens, clusters, cluster_block[None, :],
        emit_states, trans_out, trans_in, word_emb,
    )


def score_kernel(msg_ref, mat_ref, exps_ref, out_ref, words, raw):
    share = lax.axis_index("seq")
    total = jnp.zeros((1, LANES), f32)
    for tile in range(8):
        got = msg_ref[tile * 8 : tile * 8 + 8].reshape(8 * ROWS, msg_ref.shape[2])
        res = lax.dot_general(
            got, mat_ref[...], (((1,), (1,)), ((), ())), preferred_element_type=f32
        ).reshape(8, ROWS, 2 * LANES)
        exps = jnp.exp(res[:, :16, :LANES]).reshape(LANES, LANES)
        exps_ref[tile * LANES : (tile + 1) * LANES, :] = exps
        total = total + jnp.sum(exps, axis=0, keepdims=True)
        words[tile * 64 : (tile + 1) * 64, :] = res[:, 16:, LANES:].reshape(64, LANES)
        raw[tile * 64 : (tile + 1) * 64, :] = (
            msg_ref[tile * 8 : tile * 8 + 8, 16:24, :LANES].astype(f32).reshape(64, LANES)
        )
    asked = raw[pl.ds(6, SHARDS, stride=8), :]
    spread = one_hot(iota((LANES, LANES), 0) == 12 + (iota((LANES, LANES), 1) >> 6))
    counts = jnp.dot(asked.astype(bf16), spread, preferred_element_type=f32)
    low = iota((SHARDS, LANES), 1) < KW
    for x in range(RANKS):
        scores = jnp.where(
            low,
            words[pl.ds(2 * x, SHARDS, stride=8), :],
            words[pl.ds(2 * x + 1, SHARDS, stride=8), :],
        )
        valid = (RANKS * share + x).astype(f32) < counts
        out_ref[x * SHARDS : (x + 1) * SHARDS, :] = jnp.where(valid, scores, -1e30)
    lane16 = iota((8, LANES), 1) >> 4
    packed = jnp.zeros((8, LANES), f32)
    for m in range(8):
        some = raw[pl.ds(m * 8 + 6, 8, stride=64), :]
        some = pltpu.roll(some, m * 16, 1) if m else some
        packed = jnp.where(lane16 == m, some, packed)
    out_ref[192:200, :] = packed
    out_ref[200:208, :] = jnp.broadcast_to(total, (8, LANES))


def score(msg, mat):
    vmem = pl.BlockSpec(memory_space=pltpu.VMEM)
    return pl.pallas_call(
        score_kernel,
        out_shape=(
            jax.ShapeDtypeStruct((1024, LANES), f32),
            jax.ShapeDtypeStruct((XROWS, LANES), f32),
        ),
        in_specs=[vmem] * 2,
        out_specs=(vmem, vmem),
        scratch_shapes=[pltpu.VMEM((512, LANES), f32), pltpu.VMEM((512, LANES), f32)],
        compiler_params=pltpu.CompilerParams(vmem_limit_bytes=40 * 1024 * 1024),
        name="score",
    )(msg, mat)


def pick_kernel(
    exps_ref, all_ref, panel_ref, spare_ref, trans_ref, emit_ref, full_ref,
    table, emits, next_rows, word_rows, blocks, keys, stage,
):
    share = lax.axis_index("seq")
    step = pl.program_id(0)

    @pl.when(step == 0)
    def _():
        total = jnp.zeros((1, LANES), f32)
        heap = jnp.zeros((SHARDS, LANES), f32)
        full = jnp.zeros((8, LANES), f32)
        for g in range(8):
            total = total + all_ref[g, 200:201, :]
            full = jnp.maximum(full, all_ref[g, 192:200, :])
            for x in range(RANKS):
                heap = heap + jnp.exp(all_ref[g, x * SHARDS : (x + 1) * SHARDS, :])
        full = jnp.where((iota((8, LANES), 1) & 15) == 14, full, 0.0)
        full = jnp.max(jnp.max(full, axis=0, keepdims=True), axis=1, keepdims=True)
        full_ref[...] = jnp.broadcast_to(full, (8, LANES))
        trans_ref[...] = jnp.broadcast_to(jnp.log(total), (8, LANES))
        emit_norm = jnp.log(jnp.sum(heap, axis=0, keepdims=True))
        emit_ref[...] = jnp.broadcast_to(emit_norm, (8, LANES))
        for g in range(8):
            rows = slice((g & 3) * 192, (g & 3) * 192 + 192)
            lanes = slice((g >> 2) * LANES, (g >> 2) * LANES + LANES)
            emits[rows, lanes] = jnp.exp(all_ref[g, 0:192, :] - emit_norm).astype(bf16)
        low = iota((LANES, LANES), 1) < KW
        for pair in range(4):
            first = exps_ref[pl.ds(2 * pair, LANES, stride=8), :] / total
            second = exps_ref[pl.ds(2 * pair + 1, LANES, stride=8), :] / total
            lanes = slice(pair * LANES, (pair + 1) * LANES)
            table[0:LANES, lanes] = jnp.where(low, first, pltpu.roll(second, KW, 1)).astype(bf16)
            table[LANES:, lanes] = jnp.where(low, pltpu.roll(first, KW, 1), second).astype(bf16)

    row, lane = iota((256, LANES), 0), iota((256, LANES), 1)
    chain_of = one_hot((iota((256, 8), 0) & 7) == iota((256, 8), 1))
    mine = ((lane >> 4) == ((row >> 3) & 7)) & ((lane & 3) == (row >> 6))
    next_at = mine & ((lane & 15) < 4)
    key_at = mine & ((lane & 15) >= 4) & ((lane & 15) < 12)
    ones = jnp.ones((LANES, LANES), bf16)
    weights = jnp.where((iota((LANES, LANES), 0) & 15) >= 8, 64.0, 1.0).astype(bf16)
    for part in range(2):
        asked = jnp.concatenate(
            [all_ref[g, pl.ds(192 + step * 2 + part, 1), :] for g in range(8)], axis=0
        ).astype(bf16)
        spread = jnp.dot(chain_of, asked, preferred_element_type=f32)
        block = jnp.dot(
            jnp.where(next_at, spread, 0.0).astype(bf16), ones, preferred_element_type=f32
        )
        key = jnp.dot(
            jnp.where(key_at, spread, 0.0).astype(bf16), weights, preferred_element_type=f32
        )
        for n in range(SLOTS):
            rows = slice(n * LANES + part * 64, n * LANES + part * 64 + 64)
            blocks[rows, :] = block[n * 64 : n * 64 + 64, :]
            keys[rows, :] = key[n * 64 : n * 64 + 64, :]
    lane_f = iota((512, LANES), 1).astype(f32)
    block, key = blocks[...], keys[...]
    second = key >= 2048.0
    key = jnp.where(second, key - 2048.0, key)
    late = key >= 768.0
    key = jnp.where(late, key - 768.0, key)
    hit = block == lane_f
    next_rows[:, :LANES] = one_hot(hit & ~second)
    next_rows[:, LANES:] = one_hot(hit & second)
    for n in range(6):
        word_rows[:, n * LANES : (n + 1) * LANES] = one_hot(key == lane_f + float(n * LANES))
    got = jnp.dot(word_rows[...], emits[...], preferred_element_type=f32)
    emit = jnp.where(late, got[:, LANES:], got[:, :LANES])
    emit = jnp.where((lane_f < float(KW)) ^ second, emit, pltpu.roll(emit, KW, 1))
    panels = jnp.dot(next_rows[...], table[...], preferred_element_type=f32)
    last = block == float(LANES)
    row_of = iota((512, LANES), 1) & (KW - 1)
    for pair in range(4):
        column = (pair * 2 + (iota((512, LANES), 1) >> 6)) * 8 + share
        panel = panels[:, pair * LANES : (pair + 1) * LANES]
        panel = jnp.where(last & (row_of == column), 1.0, panel) * emit
        for n in range(SLOTS):
            stage[pl.ds(n * 512 + pair, LANES, stride=4), :] = panel[n * LANES : (n + 1) * LANES, :]
    for n in range(SLOTS):
        block = stage[n * 512 : (n + 1) * 512, :].reshape(LANES, 4, LANES).astype(bf16)
        if n < SENT:
            panel_ref[:, :, n * LANES : (n + 1) * LANES] = block
        else:
            spare_ref[...] = block


def pick(exps, everything):
    vmem = pl.BlockSpec(memory_space=pltpu.VMEM)
    small = pl.BlockSpec((8, LANES), lambda i: (0, 0))
    return pl.pallas_call(
        pick_kernel,
        grid=(4,),
        out_shape=(
            jax.ShapeDtypeStruct((512, 4, SENT * LANES), bf16),
            jax.ShapeDtypeStruct((512, 4, LANES), bf16),
            jax.ShapeDtypeStruct((8, LANES), f32),
            jax.ShapeDtypeStruct((8, LANES), f32),
            jax.ShapeDtypeStruct((8, LANES), f32),
        ),
        in_specs=[vmem] * 2,
        out_specs=(
            pl.BlockSpec((LANES, 4, SENT * LANES), lambda i: (i, 0, 0)),
            pl.BlockSpec((LANES, 4, LANES), lambda i: (i, 0, 0)),
            small,
            small,
            small,
        ),
        scratch_shapes=[
            pltpu.VMEM((256, 512), bf16),
            pltpu.VMEM((768, 256), bf16),
            pltpu.VMEM((512, 256), bf16),
            pltpu.VMEM((512, 768), bf16),
            pltpu.VMEM((512, LANES), f32),
            pltpu.VMEM((512, LANES), f32),
            pltpu.VMEM((2048, LANES), f32),
        ],
        compiler_params=pltpu.CompilerParams(vmem_limit_bytes=60 * 1024 * 1024),
        name="pick",
    )(exps, everything)


def chain_kernel(slot_ref, panel_ref, spare_ref, out_ref, wide, ping, pong, logs, tops):
    length = slot_ref.shape[1]

    def widen(i, _):
        some = pl.ds(pl.multiple_of(i * 32, 32), 32)
        for n in range(SLOTS):
            if n < SENT:
                got = panel_ref[some, :, n * LANES : (n + 1) * LANES].astype(f32)
            else:
                got = spare_ref[some, :, :].astype(f32)
            rows = pl.ds(pl.multiple_of(n * 4096 + i * 256, 256), 256)
            wide[rows, :] = jnp.concatenate([got, got], axis=1).reshape(256, LANES)
        return 0

    lax.fori_loop(0, panel_ref.shape[0] // 32, widen, 0)
    low = iota((8, LANES), 1) < KW

    def build(i, _):
        for u in range(8):
            t = i * 8 + u
            start = slot_ref[0, t]
            parts = [wide[pl.ds(start + pair, 8, stride=8), :] for pair in range(4)]
            top = jnp.maximum(jnp.maximum(parts[0], parts[1]), jnp.maximum(parts[2], parts[3]))
            logs[pl.ds(t, 1), :] = jnp.max(top, axis=0, keepdims=True)
            move = []
            for part in parts:
                move += [jnp.where(low, part, 0.0), jnp.where(low, pltpu.roll(part, KW, 1), 0.0)]
            ping[t] = jnp.concatenate(move, axis=0).astype(bf16)
        return 0

    lax.fori_loop(0, length // 8, build, 0)
    peak = jnp.max(logs[0:length, :], axis=1, keepdims=True)
    tops[...] = jnp.broadcast_to((1.0 / peak).astype(bf16).astype(f32), (length, LANES))
    logs[0:length, :] = 1.0 / tops[...]
    logs[length:, :] = jnp.ones((length, LANES), f32)
    src, dst, count, base = ping, pong, length // 2, length
    while count > 1:
        unroll = min(count, 16)

        def level(i, _, src=src, dst=dst, unroll=unroll, base=base, first=src is ping and base == length):
            for u in range(unroll):
                n = i * unroll + u
                left, right = src[2 * n + 1][:, :KW], src[2 * n]
                if first:
                    left = left * tops[pl.ds(2 * n + 1, 1), :KW].astype(bf16)
                    right = right * tops[pl.ds(2 * n, 1), :].astype(bf16)
                prod = jnp.dot(left, right, preferred_element_type=f32)
                top = jnp.max(jnp.max(prod, axis=0, keepdims=True), axis=1, keepdims=True)
                logs[pl.ds(base + n, 1), :] = jnp.broadcast_to(top, (1, LANES))
                dst[n] = (prod * (1.0 / top)).astype(bf16)
            return 0

        lax.fori_loop(0, count // unroll, level, 0)
        src, dst, count, base = dst, src, count // 2, base + count
    prod = jnp.dot(src[1][:, :KW], src[0], preferred_element_type=f32)
    final = jnp.sum(jnp.sum(prod, axis=0, keepdims=True), axis=1, keepdims=True)
    scale = jnp.sum(jnp.log(logs[...]), axis=0, keepdims=True)
    total = jnp.log(final) + scale - jnp.log(jnp.full((1, LANES), 8192.0, f32))
    out_ref[...] = jnp.broadcast_to(total / length, (8, LANES))


def chain(slots, panels, spare):
    length = slots.shape[1]
    vmem = pl.BlockSpec(memory_space=pltpu.VMEM)
    return pl.pallas_call(
        chain_kernel,
        out_shape=jax.ShapeDtypeStruct((8, LANES), f32),
        in_specs=[pl.BlockSpec(memory_space=pltpu.SMEM), vmem, vmem],
        out_specs=vmem,
        scratch_shapes=[
            pltpu.VMEM((SLOTS * 4096, LANES), f32),
            pltpu.VMEM((length, KW, LANES), bf16),
            pltpu.VMEM((length // 2, KW, LANES), bf16),
            pltpu.VMEM((2 * length, LANES), f32),
            pltpu.VMEM((length, LANES), f32),
        ],
        compiler_params=pltpu.CompilerParams(vmem_limit_bytes=40 * 1024 * 1024),
        name="chain",
    )(slots, panels, spare)


def local(
    emit_states, trans_out, trans_in, word_emb, word_cluster, cluster_block, kept_parts, tokens
):
    msg, mat, slots = prep(
        kept_parts, tokens, word_cluster, cluster_block, emit_states, trans_out, trans_in, word_emb
    )
    arrived = lax.all_to_all(msg, "state", split_axis=0, concat_axis=0, tiled=True)
    exps, mine = score(arrived, mat)
    everything = lax.all_gather(mine, "seq", axis=0, tiled=False)
    panels, spare, trans_norm, emit_norm, full = pick(exps, everything)

    def exchange(value):
        return lax.all_to_all(value, ("state", "seq"), split_axis=0, concat_axis=0, tiled=True)

    got = exchange(panels)
    spare = lax.cond(full[0, 0] > 0.5, exchange, lambda value: value, spare)
    token_loglik = chain(slots, got, spare)
    return (token_loglik[0, :1], trans_norm[0], emit_norm[0])


def solution(mesh):
    placed = (
        P("state", None),
        P("state", None),
        P("state", None),
        P("state", None),
        P(),
        P(),
        P(),
        P(("state", "seq"), None),
    )
    return jax.shard_map(
        local,
        mesh=mesh,
        in_specs=placed,
        out_specs=(P(("state", "seq")), P("state"), P("state")),
        check_vma=False,
    )
```

```python
import jax
import jax.numpy as jnp
from jax import lax
from jax.experimental import pallas as pl
from jax.experimental.pallas import tpu as pltpu
from jax.sharding import PartitionSpec as P

BS = 256
PART = 32
KW = 64
LANES = 128
RANKS = 3
SHARDS = 64
PICK_VMEM = 60 * 1024 * 1024 + 512 * 1024
SLOTS = 4
SENT = 3
ROWS = 24
XROWS = 208
f32 = jnp.float32
bf16 = jnp.bfloat16
i32 = jnp.int32


def iota(shape, axis):
    return lax.broadcasted_iota(i32, shape, axis)


def one_hot(mask):
    return jnp.where(mask, 1.0, 0.0).astype(bf16)


def ints(mask, value):
    return jnp.where(mask, value, 0)


def prep_kernel(
    parts_ref, token_ref, tokens_hbm, cluster_hbm, table_hbm, emit_hbm, out_hbm, in_hbm, word_hbm,
    msg_ref, mat_ref, slot_ref,
    in_kept, slot_of, near, wide, counts_of, tokens_ref, cluster_ref, table_ref, word_ref, chosen, sems,
):
    me = lax.axis_index("state")
    share = lax.axis_index("seq")
    head = []
    for n, (src, dst) in enumerate(
        ((cluster_hbm, cluster_ref), (table_hbm, table_ref), (tokens_hbm, tokens_ref))
    ):
        head.append(pltpu.make_async_copy(src, dst, sems.at[n]))
        head[-1].start()
    word_copy = pltpu.make_async_copy(word_hbm, word_ref, sems.at[3])
    word_copy.start()
    kept = []
    for blk in range(2):
        for part in range(2):
            start = blk * BS + parts_ref[part, me * 2 + blk] * PART
            src = pl.ds(pl.multiple_of(start, PART), PART)
            at = (blk * 2 + part) * PART
            for which, (hbm, ref, to) in enumerate(
                ((in_hbm, in_kept, at), (out_hbm, mat_ref, at), (emit_hbm, mat_ref, 2 * KW + at))
            ):
                sem = sems.at[4 + (blk * 2 + part) * 3 + which]
                kept.append(pltpu.make_async_copy(hbm.at[src, :], ref.at[pl.ds(to, PART), :], sem))
                kept[-1].start()
    for copy in head:
        copy.wait()
    sub = iota((LANES, LANES), 0)
    lane = iota((LANES, LANES), 1)
    eye = sub == lane

    def column(row):
        return jnp.sum(ints(eye, row), axis=1, keepdims=True)

    def line(col):
        return jnp.sum(ints(eye, col), axis=0, keepdims=True)

    sums = jnp.concatenate([one_hot(sub < lane), jnp.ones((LANES, LANES), bf16)], axis=1)
    block_row = table_ref[...]
    block_col = column(block_row)
    block_col_f = block_col.astype(f32)
    carry = jnp.zeros((LANES, LANES), f32)
    chunks = 2048 // LANES
    own = pl.multiple_of(me * chunks, chunks)
    own_rows = cluster_ref[pl.ds(own, chunks), :]
    for c in range(chunks):
        hit = sub == own_rows[c : c + 1, :]
        found = jnp.dot(one_hot(hit), sums, preferred_element_type=f32)
        before = found[:, :LANES] + carry
        carry = carry + found[:, LANES:]
        rank = jnp.sum(jnp.where(hit, before, 0.0), axis=0, keepdims=True).astype(i32)
        block = jnp.sum(jnp.where(hit, block_col_f, 0.0), axis=0, keepdims=True).astype(i32)
        x = rank - RANKS * share
        slot = (block >> 1) * 8 + x * 2 + (block & 1)
        slot_of[c : c + 1, :] = jnp.where((x >= 0) & (x < RANKS), slot, -1)
    counts_of[...] = carry

    length = token_ref.shape[1]

    def pull(i, _):
        for u in range(8):
            t = i * 8 + u
            near[pl.ds(t, 1), :] = cluster_ref[pl.ds(token_ref[0, t] >> 7, 1), :]
        return 0

    lax.fori_loop(0, length // 8, pull, 0)
    token_col = column(tokens_ref[...])
    cluster_col = jnp.sum(ints(lane == (token_col & 127), near[...]), axis=1, keepdims=True)
    near[...] = jnp.broadcast_to(cluster_col, (LANES, LANES))
    place = iota((chunks, LANES), 0) * LANES + iota((chunks, LANES), 1)

    def tally(i, _):
        for u in range(8):
            t = i * 8 + u
            token = token_ref[0, t]
            shard_rows = cluster_ref[pl.ds(pl.multiple_of((token >> 11) * chunks, chunks), chunks), :]
            earlier = (shard_rows == near[pl.ds(t, 1), :]) & (place < (token & 2047))
            wide[pl.ds(t, 1), :] = jnp.sum(ints(earlier, 1), axis=0, keepdims=True)
        return 0

    lax.fori_loop(0, length // 8, tally, 0)
    rank_col = jnp.sum(wide[...], axis=1, keepdims=True)
    own_block_col = jnp.sum(ints(lane == cluster_col, block_row), axis=1, keepdims=True)
    own_block_row = line(own_block_col)
    same = (own_block_col >> 1) == (own_block_row >> 1)
    times_col = jnp.sum(ints(same & (lane < sub), 1), axis=1, keepdims=True)
    times_row = jnp.sum(ints(same & (sub < lane), 1), axis=0, keepdims=True)
    slot_ref[...] = times_row * 4096 + (own_block_row >> 1) * 64
    following = jnp.sum(ints(lane == sub + 1, own_block_row), axis=1, keepdims=True)
    following = jnp.where(iota((LANES, 1), 0) == length - 1, LANES, following)
    slots_col = (own_block_col >> 1) * SLOTS + times_col
    asked = jnp.zeros((SHARDS, LANES), f32)
    slot_line = iota((LANES, 2 * LANES), 1)
    at_slot = slot_line == slots_col
    owner = (iota((SHARDS, 2 * LANES), 1) >> 2) == iota((SHARDS, 2 * LANES), 0)
    slot_sub = iota((2 * LANES, LANES), 0) & 3
    slot_lane = iota((2 * LANES, LANES), 1)
    for field, values in enumerate((following, token_col >> 11, rank_col + 32 * (own_block_col & 1))):
        value_row = jnp.sum(ints(at_slot, values), axis=0, keepdims=True)
        spread = jnp.where(owner, value_row.astype(f32), 0.0).astype(bf16)
        asked += jnp.dot(
            spread, one_hot(slot_lane == field * 4 + slot_sub), preferred_element_type=f32
        )
    count_lane = jnp.where(lane == 12 + (block_col & 1), counts_of[...], 0.0).astype(bf16)
    count_owner = one_hot((block_row >> 1) == iota((SHARDS, LANES), 0))
    asked += jnp.dot(count_owner, count_lane, preferred_element_type=f32)
    full = jnp.max(times_row, axis=1, keepdims=True) >= SENT
    asked += jnp.where(full & (iota((SHARDS, LANES), 1) == 14), 1.0, 0.0)

    for copy in kept:
        copy.wait()
    row = iota((16, LANES), 0)
    want = (row >> 3) * KW + (row & 7) * 8 + share
    targets = jnp.dot(
        one_hot(iota((16, LANES), 1) == want), in_kept[...], preferred_element_type=f32
    ).astype(bf16)
    for to in range(SHARDS):
        msg_ref[to, 0:16, :] = targets
    for tile in range(4):
        for c in range(chunks):
            chosen[tile * LANES : (tile + 1) * LANES, c * LANES : (c + 1) * LANES] = one_hot(
                sub + tile * LANES == slot_of[c : c + 1, :]
            )
    word_copy.wait()
    request_row = iota((8, LANES), 0) == 6
    words = jnp.dot(chosen[...], word_ref[...], preferred_element_type=f32)
    for to in range(SHARDS):
        mine = words[to * 8 : to * 8 + 8, :]
        first = jnp.where(request_row, asked[to : to + 1, :], mine[:, :LANES])
        msg_ref[to, 16:24, :] = jnp.concatenate([first, mine[:, LANES:]], axis=1).astype(bf16)


def prep(kept_parts, tokens, word_cluster, cluster_block, emit_states, trans_out, trans_in, word_emb):
    width = emit_states.shape[1]
    vmem = pl.BlockSpec(memory_space=pltpu.VMEM)
    smem = pl.BlockSpec(memory_space=pltpu.SMEM)
    clusters = word_cluster.reshape(-1, LANES)
    return pl.pallas_call(
        prep_kernel,
        out_shape=(
            jax.ShapeDtypeStruct((SHARDS, ROWS, width), bf16),
            jax.ShapeDtypeStruct((4 * KW, width), bf16),
            jax.ShapeDtypeStruct((1, LANES), i32),
        ),
        in_specs=[smem, smem] + [pl.BlockSpec(memory_space=pltpu.HBM)] * 7,
        out_specs=(vmem, vmem, vmem),
        scratch_shapes=[
            pltpu.VMEM((2 * KW, width), bf16),
            pltpu.VMEM((16, LANES), i32),
            pltpu.VMEM((LANES, LANES), i32),
            pltpu.VMEM((LANES, LANES), i32),
            pltpu.VMEM((LANES, LANES), f32),
            pltpu.VMEM((1, LANES), i32),
            pltpu.VMEM(clusters.shape, i32),
            pltpu.VMEM((1, LANES), i32),
            pltpu.VMEM(word_emb.shape, bf16),
            pltpu.VMEM((8 * SHARDS, word_emb.shape[0]), bf16),
            pltpu.SemaphoreType.DMA((16,)),
        ],
        compiler_params=pltpu.CompilerParams(vmem_limit_bytes=60 * 1024 * 1024),
        name="prep",
    )(
        kept_parts.T, tokens, tokens, clusters, cluster_block[None, :],
        emit_states, trans_out, trans_in, word_emb,
    )


def thirds(value):
    high = value.astype(bf16).astype(f32)
    mid = (value - high).astype(bf16).astype(f32)
    return [high, mid, value - high - mid]


def score_kernel(msg_ref, mat_ref, exps_ref, out_ref, words, raw):
    share = lax.axis_index("seq")
    total = jnp.zeros((1, LANES), f32)
    for tile in range(8):
        got = msg_ref[tile * 8 : tile * 8 + 8].reshape(8 * ROWS, msg_ref.shape[2])
        res = lax.dot_general(
            got, mat_ref[...], (((1,), (1,)), ((), ())), preferred_element_type=f32
        ).reshape(8, ROWS, 2 * LANES)
        exps = jnp.exp(res[:, :16, :LANES]).reshape(LANES, LANES)
        exps_ref[tile * LANES : (tile + 1) * LANES, :] = exps
        total = total + jnp.sum(exps, axis=0, keepdims=True)
        words[tile * 64 : (tile + 1) * 64, :] = res[:, 16:, LANES:].reshape(64, LANES)
        raw[tile * 64 : (tile + 1) * 64, :] = (
            msg_ref[tile * 8 : tile * 8 + 8, 16:24, :LANES].astype(f32).reshape(64, LANES)
        )
    asked = raw[pl.ds(6, SHARDS, stride=8), :]
    spread = one_hot(iota((LANES, LANES), 0) == 12 + (iota((LANES, LANES), 1) >> 6))
    counts = jnp.dot(asked.astype(bf16), spread, preferred_element_type=f32)
    low = iota((SHARDS, LANES), 1) < KW
    scores, valid = [], []
    for x in range(RANKS):
        some = jnp.where(
            low,
            words[pl.ds(2 * x, SHARDS, stride=8), :],
            words[pl.ds(2 * x + 1, SHARDS, stride=8), :],
        )
        valid.append((RANKS * share + x).astype(f32) < counts)
        scores.append(jnp.where(valid[-1], some, -1e30))
    top = jnp.max(jnp.maximum(jnp.maximum(scores[0], scores[1]), scores[2]), axis=0, keepdims=True)
    top = top.astype(bf16).astype(f32)
    parts = [jnp.where(v, jnp.exp(s - top), 0.0) for s, v in zip(scores, valid)]
    mass = jnp.sum(parts[0] + parts[1] + parts[2], axis=0, keepdims=True)
    lane16 = iota((8, LANES), 1) >> 4
    packed = jnp.zeros((8, LANES), f32)
    for m in range(8):
        some = raw[pl.ds(m * 8 + 6, 8, stride=64), :]
        some = pltpu.roll(some, m * 16, 1) if m else some
        packed = jnp.where(lane16 == m, some, packed)
    sums = jnp.concatenate([top] + thirds(mass) + thirds(total) + [jnp.zeros_like(top)], axis=0)
    message = jnp.concatenate(parts + [packed, sums], axis=0).astype(bf16)
    for copy in range(4):
        out_ref[copy] = message


def score(msg, mat):
    vmem = pl.BlockSpec(memory_space=pltpu.VMEM)
    return pl.pallas_call(
        score_kernel,
        out_shape=(
            jax.ShapeDtypeStruct((1024, LANES), f32),
            jax.ShapeDtypeStruct((4, XROWS, LANES), bf16),
        ),
        in_specs=[vmem] * 2,
        out_specs=(vmem, vmem),
        scratch_shapes=[pltpu.VMEM((512, LANES), f32), pltpu.VMEM((512, LANES), f32)],
        compiler_params=pltpu.CompilerParams(vmem_limit_bytes=40 * 1024 * 1024),
        name="score",
    )(msg, mat)


def pick_kernel(
    exps_ref, all_ref, panel_hbm, spare_hbm, trans_ref, emit_ref, full_ref,
    table, emits, next_rows, word_rows, blocks, keys, stage, panel_ref, spare_ref, sems,
):
    share = lax.axis_index("seq")
    order = [(g & 1) * 4 + (g >> 1) for g in range(8)]
    if True:
        sums = [all_ref[n, 200:208, :].astype(f32) for n in order]
        total = jnp.zeros((1, LANES), f32)
        top = sums[0][0:1, :]
        full = jnp.zeros((8, LANES), f32)
        for g in range(8):
            total = total + (sums[g][4:5, :] + sums[g][5:6, :] + sums[g][6:7, :])
            top = jnp.maximum(top, sums[g][0:1, :])
            full = jnp.maximum(full, all_ref[order[g], 192:200, :].astype(f32))
        mass = jnp.zeros((1, LANES), f32)
        for g in range(8):
            part = sums[g][1:2, :] + sums[g][2:3, :] + sums[g][3:4, :]
            mass = mass + part * jnp.exp(sums[g][0:1, :] - top)
        full = jnp.where((iota((8, LANES), 1) & 15) == 14, full, 0.0)
        full = jnp.max(jnp.max(full, axis=0, keepdims=True), axis=1, keepdims=True)
        full_ref[...] = jnp.broadcast_to(full, (8, LANES))
        trans_ref[...] = jnp.broadcast_to(jnp.log(total), (8, LANES))
        emit_norm = top + jnp.log(mass)
        emit_ref[...] = jnp.broadcast_to(emit_norm, (8, LANES))
        for g in range(8):
            rows = slice((g & 3) * 192, (g & 3) * 192 + 192)
            lanes = slice((g >> 2) * LANES, (g >> 2) * LANES + LANES)
            scale = jnp.exp(sums[g][0:1, :] - emit_norm)
            emits[rows, lanes] = (all_ref[order[g], 0:192, :].astype(f32) * scale).astype(bf16)
        low = iota((LANES, LANES), 1) < KW
        for pair in range(4):
            first = exps_ref[pl.ds(2 * pair, LANES, stride=8), :] / total
            second = exps_ref[pl.ds(2 * pair + 1, LANES, stride=8), :] / total
            lanes = slice(pair * LANES, (pair + 1) * LANES)
            table[0:LANES, lanes] = jnp.where(low, first, pltpu.roll(second, KW, 1)).astype(bf16)
            table[LANES:, lanes] = jnp.where(low, pltpu.roll(first, KW, 1), second).astype(bf16)

    row, lane = iota((512, LANES), 0), iota((512, LANES), 1)
    pick_row, pick_lane = iota((512, 64), 0), iota((512, 64), 1)
    mine = ((lane >> 4) == ((row >> 3) & 7)) & ((lane & 3) == (row >> 7))
    next_at = mine & ((lane & 15) < 4)
    key_at = mine & ((lane & 15) >= 4) & ((lane & 15) < 12)
    ones = jnp.ones((LANES, LANES), bf16)
    weights = jnp.where((iota((LANES, LANES), 0) & 15) >= 8, 64.0, 1.0).astype(bf16)
    asked = jnp.concatenate([all_ref[n, 192:200, :].astype(f32) for n in order], axis=0)
    asked = asked.astype(bf16)
    lane_f = lane.astype(f32)
    row_of = lane & (KW - 1)
    copies = []
    for step in range(4):
        source = (pick_row & 7) * 8 + step * 2 + ((pick_row >> 6) & 1)
        spread = jnp.dot(one_hot(pick_lane == source), asked, preferred_element_type=f32)
        block = jnp.dot(
            jnp.where(next_at, spread, 0.0).astype(bf16), ones, preferred_element_type=f32
        )
        key = jnp.dot(
            jnp.where(key_at, spread, 0.0).astype(bf16), weights, preferred_element_type=f32
        )
        blocks[step * 512 : (step + 1) * 512, :] = block
        keys[step * 512 : (step + 1) * 512, :] = key
    for step in range(4):
        rows = slice(step * 512, (step + 1) * 512)
        block, key = blocks[rows, :], keys[rows, :]
        second = key >= 2048.0
        key = jnp.where(second, key - 2048.0, key)
        key = jnp.where(key >= 768.0, key - 768.0, key)
        hit = block == lane_f
        next_rows[rows, :LANES] = one_hot(hit & ~second)
        next_rows[rows, LANES:] = one_hot(hit & second)
        for n in range(6):
            word_rows[rows, n * LANES : (n + 1) * LANES] = one_hot(key == lane_f + float(n * LANES))
    for step in range(4):
        rows = slice(step * 512, (step + 1) * 512)
        got = jnp.dot(word_rows[rows, :], emits[...], preferred_element_type=f32)
        panels = jnp.dot(next_rows[rows, :], table[...], preferred_element_type=f32)
        block, key = blocks[rows, :], keys[rows, :]
        second = key >= 2048.0
        late = jnp.where(second, key - 2048.0, key) >= 768.0
        emit = jnp.where(late, got[:, LANES:], got[:, :LANES])
        emit = jnp.where((lane_f < float(KW)) ^ second, emit, pltpu.roll(emit, KW, 1))
        last = block == float(LANES)
        for pair in range(4):
            column = (pair * 2 + (lane >> 6)) * 8 + share
            panel = panels[:, pair * LANES : (pair + 1) * LANES]
            panel = jnp.where(last & (row_of == column), 1.0, panel) * emit
            for n in range(SLOTS):
                stage[pl.ds(step * 2048 + n * 512 + pair, LANES, stride=4), :] = panel[
                    n * LANES : (n + 1) * LANES, :
                ]
        for n in range(SLOTS):
            block = stage[step * 2048 + n * 512 : step * 2048 + (n + 1) * 512, :]
            block = block.reshape(LANES, 4, LANES).astype(bf16)
            if n < SENT:
                panel_ref[step * LANES : (step + 1) * LANES, :, n * LANES : (n + 1) * LANES] = block
            else:
                spare_ref[step * LANES : (step + 1) * LANES, :, :] = block
        some = pl.ds(step * LANES, LANES)
        for n, (ref, hbm) in enumerate(((panel_ref, panel_hbm), (spare_ref, spare_hbm))):
            copies.append(pltpu.make_async_copy(ref.at[some], hbm.at[some], sems.at[step * 2 + n]))
            copies[-1].start()
    for copy in copies:
        copy.wait()


def pick(exps, everything):
    vmem = pl.BlockSpec(memory_space=pltpu.VMEM)
    return pl.pallas_call(
        pick_kernel,
        out_shape=(
            jax.ShapeDtypeStruct((512, 4, SENT * LANES), bf16),
            jax.ShapeDtypeStruct((512, 4, LANES), bf16),
            jax.ShapeDtypeStruct((8, LANES), f32),
            jax.ShapeDtypeStruct((8, LANES), f32),
            jax.ShapeDtypeStruct((8, LANES), f32),
        ),
        in_specs=[vmem] * 2,
        out_specs=(pl.BlockSpec(memory_space=pl.ANY),) * 2 + (vmem,) * 3,
        scratch_shapes=[
            pltpu.VMEM((256, 512), bf16),
            pltpu.VMEM((768, 256), bf16),
            pltpu.VMEM((2048, 256), bf16),
            pltpu.VMEM((2048, 768), bf16),
            pltpu.VMEM((2048, LANES), f32),
            pltpu.VMEM((2048, LANES), f32),
            pltpu.VMEM((8192, LANES), f32),
            pltpu.VMEM((512, 4, SENT * LANES), bf16),
            pltpu.VMEM((512, 4, LANES), bf16),
            pltpu.SemaphoreType.DMA((8,)),
        ],
        compiler_params=pltpu.CompilerParams(vmem_limit_bytes=PICK_VMEM),
        name="pick",
    )(exps, everything)


def chain_kernel(slot_ref, panel_ref, spare_ref, out_ref, wide, ping, pong, logs, tops):
    length = slot_ref.shape[1]

    def widen(i, _):
        some = pl.ds(pl.multiple_of(i * 32, 32), 32)
        for n in range(SLOTS):
            if n < SENT:
                got = panel_ref[some, :, n * LANES : (n + 1) * LANES].astype(f32)
            else:
                got = spare_ref[some, :, :].astype(f32)
            rows = pl.ds(pl.multiple_of(n * 4096 + i * 256, 256), 256)
            wide[rows, :] = jnp.concatenate([got, got], axis=1).reshape(256, LANES)
        return 0

    lax.fori_loop(0, panel_ref.shape[0] // 32, widen, 0)
    low = iota((8, LANES), 1) < KW

    def build(i, _):
        for u in range(8):
            t = i * 8 + u
            start = slot_ref[0, t]
            parts = [wide[pl.ds(start + pair, 8, stride=8), :] for pair in range(4)]
            top = jnp.maximum(jnp.maximum(parts[0], parts[1]), jnp.maximum(parts[2], parts[3]))
            logs[pl.ds(t, 1), :] = jnp.max(top, axis=0, keepdims=True)
            move = []
            for part in parts:
                move += [jnp.where(low, part, 0.0), jnp.where(low, pltpu.roll(part, KW, 1), 0.0)]
            ping[t] = jnp.concatenate(move, axis=0).astype(bf16)
        return 0

    lax.fori_loop(0, length // 8, build, 0)
    peak = jnp.max(logs[0:length, :], axis=1, keepdims=True)
    tops[...] = jnp.broadcast_to((1.0 / peak).astype(bf16).astype(f32), (length, LANES))
    logs[0:length, :] = 1.0 / tops[...]
    logs[length:, :] = jnp.ones((length, LANES), f32)
    src, dst, count, base = ping, pong, length // 2, length
    while count > 1:
        unroll = min(count, 16)

        def level(i, _, src=src, dst=dst, unroll=unroll, base=base, first=src is ping and base == length):
            for u in range(unroll):
                n = i * unroll + u
                left, right = src[2 * n + 1][:, :KW], src[2 * n]
                if first:
                    left = left * tops[pl.ds(2 * n + 1, 1), :KW].astype(bf16)
                    right = right * tops[pl.ds(2 * n, 1), :].astype(bf16)
                prod = jnp.dot(left, right, preferred_element_type=f32)
                top = jnp.max(jnp.max(prod, axis=0, keepdims=True), axis=1, keepdims=True)
                logs[pl.ds(base + n, 1), :] = jnp.broadcast_to(top, (1, LANES))
                dst[n] = (prod * (1.0 / top)).astype(bf16)
            return 0

        lax.fori_loop(0, count // unroll, level, 0)
        src, dst, count, base = dst, src, count // 2, base + count
    prod = jnp.dot(src[1][:, :KW], src[0], preferred_element_type=f32)
    final = jnp.sum(jnp.sum(prod, axis=0, keepdims=True), axis=1, keepdims=True)
    scale = jnp.sum(jnp.log(logs[...]), axis=0, keepdims=True)
    total = jnp.log(final) + scale - jnp.log(jnp.full((1, LANES), 8192.0, f32))
    out_ref[...] = jnp.broadcast_to(total / length, (8, LANES))


def chain(slots, panels, spare):
    length = slots.shape[1]
    vmem = pl.BlockSpec(memory_space=pltpu.VMEM)
    return pl.pallas_call(
        chain_kernel,
        out_shape=jax.ShapeDtypeStruct((8, LANES), f32),
        in_specs=[pl.BlockSpec(memory_space=pltpu.SMEM), vmem, vmem],
        out_specs=vmem,
        scratch_shapes=[
            pltpu.VMEM((SLOTS * 4096, LANES), f32),
            pltpu.VMEM((length, KW, LANES), bf16),
            pltpu.VMEM((length // 2, KW, LANES), bf16),
            pltpu.VMEM((2 * length, LANES), f32),
            pltpu.VMEM((length, LANES), f32),
        ],
        compiler_params=pltpu.CompilerParams(vmem_limit_bytes=40 * 1024 * 1024),
        name="chain",
    )(slots, panels, spare)


def local(
    emit_states, trans_out, trans_in, word_emb, word_cluster, cluster_block, kept_parts, tokens
):
    msg, mat, slots = prep(
        kept_parts, tokens, word_cluster, cluster_block, emit_states, trans_out, trans_in, word_emb
    )
    arrived = lax.all_to_all(msg, "state", split_axis=0, concat_axis=0, tiled=True)
    exps, mine = score(arrived, mat)
    along_x = lax.all_to_all(
        mine, "seq", split_axis=0, concat_axis=0, tiled=True,
        axis_index_groups=[[0, 2, 4, 6], [1, 3, 5, 7]],
    )
    everything = lax.all_gather(
        along_x, "seq", axis=0, tiled=True, axis_index_groups=[[0, 1], [2, 3], [4, 5], [6, 7]]
    )
    panels, spare, trans_norm, emit_norm, full = pick(exps, everything)

    def exchange(value):
        return lax.all_to_all(value, ("state", "seq"), split_axis=0, concat_axis=0, tiled=True)

    got = exchange(panels)
    spare = lax.cond(full[0, 0] > 0.5, exchange, lambda value: value, spare)
    token_loglik = chain(slots, got, spare)
    return (token_loglik[0, :1], trans_norm[0], emit_norm[0])


def solution(mesh):
    placed = (
        P("state", None),
        P("state", None),
        P("state", None),
        P("state", None),
        P(),
        P(),
        P(),
        P(("state", "seq"), None),
    )
    return jax.shard_map(
        local,
        mesh=mesh,
        in_specs=placed,
        out_specs=(P(("state", "seq")), P("state"), P("state")),
        check_vma=False,
    )
```

```python
import jax
import jax.numpy as jnp
from jax import lax
from jax.experimental import pallas as pl
from jax.experimental.pallas import tpu as pltpu
from jax.sharding import PartitionSpec as P

BS = 256
PART = 32
KW = 64
LANES = 128
RANKS = 3
SHARDS = 64
SLOTS = 4
SENT = 3
ROWS = 24
XROWS = 208
f32 = jnp.float32
bf16 = jnp.bfloat16
i32 = jnp.int32


def iota(shape, axis):
    return lax.broadcasted_iota(i32, shape, axis)


def one_hot(mask):
    return jnp.where(mask, 1.0, 0.0).astype(bf16)


def ints(mask, value):
    return jnp.where(mask, value, 0)


def prep_kernel(
    parts_ref, token_ref, tokens_hbm, cluster_hbm, table_hbm, emit_hbm, out_hbm, in_hbm, word_hbm,
    msg_ref, mat_ref, slot_ref,
    in_kept, slot_of, near, wide, counts_of, tokens_ref, cluster_ref, table_ref, word_ref, chosen, sems,
):
    me = lax.axis_index("state")
    share = lax.axis_index("seq")
    head = []
    for n, (src, dst) in enumerate(
        ((cluster_hbm, cluster_ref), (table_hbm, table_ref), (tokens_hbm, tokens_ref))
    ):
        head.append(pltpu.make_async_copy(src, dst, sems.at[n]))
        head[-1].start()
    word_copy = pltpu.make_async_copy(word_hbm, word_ref, sems.at[3])
    word_copy.start()
    kept = []
    for blk in range(2):
        for part in range(2):
            start = blk * BS + parts_ref[part, me * 2 + blk] * PART
            src = pl.ds(pl.multiple_of(start, PART), PART)
            at = (blk * 2 + part) * PART
            for which, (hbm, ref, to) in enumerate(
                ((in_hbm, in_kept, at), (out_hbm, mat_ref, at), (emit_hbm, mat_ref, 2 * KW + at))
            ):
                sem = sems.at[4 + (blk * 2 + part) * 3 + which]
                kept.append(pltpu.make_async_copy(hbm.at[src, :], ref.at[pl.ds(to, PART), :], sem))
                kept[-1].start()
    for copy in head:
        copy.wait()
    sub = iota((LANES, LANES), 0)
    lane = iota((LANES, LANES), 1)
    eye = sub == lane

    def column(row):
        return jnp.sum(ints(eye, row), axis=1, keepdims=True)

    def line(col):
        return jnp.sum(ints(eye, col), axis=0, keepdims=True)

    sums = jnp.concatenate([one_hot(sub < lane), jnp.ones((LANES, LANES), bf16)], axis=1)
    block_row = table_ref[...]
    block_col = column(block_row)
    block_col_f = block_col.astype(f32)
    carry = jnp.zeros((LANES, LANES), f32)
    chunks = 2048 // LANES
    own = pl.multiple_of(me * chunks, chunks)
    own_rows = cluster_ref[pl.ds(own, chunks), :]
    for c in range(chunks):
        hit = sub == own_rows[c : c + 1, :]
        found = jnp.dot(one_hot(hit), sums, preferred_element_type=f32)
        before = found[:, :LANES] + carry
        carry = carry + found[:, LANES:]
        rank = jnp.sum(jnp.where(hit, before, 0.0), axis=0, keepdims=True).astype(i32)
        block = jnp.sum(jnp.where(hit, block_col_f, 0.0), axis=0, keepdims=True).astype(i32)
        x = rank - RANKS * share
        slot = (block >> 1) * 8 + x * 2 + (block & 1)
        slot_of[c : c + 1, :] = jnp.where((x >= 0) & (x < RANKS), slot, -1)
    counts_of[...] = carry

    length = token_ref.shape[1]

    for t in range(length):
        near[t : t + 1, :] = cluster_ref[pl.ds(token_ref[0, t] >> 7, 1), :]
    token_col = column(tokens_ref[...])
    cluster_col = jnp.sum(ints(lane == (token_col & 127), near[...]), axis=1, keepdims=True)
    near[...] = jnp.broadcast_to(cluster_col, (LANES, LANES))
    place = iota((chunks, LANES), 0) * LANES + iota((chunks, LANES), 1)

    for t in range(length):
        token = token_ref[0, t]
        shard_rows = cluster_ref[pl.ds(pl.multiple_of((token >> 11) * chunks, chunks), chunks), :]
        earlier = (shard_rows == near[t : t + 1, :]) & (place < (token & 2047))
        wide[t : t + 1, :] = jnp.sum(ints(earlier, 1), axis=0, keepdims=True)
    rank_col = jnp.sum(wide[...], axis=1, keepdims=True)
    own_block_col = jnp.sum(ints(lane == cluster_col, block_row), axis=1, keepdims=True)
    own_block_row = line(own_block_col)
    same = (own_block_col >> 1) == (own_block_row >> 1)
    times_col = jnp.sum(ints(same & (lane < sub), 1), axis=1, keepdims=True)
    times_row = jnp.sum(ints(same & (sub < lane), 1), axis=0, keepdims=True)
    slot_ref[...] = times_row * 4096 + (own_block_row >> 1) * 64
    following = jnp.sum(ints(lane == sub + 1, own_block_row), axis=1, keepdims=True)
    following = jnp.where(iota((LANES, 1), 0) == length - 1, LANES, following)
    slots_col = (own_block_col >> 1) * SLOTS + times_col
    asked = jnp.zeros((SHARDS, LANES), f32)
    slot_line = iota((LANES, 2 * LANES), 1)
    at_slot = slot_line == slots_col
    owner = (iota((SHARDS, 2 * LANES), 1) >> 2) == iota((SHARDS, 2 * LANES), 0)
    slot_sub = iota((2 * LANES, LANES), 0) & 3
    slot_lane = iota((2 * LANES, LANES), 1)
    for field, values in enumerate((following, token_col >> 11, rank_col + 32 * (own_block_col & 1))):
        value_row = jnp.sum(ints(at_slot, values), axis=0, keepdims=True)
        spread = jnp.where(owner, value_row.astype(f32), 0.0).astype(bf16)
        asked += jnp.dot(
            spread, one_hot(slot_lane == field * 4 + slot_sub), preferred_element_type=f32
        )
    count_lane = jnp.where(lane == 12 + (block_col & 1), counts_of[...], 0.0).astype(bf16)
    count_owner = one_hot((block_row >> 1) == iota((SHARDS, LANES), 0))
    asked += jnp.dot(count_owner, count_lane, preferred_element_type=f32)
    full = jnp.max(times_row, axis=1, keepdims=True) >= SENT
    asked += jnp.where(full & (iota((SHARDS, LANES), 1) == 14), 1.0, 0.0)

    for copy in kept:
        copy.wait()
    row = iota((16, LANES), 0)
    want = (row >> 3) * KW + (row & 7) * 8 + share
    targets = jnp.dot(
        one_hot(iota((16, LANES), 1) == want), in_kept[...], preferred_element_type=f32
    ).astype(bf16)
    for to in range(SHARDS):
        msg_ref[to, 0:16, :] = targets
    for tile in range(4):
        for c in range(chunks):
            chosen[tile * LANES : (tile + 1) * LANES, c * LANES : (c + 1) * LANES] = one_hot(
                sub + tile * LANES == slot_of[c : c + 1, :]
            )
    word_copy.wait()
    request_row = iota((8, LANES), 0) == 6
    words = jnp.dot(chosen[...], word_ref[...], preferred_element_type=f32)
    for to in range(SHARDS):
        mine = words[to * 8 : to * 8 + 8, :]
        first = jnp.where(request_row, asked[to : to + 1, :], mine[:, :LANES])
        msg_ref[to, 16:24, :] = jnp.concatenate([first, mine[:, LANES:]], axis=1).astype(bf16)


def prep(kept_parts, tokens, word_cluster, cluster_block, emit_states, trans_out, trans_in, word_emb):
    width = emit_states.shape[1]
    vmem = pl.BlockSpec(memory_space=pltpu.VMEM)
    smem = pl.BlockSpec(memory_space=pltpu.SMEM)
    clusters = word_cluster.reshape(-1, LANES)
    return pl.pallas_call(
        prep_kernel,
        out_shape=(
            jax.ShapeDtypeStruct((SHARDS, ROWS, width), bf16),
            jax.ShapeDtypeStruct((4 * KW, width), bf16),
            jax.ShapeDtypeStruct((1, LANES), i32),
        ),
        in_specs=[smem, smem] + [pl.BlockSpec(memory_space=pltpu.HBM)] * 7,
        out_specs=(vmem, vmem, vmem),
        scratch_shapes=[
            pltpu.VMEM((2 * KW, width), bf16),
            pltpu.VMEM((16, LANES), i32),
            pltpu.VMEM((LANES, LANES), i32),
            pltpu.VMEM((LANES, LANES), i32),
            pltpu.VMEM((LANES, LANES), f32),
            pltpu.VMEM((1, LANES), i32),
            pltpu.VMEM(clusters.shape, i32),
            pltpu.VMEM((1, LANES), i32),
            pltpu.VMEM(word_emb.shape, bf16),
            pltpu.VMEM((8 * SHARDS, word_emb.shape[0]), bf16),
            pltpu.SemaphoreType.DMA((16,)),
        ],
        compiler_params=pltpu.CompilerParams(vmem_limit_bytes=60 * 1024 * 1024),
        name="prep",
    )(
        kept_parts.T, tokens, tokens, clusters, cluster_block[None, :],
        emit_states, trans_out, trans_in, word_emb,
    )


def thirds(value):
    high = value.astype(bf16).astype(f32)
    mid = (value - high).astype(bf16).astype(f32)
    return [high, mid, value - high - mid]


def score_kernel(msg_ref, mat_ref, exps_ref, out_ref, words, raw):
    share = lax.axis_index("seq")
    total = jnp.zeros((1, LANES), f32)
    for tile in range(8):
        got = msg_ref[tile * 8 : tile * 8 + 8].reshape(8 * ROWS, msg_ref.shape[2])
        res = lax.dot_general(
            got, mat_ref[...], (((1,), (1,)), ((), ())), preferred_element_type=f32
        ).reshape(8, ROWS, 2 * LANES)
        exps = jnp.exp(res[:, :16, :LANES]).reshape(LANES, LANES)
        exps_ref[tile * LANES : (tile + 1) * LANES, :] = exps
        total = total + jnp.sum(exps, axis=0, keepdims=True)
        words[tile * 64 : (tile + 1) * 64, :] = res[:, 16:, LANES:].reshape(64, LANES)
        raw[tile * 64 : (tile + 1) * 64, :] = (
            msg_ref[tile * 8 : tile * 8 + 8, 16:24, :LANES].astype(f32).reshape(64, LANES)
        )
    asked = raw[pl.ds(6, SHARDS, stride=8), :]
    spread = one_hot(iota((LANES, LANES), 0) == 12 + (iota((LANES, LANES), 1) >> 6))
    counts = jnp.dot(asked.astype(bf16), spread, preferred_element_type=f32)
    low = iota((SHARDS, LANES), 1) < KW
    scores, valid = [], []
    for x in range(RANKS):
        some = jnp.where(
            low,
            words[pl.ds(2 * x, SHARDS, stride=8), :],
            words[pl.ds(2 * x + 1, SHARDS, stride=8), :],
        )
        valid.append((RANKS * share + x).astype(f32) < counts)
        scores.append(jnp.where(valid[-1], some, -1e30))
    top = jnp.max(jnp.maximum(jnp.maximum(scores[0], scores[1]), scores[2]), axis=0, keepdims=True)
    top = top.astype(bf16).astype(f32)
    parts = [jnp.where(v, jnp.exp(s - top), 0.0) for s, v in zip(scores, valid)]
    mass = jnp.sum(parts[0] + parts[1] + parts[2], axis=0, keepdims=True)
    lane16 = iota((8, LANES), 1) >> 4
    packed = jnp.zeros((8, LANES), f32)
    for m in range(8):
        some = raw[pl.ds(m * 8 + 6, 8, stride=64), :]
        some = pltpu.roll(some, m * 16, 1) if m else some
        packed = jnp.where(lane16 == m, some, packed)
    sums = jnp.concatenate([top] + thirds(mass) + thirds(total) + [jnp.zeros_like(top)], axis=0)
    message = jnp.concatenate(parts + [packed, sums], axis=0).astype(bf16)
    for copy in range(4):
        out_ref[copy] = message


def score(msg, mat):
    vmem = pl.BlockSpec(memory_space=pltpu.VMEM)
    return pl.pallas_call(
        score_kernel,
        out_shape=(
            jax.ShapeDtypeStruct((1024, LANES), f32),
            jax.ShapeDtypeStruct((4, XROWS, LANES), bf16),
        ),
        in_specs=[vmem] * 2,
        out_specs=(vmem, vmem),
        scratch_shapes=[pltpu.VMEM((512, LANES), f32), pltpu.VMEM((512, LANES), f32)],
        compiler_params=pltpu.CompilerParams(vmem_limit_bytes=40 * 1024 * 1024),
        name="score",
    )(msg, mat)


def pick_kernel(
    exps_ref, all_ref, panel_ref, spare_ref, trans_ref, emit_ref, full_ref,
    table, emits, next_rows, word_rows, blocks, keys, stage,
):
    share = lax.axis_index("seq")
    order = [(g & 1) * 4 + (g >> 1) for g in range(8)]
    sums = [all_ref[n, 200:208, :].astype(f32) for n in order]
    total = jnp.zeros((1, LANES), f32)
    top = sums[0][0:1, :]
    full = jnp.zeros((8, LANES), f32)
    for g in range(8):
        total = total + (sums[g][4:5, :] + sums[g][5:6, :] + sums[g][6:7, :])
        top = jnp.maximum(top, sums[g][0:1, :])
        full = jnp.maximum(full, all_ref[order[g], 192:200, :].astype(f32))
    mass = jnp.zeros((1, LANES), f32)
    for g in range(8):
        part = sums[g][1:2, :] + sums[g][2:3, :] + sums[g][3:4, :]
        mass = mass + part * jnp.exp(sums[g][0:1, :] - top)
    full = jnp.where((iota((8, LANES), 1) & 15) == 14, full, 0.0)
    full = jnp.max(jnp.max(full, axis=0, keepdims=True), axis=1, keepdims=True)
    full_ref[...] = full.astype(i32)
    trans_ref[...] = jnp.log(total)
    emit_norm = top + jnp.log(mass)
    emit_ref[...] = emit_norm
    for g in range(8):
        rows = slice((g & 3) * 192, (g & 3) * 192 + 192)
        lanes = slice((g >> 2) * LANES, (g >> 2) * LANES + LANES)
        scale = jnp.exp(sums[g][0:1, :] - emit_norm)
        emits[rows, lanes] = (all_ref[order[g], 0:192, :].astype(f32) * scale).astype(bf16)
    low = iota((LANES, LANES), 1) < KW
    for pair in range(4):
        first = exps_ref[pl.ds(2 * pair, LANES, stride=8), :] / total
        second = exps_ref[pl.ds(2 * pair + 1, LANES, stride=8), :] / total
        lanes = slice(pair * LANES, (pair + 1) * LANES)
        table[0:LANES, lanes] = jnp.where(low, first, pltpu.roll(second, KW, 1)).astype(bf16)
        table[LANES:, lanes] = jnp.where(low, pltpu.roll(first, KW, 1), second).astype(bf16)

    row, lane = iota((512, LANES), 0), iota((512, LANES), 1)
    pick_row, pick_lane = iota((512, 64), 0), iota((512, 64), 1)
    mine = ((lane >> 4) == ((row >> 3) & 7)) & ((lane & 3) == (row >> 7))
    next_at = mine & ((lane & 15) < 4)
    key_at = mine & ((lane & 15) >= 4) & ((lane & 15) < 12)
    ones = jnp.ones((LANES, LANES), bf16)
    weights = jnp.where((iota((LANES, LANES), 0) & 15) >= 8, 64.0, 1.0).astype(bf16)
    asked = jnp.concatenate([all_ref[n, 192:200, :].astype(f32) for n in order], axis=0)
    asked = asked.astype(bf16)
    lane_f = lane.astype(f32)
    row_of = lane & (KW - 1)
    for step in range(4):
        source = (pick_row & 7) * 8 + step * 2 + ((pick_row >> 6) & 1)
        spread = jnp.dot(one_hot(pick_lane == source), asked, preferred_element_type=f32)
        block = jnp.dot(
            jnp.where(next_at, spread, 0.0).astype(bf16), ones, preferred_element_type=f32
        )
        key = jnp.dot(
            jnp.where(key_at, spread, 0.0).astype(bf16), weights, preferred_element_type=f32
        )
        blocks[step * 512 : (step + 1) * 512, :] = block
        keys[step * 512 : (step + 1) * 512, :] = key
    for step in range(4):
        rows = slice(step * 512, (step + 1) * 512)
        block, key = blocks[rows, :], keys[rows, :]
        second = key >= 2048.0
        key = jnp.where(second, key - 2048.0, key)
        key = jnp.where(key >= 768.0, key - 768.0, key)
        hit = block == lane_f
        next_rows[rows, :LANES] = one_hot(hit & ~second)
        next_rows[rows, LANES:] = one_hot(hit & second)
        for n in range(6):
            word_rows[rows, n * LANES : (n + 1) * LANES] = one_hot(key == lane_f + float(n * LANES))
    for step in range(4):
        rows = slice(step * 512, (step + 1) * 512)
        got = jnp.dot(word_rows[rows, :], emits[...], preferred_element_type=f32)
        panels = jnp.dot(next_rows[rows, :], table[...], preferred_element_type=f32)
        block, key = blocks[rows, :], keys[rows, :]
        second = key >= 2048.0
        late = jnp.where(second, key - 2048.0, key) >= 768.0
        emit = jnp.where(late, got[:, LANES:], got[:, :LANES])
        emit = jnp.where((lane_f < float(KW)) ^ second, emit, pltpu.roll(emit, KW, 1))
        last = block == float(LANES)
        for pair in range(4):
            column = (pair * 2 + (lane >> 6)) * 8 + share
            panel = panels[:, pair * LANES : (pair + 1) * LANES]
            panel = jnp.where(last & (row_of == column), 1.0, panel) * emit
            for n in range(SLOTS):
                stage[pl.ds(step * 2048 + n * 512 + pair, LANES, stride=4), :] = panel[
                    n * LANES : (n + 1) * LANES, :
                ]
        for n in range(SLOTS):
            block = stage[step * 2048 + n * 512 : step * 2048 + (n + 1) * 512, :]
            block = block.reshape(LANES, 4, LANES).astype(bf16)
            if n < SENT:
                panel_ref[step * LANES : (step + 1) * LANES, :, n * LANES : (n + 1) * LANES] = block
            else:
                spare_ref[step * LANES : (step + 1) * LANES, :, :] = block


def pick(exps, everything):
    vmem = pl.BlockSpec(memory_space=pltpu.VMEM)
    return pl.pallas_call(
        pick_kernel,
        out_shape=(
            jax.ShapeDtypeStruct((512, 4, SENT * LANES), bf16),
            jax.ShapeDtypeStruct((512, 4, LANES), bf16),
            jax.ShapeDtypeStruct((1, LANES), f32),
            jax.ShapeDtypeStruct((1, LANES), f32),
            jax.ShapeDtypeStruct((1, 1), i32),
        ),
        in_specs=[vmem] * 2,
        out_specs=(vmem,) * 5,
        scratch_shapes=[
            pltpu.VMEM((256, 512), bf16),
            pltpu.VMEM((768, 256), bf16),
            pltpu.VMEM((2048, 256), bf16),
            pltpu.VMEM((2048, 768), bf16),
            pltpu.VMEM((2048, LANES), f32),
            pltpu.VMEM((2048, LANES), f32),
            pltpu.VMEM((8192, LANES), f32),
        ],
        compiler_params=pltpu.CompilerParams(vmem_limit_bytes=40 * 1024 * 1024),
        name="pick",
    )(exps, everything)


def chain_kernel(slot_ref, panel_ref, spare_ref, out_ref, wide, ping, pong, logs, tops):
    length = slot_ref.shape[1]

    def widen(i, _):
        some = pl.ds(pl.multiple_of(i * 32, 32), 32)
        for n in range(SLOTS):
            if n < SENT:
                got = panel_ref[some, :, n * LANES : (n + 1) * LANES].astype(f32)
            else:
                got = spare_ref[some, :, :].astype(f32)
            rows = pl.ds(pl.multiple_of(n * 4096 + i * 256, 256), 256)
            wide[rows, :] = jnp.concatenate([got, got], axis=1).reshape(256, LANES)
        return 0

    lax.fori_loop(0, panel_ref.shape[0] // 32, widen, 0)
    low = iota((8, LANES), 1) < KW

    def build(i, _):
        for u in range(8):
            t = i * 8 + u
            start = slot_ref[0, t]
            parts = [wide[pl.ds(start + pair, 8, stride=8), :] for pair in range(4)]
            top = jnp.maximum(jnp.maximum(parts[0], parts[1]), jnp.maximum(parts[2], parts[3]))
            logs[pl.ds(t, 1), :] = jnp.max(top, axis=0, keepdims=True)
            move = []
            for part in parts:
                move += [jnp.where(low, part, 0.0), jnp.where(low, pltpu.roll(part, KW, 1), 0.0)]
            ping[t] = jnp.concatenate(move, axis=0).astype(bf16)
        return 0

    lax.fori_loop(0, length // 8, build, 0, unroll=2)
    peak = jnp.max(logs[0:length, :], axis=1, keepdims=True)
    tops[...] = jnp.broadcast_to((1.0 / peak).astype(bf16).astype(f32), (length, LANES))
    logs[0:length, :] = 1.0 / tops[...]
    logs[length:, :] = jnp.ones((length, LANES), f32)
    src, dst, count, base = ping, pong, length // 2, length
    while count > 1:
        unroll = min(count, 32)

        def level(i, _, src=src, dst=dst, unroll=unroll, base=base, first=src is ping and base == length):
            for u in range(unroll):
                n = i * unroll + u
                left, right = src[2 * n + 1][:, :KW], src[2 * n]
                if first:
                    left = left * tops[pl.ds(2 * n + 1, 1), :KW].astype(bf16)
                    right = right * tops[pl.ds(2 * n, 1), :].astype(bf16)
                prod = jnp.dot(left, right, preferred_element_type=f32)
                top = jnp.max(jnp.max(prod, axis=0, keepdims=True), axis=1, keepdims=True)
                logs[pl.ds(base + n, 1), :] = jnp.broadcast_to(top, (1, LANES))
                dst[n] = (prod * (1.0 / top)).astype(bf16)
            return 0

        lax.fori_loop(0, count // unroll, level, 0)
        src, dst, count, base = dst, src, count // 2, base + count
    prod = jnp.dot(src[1][:, :KW], src[0], preferred_element_type=f32)
    final = jnp.sum(jnp.sum(prod, axis=0, keepdims=True), axis=1, keepdims=True)
    scale = jnp.sum(jnp.log(logs[...]), axis=0, keepdims=True)
    total = jnp.log(final) + scale - jnp.log(jnp.full((1, LANES), 8192.0, f32))
    out_ref[...] = total[:, :1] / length


def chain(slots, panels, spare):
    length = slots.shape[1]
    vmem = pl.BlockSpec(memory_space=pltpu.VMEM)
    return pl.pallas_call(
        chain_kernel,
        out_shape=jax.ShapeDtypeStruct((1, 1), f32),
        in_specs=[pl.BlockSpec(memory_space=pltpu.SMEM), vmem, vmem],
        out_specs=vmem,
        scratch_shapes=[
            pltpu.VMEM((SLOTS * 4096, LANES), f32),
            pltpu.VMEM((length, KW, LANES), bf16),
            pltpu.VMEM((length // 2, KW, LANES), bf16),
            pltpu.VMEM((2 * length, LANES), f32),
            pltpu.VMEM((length, LANES), f32),
        ],
        compiler_params=pltpu.CompilerParams(vmem_limit_bytes=40 * 1024 * 1024),
        name="chain",
    )(slots, panels, spare)


def local(
    emit_states, trans_out, trans_in, word_emb, word_cluster, cluster_block, kept_parts, tokens
):
    msg, mat, slots = prep(
        kept_parts, tokens, word_cluster, cluster_block, emit_states, trans_out, trans_in, word_emb
    )
    arrived = lax.all_to_all(msg, "state", split_axis=0, concat_axis=0, tiled=True)
    exps, mine = score(arrived, mat)
    along_x = lax.all_to_all(
        mine, "seq", split_axis=0, concat_axis=0, tiled=True,
        axis_index_groups=[[0, 2, 4, 6], [1, 3, 5, 7]],
    )
    everything = lax.all_gather(
        along_x, "seq", axis=0, tiled=True, axis_index_groups=[[0, 1], [2, 3], [4, 5], [6, 7]]
    )
    panels, spare, trans_norm, emit_norm, full = pick(exps, everything)

    def exchange(value):
        return lax.all_to_all(value, ("state", "seq"), split_axis=0, concat_axis=0, tiled=True)

    got = exchange(panels)
    spare = lax.cond(full.reshape(()) > 0, exchange, lambda value: value, spare)
    token_loglik = chain(slots, got, spare)
    return (token_loglik.reshape(1), trans_norm.reshape(-1), emit_norm.reshape(-1))


def solution(mesh):
    placed = (
        P("state", None),
        P("state", None),
        P("state", None),
        P("state", None),
        P(),
        P(),
        P(),
        P(("state", "seq"), None),
    )
    return jax.shard_map(
        local,
        mesh=mesh,
        in_specs=placed,
        out_specs=(P(("state", "seq")), P("state"), P("state")),
        check_vma=False,
    )
```

```python
import jax
import jax.numpy as jnp
from jax import lax
from jax.experimental import pallas as pl
from jax.experimental.pallas import tpu as pltpu
from jax.sharding import PartitionSpec as P

BS = 256
PART = 32
KW = 64
LANES = 128
RANKS = 3
SHARDS = 64
SLOTS = 4
SENT = 3
ROWS = 16
SWAP = 528
XROWS = 208
f32 = jnp.float32
bf16 = jnp.bfloat16
i32 = jnp.int32


def iota(shape, axis):
    return lax.broadcasted_iota(i32, shape, axis)


def one_hot(mask):
    return jnp.where(mask, 1.0, 0.0).astype(bf16)


def ints(mask, value):
    return jnp.where(mask, value, 0)


def prep_kernel(
    parts_ref, token_ref, tokens_hbm, cluster_hbm, table_hbm, emit_hbm, out_hbm, in_hbm, word_hbm,
    msg_ref, out_kept, emit_kept, slot_ref,
    in_kept, slot_of, near, wide, counts_of, tokens_ref, cluster_ref, table_ref, word_ref, chosen, sems,
):
    me = lax.axis_index("state")
    share = lax.axis_index("seq")
    head = []
    for n, (src, dst) in enumerate(
        ((cluster_hbm, cluster_ref), (table_hbm, table_ref), (tokens_hbm, tokens_ref))
    ):
        head.append(pltpu.make_async_copy(src, dst, sems.at[n]))
        head[-1].start()
    word_copy = pltpu.make_async_copy(word_hbm, word_ref, sems.at[3])
    word_copy.start()
    kept = []
    for blk in range(2):
        for part in range(2):
            start = blk * BS + parts_ref[part, me * 2 + blk] * PART
            src = pl.ds(pl.multiple_of(start, PART), PART)
            at = (blk * 2 + part) * PART
            for which, (hbm, ref, to) in enumerate(
                ((in_hbm, in_kept, at), (out_hbm, out_kept, at), (emit_hbm, emit_kept, at))
            ):
                sem = sems.at[4 + (blk * 2 + part) * 3 + which]
                kept.append(pltpu.make_async_copy(hbm.at[src, :], ref.at[pl.ds(to, PART), :], sem))
                kept[-1].start()
    for copy in head:
        copy.wait()
    sub = iota((LANES, LANES), 0)
    lane = iota((LANES, LANES), 1)
    eye = sub == lane

    def column(row):
        return jnp.sum(ints(eye, row), axis=1, keepdims=True)

    def line(col):
        return jnp.sum(ints(eye, col), axis=0, keepdims=True)

    sums = jnp.concatenate([one_hot(sub < lane), jnp.ones((LANES, LANES), bf16)], axis=1)
    block_row = table_ref[...]
    block_col = column(block_row)
    block_col_f = block_col.astype(f32)
    carry = jnp.zeros((LANES, LANES), f32)
    chunks = 2048 // LANES
    own = pl.multiple_of(me * chunks, chunks)
    own_rows = cluster_ref[pl.ds(own, chunks), :]
    for c in range(chunks):
        hit = sub == own_rows[c : c + 1, :]
        found = jnp.dot(one_hot(hit), sums, preferred_element_type=f32)
        before = found[:, :LANES] + carry
        carry = carry + found[:, LANES:]
        rank = jnp.sum(jnp.where(hit, before, 0.0), axis=0, keepdims=True).astype(i32)
        block = jnp.sum(jnp.where(hit, block_col_f, 0.0), axis=0, keepdims=True).astype(i32)
        x = rank - RANKS * share
        slot = (block >> 1) * 8 + x * 2 + (block & 1)
        slot_of[c : c + 1, :] = jnp.where((x >= 0) & (x < RANKS), slot, -1)
    counts_of[...] = carry

    length = token_ref.shape[1]

    for t in range(length):
        near[t : t + 1, :] = cluster_ref[pl.ds(token_ref[0, t] >> 7, 1), :]
    token_col = column(tokens_ref[...])
    cluster_col = jnp.sum(ints(lane == (token_col & 127), near[...]), axis=1, keepdims=True)
    near[...] = jnp.broadcast_to(cluster_col, (LANES, LANES))
    place = iota((chunks, LANES), 0) * LANES + iota((chunks, LANES), 1)

    for t in range(length):
        token = token_ref[0, t]
        shard_rows = cluster_ref[pl.ds(pl.multiple_of((token >> 11) * chunks, chunks), chunks), :]
        earlier = (shard_rows == near[t : t + 1, :]) & (place < (token & 2047))
        wide[t : t + 1, :] = jnp.sum(ints(earlier, 1), axis=0, keepdims=True)
    rank_col = jnp.sum(wide[...], axis=1, keepdims=True)
    own_block_col = jnp.sum(ints(lane == cluster_col, block_row), axis=1, keepdims=True)
    own_block_row = line(own_block_col)
    same = (own_block_col >> 1) == (own_block_row >> 1)
    times_col = jnp.sum(ints(same & (lane < sub), 1), axis=1, keepdims=True)
    times_row = jnp.sum(ints(same & (sub < lane), 1), axis=0, keepdims=True)
    slot_ref[...] = times_row * 4096 + (own_block_row >> 1) * 64
    following = jnp.sum(ints(lane == sub + 1, own_block_row), axis=1, keepdims=True)
    following = jnp.where(iota((LANES, 1), 0) == length - 1, LANES, following)
    slots_col = (own_block_col >> 1) * SLOTS + times_col
    asked = jnp.zeros((SHARDS, LANES), f32)
    slot_line = iota((LANES, 2 * LANES), 1)
    at_slot = slot_line == slots_col
    owner = (iota((SHARDS, 2 * LANES), 1) >> 2) == iota((SHARDS, 2 * LANES), 0)
    slot_sub = iota((2 * LANES, LANES), 0) & 3
    slot_lane = iota((2 * LANES, LANES), 1)
    for field, values in enumerate((following, token_col >> 11, rank_col + 32 * (own_block_col & 1))):
        value_row = jnp.sum(ints(at_slot, values), axis=0, keepdims=True)
        spread = jnp.where(owner, value_row.astype(f32), 0.0).astype(bf16)
        asked += jnp.dot(
            spread, one_hot(slot_lane == field * 4 + slot_sub), preferred_element_type=f32
        )
    count_lane = jnp.where(lane == 12 + (block_col & 1), counts_of[...], 0.0).astype(bf16)
    count_owner = one_hot((block_row >> 1) == iota((SHARDS, LANES), 0))
    asked += jnp.dot(count_owner, count_lane, preferred_element_type=f32)
    full = jnp.max(times_row, axis=1, keepdims=True) >= SENT
    asked += jnp.where(full & (iota((SHARDS, LANES), 1) == 14), 1.0, 0.0)

    for copy in kept:
        copy.wait()
    row = iota((16, LANES), 0)
    want = ((row >> 2) & 1) * KW + ((row >> 3) * 4 + (row & 3)) * 8 + share
    targets = jnp.dot(
        one_hot(iota((16, LANES), 1) == want), in_kept[...], preferred_element_type=f32
    )
    for tile in range(4):
        for c in range(chunks):
            chosen[tile * LANES : (tile + 1) * LANES, c * LANES : (c + 1) * LANES] = one_hot(
                sub + tile * LANES == slot_of[c : c + 1, :]
            )
    word_copy.wait()
    request_row = iota((8, LANES), 0) == 6
    words = jnp.dot(chosen[...], word_ref[...], preferred_element_type=f32)
    for to in range(SHARDS):
        mine = words[to * 8 : to * 8 + 8, :]
        first = jnp.where(request_row, asked[to : to + 1, :], mine[:, :LANES])
        mine = jnp.concatenate([first, mine[:, LANES:]], axis=1)
        head = targets[(to & 1) * 8 : (to & 1) * 8 + 8, :]
        msg_ref[to] = jnp.concatenate([head, mine], axis=0).astype(bf16)


def prep(kept_parts, tokens, word_cluster, cluster_block, emit_states, trans_out, trans_in, word_emb):
    width = emit_states.shape[1]
    vmem = pl.BlockSpec(memory_space=pltpu.VMEM)
    smem = pl.BlockSpec(memory_space=pltpu.SMEM)
    clusters = word_cluster.reshape(-1, LANES)
    return pl.pallas_call(
        prep_kernel,
        out_shape=(
            jax.ShapeDtypeStruct((SHARDS, ROWS, width), bf16),
            jax.ShapeDtypeStruct((2 * KW, width), bf16),
            jax.ShapeDtypeStruct((2 * KW, width), bf16),
            jax.ShapeDtypeStruct((1, LANES), i32),
        ),
        in_specs=[smem, smem] + [pl.BlockSpec(memory_space=pltpu.HBM)] * 7,
        out_specs=(vmem,) * 4,
        scratch_shapes=[
            pltpu.VMEM((2 * KW, width), bf16),
            pltpu.VMEM((16, LANES), i32),
            pltpu.VMEM((LANES, LANES), i32),
            pltpu.VMEM((LANES, LANES), i32),
            pltpu.VMEM((LANES, LANES), f32),
            pltpu.VMEM((1, LANES), i32),
            pltpu.VMEM(clusters.shape, i32),
            pltpu.VMEM((1, LANES), i32),
            pltpu.VMEM(word_emb.shape, bf16),
            pltpu.VMEM((8 * SHARDS, word_emb.shape[0]), bf16),
            pltpu.SemaphoreType.DMA((16,)),
        ],
        compiler_params=pltpu.CompilerParams(vmem_limit_bytes=60 * 1024 * 1024),
        name="prep",
    )(
        kept_parts.T, tokens, tokens, clusters, cluster_block[None, :],
        emit_states, trans_out, trans_in, word_emb,
    )


def thirds(value):
    high = value.astype(bf16).astype(f32)
    mid = (value - high).astype(bf16).astype(f32)
    return [high, mid, value - high - mid]


def score_kernel(msg_ref, own_ref, other_ref, exps_ref, z_ref, swap_ref):
    states = jnp.concatenate([own_ref[...], other_ref[...]], axis=0)
    total = jnp.zeros((1, 2 * LANES), f32)
    for tile in range(4):
        got = msg_ref[tile * 16 : tile * 16 + 16].reshape(16 * ROWS, msg_ref.shape[2])
        res = lax.dot_general(
            got, states, (((1,), (1,)), ((), ())), preferred_element_type=f32
        ).reshape(16, ROWS, 2 * LANES)
        exps = jnp.exp(res[:, :8, :]).reshape(LANES, 2 * LANES)
        total = total + jnp.sum(exps, axis=0, keepdims=True)
        rows = slice(tile * LANES, (tile + 1) * LANES)
        exps_ref[rows, :] = exps[:, :LANES]
        swap_ref[rows, :] = jnp.minimum(exps[:, LANES:], 3.38e38).astype(bf16)
    z_ref[...] = jnp.broadcast_to(total[:, :LANES], (8, LANES))
    sums = thirds(total[:, LANES:]) + [jnp.zeros((13, LANES), f32)]
    swap_ref[512:SWAP, :] = jnp.concatenate(sums, axis=0).astype(bf16)


def words_kernel(msg_ref, emit_ref, z_ref, swap_ref, out_ref, words, raw):
    share = lax.axis_index("seq")
    sums = swap_ref[512:SWAP, :].astype(f32)
    total = z_ref[0:1, :] + (sums[0:1, :] + sums[1:2, :] + sums[2:3, :])
    for tile in range(4):
        got = msg_ref[tile * 16 : tile * 16 + 16].reshape(16 * ROWS, msg_ref.shape[2])
        res = lax.dot_general(
            got, emit_ref[...], (((1,), (1,)), ((), ())), preferred_element_type=f32
        ).reshape(16, ROWS, LANES)
        rows = slice(tile * LANES, (tile + 1) * LANES)
        words[rows, :] = res[:, 8:, :].reshape(LANES, LANES)
        some = got[:, :LANES].astype(f32).reshape(16, ROWS, LANES)
        raw[rows, :] = some[:, 8:, :].reshape(LANES, LANES)
    asked = raw[pl.ds(6, SHARDS, stride=8), :]
    spread = one_hot(iota((LANES, LANES), 0) == 12 + (iota((LANES, LANES), 1) >> 6))
    counts = jnp.dot(asked.astype(bf16), spread, preferred_element_type=f32)
    low = iota((SHARDS, LANES), 1) < KW
    scores, valid = [], []
    for x in range(RANKS):
        some = jnp.where(
            low,
            words[pl.ds(2 * x, SHARDS, stride=8), :],
            words[pl.ds(2 * x + 1, SHARDS, stride=8), :],
        )
        valid.append((RANKS * share + x).astype(f32) < counts)
        scores.append(jnp.where(valid[-1], some, -1e30))
    top = jnp.max(jnp.maximum(jnp.maximum(scores[0], scores[1]), scores[2]), axis=0, keepdims=True)
    top = top.astype(bf16).astype(f32)
    parts = [jnp.where(v, jnp.exp(s - top), 0.0) for s, v in zip(scores, valid)]
    mass = jnp.sum(parts[0] + parts[1] + parts[2], axis=0, keepdims=True)
    lane16 = iota((8, LANES), 1) >> 4
    packed = jnp.zeros((8, LANES), f32)
    for m in range(8):
        some = raw[pl.ds(m * 8 + 6, 8, stride=64), :]
        some = pltpu.roll(some, m * 16, 1) if m else some
        packed = jnp.where(lane16 == m, some, packed)
    sums = jnp.concatenate([top] + thirds(mass) + thirds(total) + [jnp.zeros_like(top)], axis=0)
    message = jnp.concatenate(parts + [packed, sums], axis=0).astype(bf16)
    for copy in range(4):
        out_ref[copy] = message


def call(kernel, name, outs, scratch, *args):
    vmem = pl.BlockSpec(memory_space=pltpu.VMEM)
    return pl.pallas_call(
        kernel,
        out_shape=tuple(jax.ShapeDtypeStruct(shape, kind) for shape, kind in outs),
        in_specs=[vmem] * len(args),
        out_specs=(vmem,) * len(outs),
        scratch_shapes=[pltpu.VMEM(shape, kind) for shape, kind in scratch],
        compiler_params=pltpu.CompilerParams(vmem_limit_bytes=40 * 1024 * 1024),
        name=name,
    )(*args)


def score(msg, own, other):
    outs = [((512, LANES), f32), ((8, LANES), f32), ((SWAP, LANES), bf16)]
    return call(score_kernel, "score", outs, [], msg, own, other)


def words(msg, emit_kept, z_part, swapped):
    outs = [((4, XROWS, LANES), bf16)]
    scratch = [((512, LANES), f32)] * 2
    return call(words_kernel, "words", outs, scratch, msg, emit_kept, z_part, swapped)[0]


def pick_kernel(
    exps_ref, swap_ref, all_ref, panel_ref, spare_ref, trans_ref, emit_ref, full_ref,
    halves, table, emits, next_rows, word_rows, blocks, keys, stage,
):
    share = lax.axis_index("seq")
    order = [(g & 1) * 4 + (g >> 1) for g in range(8)]
    sums = [all_ref[n, 200:208, :].astype(f32) for n in order]
    total = jnp.zeros((1, LANES), f32)
    top = sums[0][0:1, :]
    full = jnp.zeros((8, LANES), f32)
    for g in range(8):
        total = total + (sums[g][4:5, :] + sums[g][5:6, :] + sums[g][6:7, :])
        top = jnp.maximum(top, sums[g][0:1, :])
        full = jnp.maximum(full, all_ref[order[g], 192:200, :].astype(f32))
    mass = jnp.zeros((1, LANES), f32)
    for g in range(8):
        part = sums[g][1:2, :] + sums[g][2:3, :] + sums[g][3:4, :]
        mass = mass + part * jnp.exp(sums[g][0:1, :] - top)
    full = jnp.where((iota((8, LANES), 1) & 15) == 14, full, 0.0)
    full = jnp.max(jnp.max(full, axis=0, keepdims=True), axis=1, keepdims=True)
    full_ref[...] = full.astype(i32)
    trans_ref[...] = jnp.log(total)
    emit_norm = top + jnp.log(mass)
    emit_ref[...] = emit_norm
    for g in range(8):
        rows = slice((g & 3) * 192, (g & 3) * 192 + 192)
        lanes = slice((g >> 2) * LANES, (g >> 2) * LANES + LANES)
        scale = jnp.exp(sums[g][0:1, :] - emit_norm)
        emits[rows, lanes] = (all_ref[order[g], 0:192, :].astype(f32) * scale).astype(bf16)
    odd = lax.axis_index("state") & 1
    halves[pl.ds(pl.multiple_of(odd * 512, 512), 512), :] = exps_ref[...]
    halves[pl.ds(pl.multiple_of((1 - odd) * 512, 512), 512), :] = swap_ref[0:512, :].astype(f32)
    low = iota((LANES, LANES), 1) < KW
    for pair in range(4):
        start = (pair >> 1) * 512 + (pair & 1) * 2
        first = halves[pl.ds(start, LANES, stride=4), :] / total
        second = halves[pl.ds(start + 1, LANES, stride=4), :] / total
        lanes = slice(pair * LANES, (pair + 1) * LANES)
        table[0:LANES, lanes] = jnp.where(low, first, pltpu.roll(second, KW, 1)).astype(bf16)
        table[LANES:, lanes] = jnp.where(low, pltpu.roll(first, KW, 1), second).astype(bf16)
    row, lane = iota((512, LANES), 0), iota((512, LANES), 1)
    pick_row, pick_lane = iota((512, 64), 0), iota((512, 64), 1)
    mine = ((lane >> 4) == ((row >> 3) & 7)) & ((lane & 3) == (row >> 7))
    next_at = mine & ((lane & 15) < 4)
    key_at = mine & ((lane & 15) >= 4) & ((lane & 15) < 12)
    ones = jnp.ones((LANES, LANES), bf16)
    weights = jnp.where((iota((LANES, LANES), 0) & 15) >= 8, 64.0, 1.0).astype(bf16)
    asked = jnp.concatenate([all_ref[n, 192:200, :].astype(f32) for n in order], axis=0)
    asked = asked.astype(bf16)
    lane_f = lane.astype(f32)
    row_of = lane & (KW - 1)
    for step in range(4):
        source = (pick_row & 7) * 8 + step * 2 + ((pick_row >> 6) & 1)
        spread = jnp.dot(one_hot(pick_lane == source), asked, preferred_element_type=f32)
        block = jnp.dot(
            jnp.where(next_at, spread, 0.0).astype(bf16), ones, preferred_element_type=f32
        )
        key = jnp.dot(
            jnp.where(key_at, spread, 0.0).astype(bf16), weights, preferred_element_type=f32
        )
        blocks[step * 512 : (step + 1) * 512, :] = block
        keys[step * 512 : (step + 1) * 512, :] = key
    for step in range(4):
        rows = slice(step * 512, (step + 1) * 512)
        block, key = blocks[rows, :], keys[rows, :]
        second = key >= 2048.0
        key = jnp.where(second, key - 2048.0, key)
        key = jnp.where(key >= 768.0, key - 768.0, key)
        hit = block == lane_f
        next_rows[rows, :LANES] = one_hot(hit & ~second)
        next_rows[rows, LANES:] = one_hot(hit & second)
        for n in range(6):
            word_rows[rows, n * LANES : (n + 1) * LANES] = one_hot(key == lane_f + float(n * LANES))
    for step in range(4):
        rows = slice(step * 512, (step + 1) * 512)
        got = jnp.dot(word_rows[rows, :], emits[...], preferred_element_type=f32)
        panels = jnp.dot(next_rows[rows, :], table[...], preferred_element_type=f32)
        block, key = blocks[rows, :], keys[rows, :]
        second = key >= 2048.0
        late = jnp.where(second, key - 2048.0, key) >= 768.0
        emit = jnp.where(late, got[:, LANES:], got[:, :LANES])
        emit = jnp.where((lane_f < float(KW)) ^ second, emit, pltpu.roll(emit, KW, 1))
        last = block == float(LANES)
        for pair in range(4):
            column = (pair * 2 + (lane >> 6)) * 8 + share
            panel = panels[:, pair * LANES : (pair + 1) * LANES]
            panel = jnp.where(last & (row_of == column), 1.0, panel) * emit
            for n in range(SLOTS):
                stage[pl.ds(step * 2048 + n * 512 + pair, LANES, stride=4), :] = panel[
                    n * LANES : (n + 1) * LANES, :
                ]
        for n in range(SLOTS):
            block = stage[step * 2048 + n * 512 : step * 2048 + (n + 1) * 512, :]
            block = block.reshape(LANES, 4, LANES).astype(bf16)
            if n < SENT:
                panel_ref[step * LANES : (step + 1) * LANES, :, n * LANES : (n + 1) * LANES] = block
            else:
                spare_ref[step * LANES : (step + 1) * LANES, :, :] = block


def pick(exps, swapped, everything):
    vmem = pl.BlockSpec(memory_space=pltpu.VMEM)
    return pl.pallas_call(
        pick_kernel,
        out_shape=(
            jax.ShapeDtypeStruct((512, 4, SENT * LANES), bf16),
            jax.ShapeDtypeStruct((512, 4, LANES), bf16),
            jax.ShapeDtypeStruct((1, LANES), f32),
            jax.ShapeDtypeStruct((1, LANES), f32),
            jax.ShapeDtypeStruct((1, 1), i32),
        ),
        in_specs=[vmem] * 3,
        out_specs=(vmem,) * 5,
        scratch_shapes=[
            pltpu.VMEM((1024, LANES), f32),
            pltpu.VMEM((256, 512), bf16),
            pltpu.VMEM((768, 256), bf16),
            pltpu.VMEM((2048, 256), bf16),
            pltpu.VMEM((2048, 768), bf16),
            pltpu.VMEM((2048, LANES), f32),
            pltpu.VMEM((2048, LANES), f32),
            pltpu.VMEM((8192, LANES), f32),
        ],
        compiler_params=pltpu.CompilerParams(vmem_limit_bytes=40 * 1024 * 1024),
        name="pick",
    )(exps, swapped, everything)


def chain_kernel(slot_ref, panel_ref, spare_ref, out_ref, wide, ping, pong, logs, tops):
    length = slot_ref.shape[1]

    def widen(i, _):
        some = pl.ds(pl.multiple_of(i * 32, 32), 32)
        for n in range(SLOTS):
            if n < SENT:
                got = panel_ref[some, :, n * LANES : (n + 1) * LANES].astype(f32)
            else:
                got = spare_ref[some, :, :].astype(f32)
            rows = pl.ds(pl.multiple_of(n * 4096 + i * 256, 256), 256)
            wide[rows, :] = jnp.concatenate([got, got], axis=1).reshape(256, LANES)
        return 0

    lax.fori_loop(0, panel_ref.shape[0] // 32, widen, 0)
    low = iota((8, LANES), 1) < KW

    def build(i, _):
        for u in range(8):
            t = i * 8 + u
            start = slot_ref[0, t]
            parts = [wide[pl.ds(start + pair, 8, stride=8), :] for pair in range(4)]
            top = jnp.maximum(jnp.maximum(parts[0], parts[1]), jnp.maximum(parts[2], parts[3]))
            logs[pl.ds(t, 1), :] = jnp.max(top, axis=0, keepdims=True)
            move = []
            for part in parts:
                move += [jnp.where(low, part, 0.0), jnp.where(low, pltpu.roll(part, KW, 1), 0.0)]
            ping[t] = jnp.concatenate(move, axis=0).astype(bf16)
        return 0

    lax.fori_loop(0, length // 8, build, 0, unroll=2)
    peak = jnp.max(logs[0:length, :], axis=1, keepdims=True)
    tops[...] = jnp.broadcast_to((1.0 / peak).astype(bf16).astype(f32), (length, LANES))
    logs[0:length, :] = 1.0 / tops[...]
    logs[length:, :] = jnp.ones((length, LANES), f32)
    src, dst, count, base = ping, pong, length // 2, length
    while count > 1:
        unroll = min(count, 32)

        def level(i, _, src=src, dst=dst, unroll=unroll, base=base, first=src is ping and base == length):
            for u in range(unroll):
                n = i * unroll + u
                left, right = src[2 * n + 1][:, :KW], src[2 * n]
                if first:
                    left = left * tops[pl.ds(2 * n + 1, 1), :KW].astype(bf16)
                    right = right * tops[pl.ds(2 * n, 1), :].astype(bf16)
                prod = jnp.dot(left, right, preferred_element_type=f32)
                top = jnp.max(jnp.max(prod, axis=0, keepdims=True), axis=1, keepdims=True)
                logs[pl.ds(base + n, 1), :] = jnp.broadcast_to(top, (1, LANES))
                dst[n] = (prod * (1.0 / top)).astype(bf16)
            return 0

        lax.fori_loop(0, count // unroll, level, 0)
        src, dst, count, base = dst, src, count // 2, base + count
    prod = jnp.dot(src[1][:, :KW], src[0], preferred_element_type=f32)
    final = jnp.sum(jnp.sum(prod, axis=0, keepdims=True), axis=1, keepdims=True)
    scale = jnp.sum(jnp.log(logs[...]), axis=0, keepdims=True)
    total = jnp.log(final) + scale - jnp.log(jnp.full((1, LANES), 8192.0, f32))
    out_ref[...] = total[:, :1] / length


def chain(slots, panels, spare):
    length = slots.shape[1]
    vmem = pl.BlockSpec(memory_space=pltpu.VMEM)
    return pl.pallas_call(
        chain_kernel,
        out_shape=jax.ShapeDtypeStruct((1, 1), f32),
        in_specs=[pl.BlockSpec(memory_space=pltpu.SMEM), vmem, vmem],
        out_specs=vmem,
        scratch_shapes=[
            pltpu.VMEM((SLOTS * 4096, LANES), f32),
            pltpu.VMEM((length, KW, LANES), bf16),
            pltpu.VMEM((length // 2, KW, LANES), bf16),
            pltpu.VMEM((2 * length, LANES), f32),
            pltpu.VMEM((length, LANES), f32),
        ],
        compiler_params=pltpu.CompilerParams(vmem_limit_bytes=40 * 1024 * 1024),
        name="chain",
    )(slots, panels, spare)


def local(
    emit_states, trans_out, trans_in, word_emb, word_cluster, cluster_block, kept_parts, tokens
):
    msg, out_kept, emit_kept, slots = prep(
        kept_parts, tokens, word_cluster, cluster_block, emit_states, trans_out, trans_in, word_emb
    )
    pairs = [(i, i ^ 1) for i in range(SHARDS)]
    other = lax.ppermute(out_kept, "state", pairs)
    arrived = lax.all_to_all(msg, "state", split_axis=0, concat_axis=0, tiled=True)
    exps, z_part, swap = score(arrived, out_kept, other)
    swapped = lax.ppermute(swap, "state", pairs)
    mine = words(arrived, emit_kept, z_part, swapped)
    along_x = lax.all_to_all(
        mine, "seq", split_axis=0, concat_axis=0, tiled=True,
        axis_index_groups=[[0, 2, 4, 6], [1, 3, 5, 7]],
    )
    everything = lax.all_gather(
        along_x, "seq", axis=0, tiled=True, axis_index_groups=[[0, 1], [2, 3], [4, 5], [6, 7]]
    )
    panels, spare, trans_norm, emit_norm, full = pick(exps, swapped, everything)

    def exchange(value):
        return lax.all_to_all(value, ("state", "seq"), split_axis=0, concat_axis=0, tiled=True)

    got = exchange(panels)
    spare = lax.cond(full.reshape(()) > 0, exchange, lambda value: value, spare)
    token_loglik = chain(slots, got, spare)
    return (token_loglik.reshape(1), trans_norm.reshape(-1), emit_norm.reshape(-1))


def solution(mesh):
    placed = (
        P("state", None),
        P("state", None),
        P("state", None),
        P("state", None),
        P(),
        P(),
        P(),
        P(("state", "seq"), None),
    )
    return jax.shard_map(
        local,
        mesh=mesh,
        in_specs=placed,
        out_specs=(P(("state", "seq")), P("state"), P("state")),
        check_vma=False,
    )
```

```python
import jax
import jax.numpy as jnp
from jax import lax
from jax.experimental import pallas as pl
from jax.experimental.pallas import tpu as pltpu
from jax.sharding import PartitionSpec as P

BS = 256
PART = 32
KW = 64
LANES = 128
RANKS = 3
SHARDS = 64
SLOTS = 4
SENT = 3
ROWS = 16
XROWS = 208
f32 = jnp.float32
bf16 = jnp.bfloat16
i32 = jnp.int32


def iota(shape, axis):
    return lax.broadcasted_iota(i32, shape, axis)


def one_hot(mask):
    return jnp.where(mask, 1.0, 0.0).astype(bf16)


def ints(mask, value):
    return jnp.where(mask, value, 0)


def prep_kernel(
    parts_ref, token_ref, tokens_hbm, cluster_hbm, table_hbm, emit_hbm, out_hbm, in_hbm, word_hbm,
    msg_ref, out_kept, emit_kept, slot_ref,
    in_kept, slot_of, near, wide, counts_of, tokens_ref, cluster_ref, table_ref, word_ref, chosen, sems,
):
    me = lax.axis_index("state")
    share = lax.axis_index("seq")
    head = []
    for n, (src, dst) in enumerate(
        ((cluster_hbm, cluster_ref), (table_hbm, table_ref), (tokens_hbm, tokens_ref))
    ):
        head.append(pltpu.make_async_copy(src, dst, sems.at[n]))
        head[-1].start()
    word_copy = pltpu.make_async_copy(word_hbm, word_ref, sems.at[3])
    word_copy.start()
    kept = []
    for blk in range(2):
        for part in range(2):
            start = blk * BS + parts_ref[part, me * 2 + blk] * PART
            src = pl.ds(pl.multiple_of(start, PART), PART)
            at = (blk * 2 + part) * PART
            for which, (hbm, ref, to) in enumerate(
                ((in_hbm, in_kept, at), (out_hbm, out_kept, at), (emit_hbm, emit_kept, at))
            ):
                sem = sems.at[4 + (blk * 2 + part) * 3 + which]
                kept.append(pltpu.make_async_copy(hbm.at[src, :], ref.at[pl.ds(to, PART), :], sem))
                kept[-1].start()
    for copy in head:
        copy.wait()
    sub = iota((LANES, LANES), 0)
    lane = iota((LANES, LANES), 1)
    eye = sub == lane

    def column(row):
        return jnp.sum(ints(eye, row), axis=1, keepdims=True)

    def line(col):
        return jnp.sum(ints(eye, col), axis=0, keepdims=True)

    sums = jnp.concatenate([one_hot(sub < lane), jnp.ones((LANES, LANES), bf16)], axis=1)
    block_row = table_ref[...]
    block_col = column(block_row)
    block_col_f = block_col.astype(f32)
    carry = jnp.zeros((LANES, LANES), f32)
    chunks = 2048 // LANES
    own = pl.multiple_of(me * chunks, chunks)
    own_rows = cluster_ref[pl.ds(own, chunks), :]
    for c in range(chunks):
        hit = sub == own_rows[c : c + 1, :]
        found = jnp.dot(one_hot(hit), sums, preferred_element_type=f32)
        before = found[:, :LANES] + carry
        carry = carry + found[:, LANES:]
        rank = jnp.sum(jnp.where(hit, before, 0.0), axis=0, keepdims=True).astype(i32)
        block = jnp.sum(jnp.where(hit, block_col_f, 0.0), axis=0, keepdims=True).astype(i32)
        x = rank - RANKS * share
        slot = (block >> 1) * 8 + x * 2 + (block & 1)
        slot_of[c : c + 1, :] = jnp.where((x >= 0) & (x < RANKS), slot, -1)
    counts_of[...] = carry

    length = token_ref.shape[1]

    for t in range(length):
        near[t : t + 1, :] = cluster_ref[pl.ds(token_ref[0, t] >> 7, 1), :]
    token_col = column(tokens_ref[...])
    cluster_col = jnp.sum(ints(lane == (token_col & 127), near[...]), axis=1, keepdims=True)
    near[...] = jnp.broadcast_to(cluster_col, (LANES, LANES))
    place = iota((chunks, LANES), 0) * LANES + iota((chunks, LANES), 1)

    for t in range(length):
        token = token_ref[0, t]
        shard_rows = cluster_ref[pl.ds(pl.multiple_of((token >> 11) * chunks, chunks), chunks), :]
        earlier = (shard_rows == near[t : t + 1, :]) & (place < (token & 2047))
        wide[t : t + 1, :] = jnp.sum(ints(earlier, 1), axis=0, keepdims=True)
    rank_col = jnp.sum(wide[...], axis=1, keepdims=True)
    own_block_col = jnp.sum(ints(lane == cluster_col, block_row), axis=1, keepdims=True)
    own_block_row = line(own_block_col)
    same = (own_block_col >> 1) == (own_block_row >> 1)
    times_col = jnp.sum(ints(same & (lane < sub), 1), axis=1, keepdims=True)
    times_row = jnp.sum(ints(same & (sub < lane), 1), axis=0, keepdims=True)
    slot_ref[...] = times_row * 4096 + (own_block_row >> 1) * 64
    following = jnp.sum(ints(lane == sub + 1, own_block_row), axis=1, keepdims=True)
    following = jnp.where(iota((LANES, 1), 0) == length - 1, LANES, following)
    slots_col = (own_block_col >> 1) * SLOTS + times_col
    asked = jnp.zeros((SHARDS, LANES), f32)
    slot_line = iota((LANES, 2 * LANES), 1)
    at_slot = slot_line == slots_col
    owner = (iota((SHARDS, 2 * LANES), 1) >> 2) == iota((SHARDS, 2 * LANES), 0)
    slot_sub = iota((2 * LANES, LANES), 0) & 3
    slot_lane = iota((2 * LANES, LANES), 1)
    for field, values in enumerate((following, token_col >> 11, rank_col + 32 * (own_block_col & 1))):
        value_row = jnp.sum(ints(at_slot, values), axis=0, keepdims=True)
        spread = jnp.where(owner, value_row.astype(f32), 0.0).astype(bf16)
        asked += jnp.dot(
            spread, one_hot(slot_lane == field * 4 + slot_sub), preferred_element_type=f32
        )
    count_lane = jnp.where(lane == 12 + (block_col & 1), counts_of[...], 0.0).astype(bf16)
    count_owner = one_hot((block_row >> 1) == iota((SHARDS, LANES), 0))
    asked += jnp.dot(count_owner, count_lane, preferred_element_type=f32)
    full = jnp.max(times_row, axis=1, keepdims=True) >= SENT
    asked += jnp.where(full & (iota((SHARDS, LANES), 1) == 14), 1.0, 0.0)

    for copy in kept:
        copy.wait()
    row = iota((16, LANES), 0)
    want = ((row >> 2) & 1) * KW + ((row >> 3) * 4 + (row & 3)) * 8 + share
    targets = jnp.dot(
        one_hot(iota((16, LANES), 1) == want), in_kept[...], preferred_element_type=f32
    )
    for tile in range(4):
        for c in range(chunks):
            chosen[tile * LANES : (tile + 1) * LANES, c * LANES : (c + 1) * LANES] = one_hot(
                sub + tile * LANES == slot_of[c : c + 1, :]
            )
    word_copy.wait()
    request_row = iota((8, LANES), 0) == 6
    words = jnp.dot(chosen[...], word_ref[...], preferred_element_type=f32)
    for to in range(SHARDS):
        mine = words[to * 8 : to * 8 + 8, :]
        first = jnp.where(request_row, asked[to : to + 1, :], mine[:, :LANES])
        mine = jnp.concatenate([first, mine[:, LANES:]], axis=1)
        head = targets[(to & 1) * 8 : (to & 1) * 8 + 8, :]
        msg_ref[to] = jnp.concatenate([head, mine], axis=0).astype(bf16)


def prep(kept_parts, tokens, word_cluster, cluster_block, emit_states, trans_out, trans_in, word_emb):
    width = emit_states.shape[1]
    vmem = pl.BlockSpec(memory_space=pltpu.VMEM)
    smem = pl.BlockSpec(memory_space=pltpu.SMEM)
    clusters = word_cluster.reshape(-1, LANES)
    return pl.pallas_call(
        prep_kernel,
        out_shape=(
            jax.ShapeDtypeStruct((SHARDS, ROWS, width), bf16),
            jax.ShapeDtypeStruct((2 * KW, width), bf16),
            jax.ShapeDtypeStruct((2 * KW, width), bf16),
            jax.ShapeDtypeStruct((1, LANES), i32),
        ),
        in_specs=[smem, smem] + [pl.BlockSpec(memory_space=pltpu.HBM)] * 7,
        out_specs=(vmem,) * 4,
        scratch_shapes=[
            pltpu.VMEM((2 * KW, width), bf16),
            pltpu.VMEM((16, LANES), i32),
            pltpu.VMEM((LANES, LANES), i32),
            pltpu.VMEM((LANES, LANES), i32),
            pltpu.VMEM((LANES, LANES), f32),
            pltpu.VMEM((1, LANES), i32),
            pltpu.VMEM(clusters.shape, i32),
            pltpu.VMEM((1, LANES), i32),
            pltpu.VMEM(word_emb.shape, bf16),
            pltpu.VMEM((8 * SHARDS, word_emb.shape[0]), bf16),
            pltpu.SemaphoreType.DMA((16,)),
        ],
        compiler_params=pltpu.CompilerParams(vmem_limit_bytes=60 * 1024 * 1024),
        name="prep",
    )(
        kept_parts.T, tokens, tokens, clusters, cluster_block[None, :],
        emit_states, trans_out, trans_in, word_emb,
    )


def thirds(value):
    high = value.astype(bf16).astype(f32)
    mid = (value - high).astype(bf16).astype(f32)
    return [high, mid, value - high - mid]


def score_kernel(msg_ref, own_ref, other_ref, exps_ref, z_ref, z_swap_ref, swap_ref):
    states = jnp.concatenate([own_ref[...], other_ref[...]], axis=0)
    total = jnp.zeros((1, 2 * LANES), f32)
    for tile in range(4):
        got = msg_ref[tile * 16 : tile * 16 + 16].reshape(16 * ROWS, msg_ref.shape[2])
        res = lax.dot_general(
            got, states, (((1,), (1,)), ((), ())), preferred_element_type=f32
        ).reshape(16, ROWS, 2 * LANES)
        exps = jnp.exp(res[:, :8, :]).reshape(LANES, 2 * LANES)
        total = total + jnp.sum(exps, axis=0, keepdims=True)
        rows = slice(tile * LANES, (tile + 1) * LANES)
        exps_ref[rows, :] = exps[:, :LANES]
        swap_ref[rows, :] = jnp.minimum(exps[:, LANES:], 3.38e38).astype(bf16)
    z_ref[...] = jnp.broadcast_to(total[:, :LANES], (8, LANES))
    z_swap_ref[...] = jnp.broadcast_to(total[:, LANES:], (8, LANES))


def words_kernel(msg_ref, emit_ref, z_ref, z_other_ref, out_ref, words, raw):
    share = lax.axis_index("seq")
    total = z_ref[0:1, :] + z_other_ref[0:1, :]
    for tile in range(4):
        got = msg_ref[tile * 16 : tile * 16 + 16].reshape(16 * ROWS, msg_ref.shape[2])
        res = lax.dot_general(
            got, emit_ref[...], (((1,), (1,)), ((), ())), preferred_element_type=f32
        ).reshape(16, ROWS, LANES)
        rows = slice(tile * LANES, (tile + 1) * LANES)
        words[rows, :] = res[:, 8:, :].reshape(LANES, LANES)
        some = got[:, :LANES].astype(f32).reshape(16, ROWS, LANES)
        raw[rows, :] = some[:, 8:, :].reshape(LANES, LANES)
    asked = raw[pl.ds(6, SHARDS, stride=8), :]
    spread = one_hot(iota((LANES, LANES), 0) == 12 + (iota((LANES, LANES), 1) >> 6))
    counts = jnp.dot(asked.astype(bf16), spread, preferred_element_type=f32)
    low = iota((SHARDS, LANES), 1) < KW
    scores, valid = [], []
    for x in range(RANKS):
        some = jnp.where(
            low,
            words[pl.ds(2 * x, SHARDS, stride=8), :],
            words[pl.ds(2 * x + 1, SHARDS, stride=8), :],
        )
        valid.append((RANKS * share + x).astype(f32) < counts)
        scores.append(jnp.where(valid[-1], some, -1e30))
    top = jnp.max(jnp.maximum(jnp.maximum(scores[0], scores[1]), scores[2]), axis=0, keepdims=True)
    top = top.astype(bf16).astype(f32)
    parts = [jnp.where(v, jnp.exp(s - top), 0.0) for s, v in zip(scores, valid)]
    mass = jnp.sum(parts[0] + parts[1] + parts[2], axis=0, keepdims=True)
    lane16 = iota((8, LANES), 1) >> 4
    packed = jnp.zeros((8, LANES), f32)
    for m in range(8):
        some = raw[pl.ds(m * 8 + 6, 8, stride=64), :]
        some = pltpu.roll(some, m * 16, 1) if m else some
        packed = jnp.where(lane16 == m, some, packed)
    sums = jnp.concatenate([top] + thirds(mass) + thirds(total) + [jnp.zeros_like(top)], axis=0)
    message = jnp.concatenate(parts + [packed, sums], axis=0).astype(bf16)
    for copy in range(4):
        out_ref[copy] = message


def call(kernel, name, outs, scratch, *args):
    vmem = pl.BlockSpec(memory_space=pltpu.VMEM)
    return pl.pallas_call(
        kernel,
        out_shape=tuple(jax.ShapeDtypeStruct(shape, kind) for shape, kind in outs),
        in_specs=[vmem] * len(args),
        out_specs=(vmem,) * len(outs),
        scratch_shapes=[pltpu.VMEM(shape, kind) for shape, kind in scratch],
        compiler_params=pltpu.CompilerParams(vmem_limit_bytes=40 * 1024 * 1024),
        name=name,
    )(*args)


def score(msg, own, other):
    outs = [((512, LANES), f32)] + [((8, LANES), f32)] * 2 + [((512, LANES), bf16)]
    return call(score_kernel, "score", outs, [], msg, own, other)


def words(msg, emit_kept, z_part, z_other):
    outs = [((4, XROWS, LANES), bf16)]
    scratch = [((512, LANES), f32)] * 2
    return call(words_kernel, "words", outs, scratch, msg, emit_kept, z_part, z_other)[0]


def pick_kernel(
    exps_ref, swap_ref, all_ref, panel_ref, spare_ref, trans_ref, emit_ref, full_ref,
    halves, table, emits, next_rows, word_rows, blocks, keys, stage,
):
    share = lax.axis_index("seq")
    order = [(g & 1) * 4 + (g >> 1) for g in range(8)]
    sums = [all_ref[n, 200:208, :].astype(f32) for n in order]
    total = jnp.zeros((1, LANES), f32)
    top = sums[0][0:1, :]
    full = jnp.zeros((8, LANES), f32)
    for g in range(8):
        total = total + (sums[g][4:5, :] + sums[g][5:6, :] + sums[g][6:7, :])
        top = jnp.maximum(top, sums[g][0:1, :])
        full = jnp.maximum(full, all_ref[order[g], 192:200, :].astype(f32))
    mass = jnp.zeros((1, LANES), f32)
    for g in range(8):
        part = sums[g][1:2, :] + sums[g][2:3, :] + sums[g][3:4, :]
        mass = mass + part * jnp.exp(sums[g][0:1, :] - top)
    full = jnp.where((iota((8, LANES), 1) & 15) == 14, full, 0.0)
    full = jnp.max(jnp.max(full, axis=0, keepdims=True), axis=1, keepdims=True)
    full_ref[...] = full.astype(i32)
    trans_ref[...] = jnp.log(total)
    emit_norm = top + jnp.log(mass)
    emit_ref[...] = emit_norm
    for g in range(8):
        rows = slice((g & 3) * 192, (g & 3) * 192 + 192)
        lanes = slice((g >> 2) * LANES, (g >> 2) * LANES + LANES)
        scale = jnp.exp(sums[g][0:1, :] - emit_norm)
        emits[rows, lanes] = (all_ref[order[g], 0:192, :].astype(f32) * scale).astype(bf16)
    odd = lax.axis_index("state") & 1
    halves[pl.ds(pl.multiple_of(odd * 512, 512), 512), :] = exps_ref[...]
    halves[pl.ds(pl.multiple_of((1 - odd) * 512, 512), 512), :] = swap_ref[...].astype(f32)
    low = iota((LANES, LANES), 1) < KW
    for pair in range(4):
        start = (pair >> 1) * 512 + (pair & 1) * 2
        first = halves[pl.ds(start, LANES, stride=4), :] / total
        second = halves[pl.ds(start + 1, LANES, stride=4), :] / total
        lanes = slice(pair * LANES, (pair + 1) * LANES)
        table[0:LANES, lanes] = jnp.where(low, first, pltpu.roll(second, KW, 1)).astype(bf16)
        table[LANES:, lanes] = jnp.where(low, pltpu.roll(first, KW, 1), second).astype(bf16)
    row, lane = iota((512, LANES), 0), iota((512, LANES), 1)
    pick_row, pick_lane = iota((512, 64), 0), iota((512, 64), 1)
    mine = ((lane >> 4) == ((row >> 3) & 7)) & ((lane & 3) == (row >> 7))
    next_at = mine & ((lane & 15) < 4)
    key_at = mine & ((lane & 15) >= 4) & ((lane & 15) < 12)
    ones = jnp.ones((LANES, LANES), bf16)
    weights = jnp.where((iota((LANES, LANES), 0) & 15) >= 8, 64.0, 1.0).astype(bf16)
    asked = jnp.concatenate([all_ref[n, 192:200, :].astype(f32) for n in order], axis=0)
    asked = asked.astype(bf16)
    lane_f = lane.astype(f32)
    row_of = lane & (KW - 1)
    for step in range(4):
        source = (pick_row & 7) * 8 + step * 2 + ((pick_row >> 6) & 1)
        spread = jnp.dot(one_hot(pick_lane == source), asked, preferred_element_type=f32)
        block = jnp.dot(
            jnp.where(next_at, spread, 0.0).astype(bf16), ones, preferred_element_type=f32
        )
        key = jnp.dot(
            jnp.where(key_at, spread, 0.0).astype(bf16), weights, preferred_element_type=f32
        )
        blocks[step * 512 : (step + 1) * 512, :] = block
        keys[step * 512 : (step + 1) * 512, :] = key
    for step in range(4):
        rows = slice(step * 512, (step + 1) * 512)
        block, key = blocks[rows, :], keys[rows, :]
        second = key >= 2048.0
        key = jnp.where(second, key - 2048.0, key)
        key = jnp.where(key >= 768.0, key - 768.0, key)
        hit = block == lane_f
        next_rows[rows, :LANES] = one_hot(hit & ~second)
        next_rows[rows, LANES:] = one_hot(hit & second)
        for n in range(6):
            word_rows[rows, n * LANES : (n + 1) * LANES] = one_hot(key == lane_f + float(n * LANES))
    for step in range(4):
        rows = slice(step * 512, (step + 1) * 512)
        got = jnp.dot(word_rows[rows, :], emits[...], preferred_element_type=f32)
        panels = jnp.dot(next_rows[rows, :], table[...], preferred_element_type=f32)
        block, key = blocks[rows, :], keys[rows, :]
        second = key >= 2048.0
        late = jnp.where(second, key - 2048.0, key) >= 768.0
        emit = jnp.where(late, got[:, LANES:], got[:, :LANES])
        emit = jnp.where((lane_f < float(KW)) ^ second, emit, pltpu.roll(emit, KW, 1))
        last = block == float(LANES)
        for pair in range(4):
            column = (pair * 2 + (lane >> 6)) * 8 + share
            panel = panels[:, pair * LANES : (pair + 1) * LANES]
            panel = jnp.where(last & (row_of == column), 1.0, panel) * emit
            for n in range(SLOTS):
                stage[pl.ds(step * 2048 + n * 512 + pair, LANES, stride=4), :] = panel[
                    n * LANES : (n + 1) * LANES, :
                ]
        for n in range(SLOTS):
            block = stage[step * 2048 + n * 512 : step * 2048 + (n + 1) * 512, :]
            block = block.reshape(LANES, 4, LANES).astype(bf16)
            if n < SENT:
                panel_ref[step * LANES : (step + 1) * LANES, :, n * LANES : (n + 1) * LANES] = block
            else:
                spare_ref[step * LANES : (step + 1) * LANES, :, :] = block


def pick(exps, swapped, everything):
    vmem = pl.BlockSpec(memory_space=pltpu.VMEM)
    return pl.pallas_call(
        pick_kernel,
        out_shape=(
            jax.ShapeDtypeStruct((512, 4, SENT * LANES), bf16),
            jax.ShapeDtypeStruct((512, 4, LANES), bf16),
            jax.ShapeDtypeStruct((1, LANES), f32),
            jax.ShapeDtypeStruct((1, LANES), f32),
            jax.ShapeDtypeStruct((1, 1), i32),
        ),
        in_specs=[vmem] * 3,
        out_specs=(vmem,) * 5,
        scratch_shapes=[
            pltpu.VMEM((1024, LANES), f32),
            pltpu.VMEM((256, 512), bf16),
            pltpu.VMEM((768, 256), bf16),
            pltpu.VMEM((2048, 256), bf16),
            pltpu.VMEM((2048, 768), bf16),
            pltpu.VMEM((2048, LANES), f32),
            pltpu.VMEM((2048, LANES), f32),
            pltpu.VMEM((8192, LANES), f32),
        ],
        compiler_params=pltpu.CompilerParams(vmem_limit_bytes=40 * 1024 * 1024),
        name="pick",
    )(exps, swapped, everything)


def chain_kernel(slot_ref, full_ref, panel_ref, spare_ref, out_ref, wide, ping, pong, logs, tops):
    length = slot_ref.shape[1]

    def widen(ref, lane, n, i):
        got = ref[pl.ds(pl.multiple_of(i * 32, 32), 32), :, lane : lane + LANES].astype(f32)
        rows = pl.ds(pl.multiple_of(n * 4096 + i * 256, 256), 256)
        wide[rows, :] = jnp.concatenate([got, got], axis=1).reshape(256, LANES)

    def widen_sent(i, _):
        for n in range(SENT):
            widen(panel_ref, n * LANES, n, i)
        return 0

    def widen_spare(i, _):
        widen(spare_ref, 0, SENT, i)
        return 0

    lax.fori_loop(0, panel_ref.shape[0] // 32, widen_sent, 0)

    @pl.when(full_ref[0, 0] > 0)
    def _():
        lax.fori_loop(0, panel_ref.shape[0] // 32, widen_spare, 0)

    low = iota((8, LANES), 1) < KW

    def build(i, _):
        for u in range(8):
            t = i * 8 + u
            start = slot_ref[0, t]
            parts = [wide[pl.ds(start + pair, 8, stride=8), :] for pair in range(4)]
            top = jnp.maximum(jnp.maximum(parts[0], parts[1]), jnp.maximum(parts[2], parts[3]))
            logs[pl.ds(t, 1), :] = jnp.max(top, axis=0, keepdims=True)
            move = []
            for part in parts:
                move += [jnp.where(low, part, 0.0), jnp.where(low, pltpu.roll(part, KW, 1), 0.0)]
            ping[t] = jnp.concatenate(move, axis=0).astype(bf16)
        return 0

    lax.fori_loop(0, length // 8, build, 0, unroll=2)
    peak = jnp.max(logs[0:length, :], axis=1, keepdims=True)
    tops[...] = jnp.broadcast_to((1.0 / peak).astype(bf16).astype(f32), (length, LANES))
    logs[0:length, :] = 1.0 / tops[...]
    logs[length:, :] = jnp.ones((length, LANES), f32)
    src, dst, count, base = ping, pong, length // 2, length
    while count > 1:
        unroll = min(count, 32)

        def level(i, _, src=src, dst=dst, unroll=unroll, base=base, first=src is ping and base == length):
            for u in range(unroll):
                n = i * unroll + u
                left, right = src[2 * n + 1][:, :KW], src[2 * n]
                if first:
                    left = left * tops[pl.ds(2 * n + 1, 1), :KW].astype(bf16)
                    right = right * tops[pl.ds(2 * n, 1), :].astype(bf16)
                prod = jnp.dot(left, right, preferred_element_type=f32)
                top = jnp.max(jnp.max(prod, axis=0, keepdims=True), axis=1, keepdims=True)
                logs[pl.ds(base + n, 1), :] = jnp.broadcast_to(top, (1, LANES))
                dst[n] = (prod * (1.0 / top)).astype(bf16)
            return 0

        lax.fori_loop(0, count // unroll, level, 0)
        src, dst, count, base = dst, src, count // 2, base + count
    prod = jnp.dot(src[1][:, :KW], src[0], preferred_element_type=f32)
    final = jnp.sum(jnp.sum(prod, axis=0, keepdims=True), axis=1, keepdims=True)
    scale = jnp.sum(jnp.log(logs[...]), axis=0, keepdims=True)
    total = jnp.log(final) + scale - jnp.log(jnp.full((1, LANES), 8192.0, f32))
    out_ref[...] = total[:, :1] / length


def chain(slots, full, panels, spare):
    length = slots.shape[1]
    vmem = pl.BlockSpec(memory_space=pltpu.VMEM)
    smem = pl.BlockSpec(memory_space=pltpu.SMEM)
    return pl.pallas_call(
        chain_kernel,
        out_shape=jax.ShapeDtypeStruct((1, 1), f32),
        in_specs=[smem, smem, vmem, vmem],
        out_specs=vmem,
        scratch_shapes=[
            pltpu.VMEM((SLOTS * 4096, LANES), f32),
            pltpu.VMEM((length, KW, LANES), bf16),
            pltpu.VMEM((length // 2, KW, LANES), bf16),
            pltpu.VMEM((2 * length, LANES), f32),
            pltpu.VMEM((length, LANES), f32),
        ],
        compiler_params=pltpu.CompilerParams(vmem_limit_bytes=40 * 1024 * 1024),
        name="chain",
    )(slots, full, panels, spare)


def local(
    emit_states, trans_out, trans_in, word_emb, word_cluster, cluster_block, kept_parts, tokens
):
    msg, out_kept, emit_kept, slots = prep(
        kept_parts, tokens, word_cluster, cluster_block, emit_states, trans_out, trans_in, word_emb
    )
    pairs = [(i, i ^ 1) for i in range(SHARDS)]
    other = lax.ppermute(out_kept, "state", pairs)
    arrived = lax.all_to_all(msg, "state", split_axis=0, concat_axis=0, tiled=True)
    exps, z_part, z_swap, swap = score(arrived, out_kept, other)
    z_other = lax.ppermute(z_swap, "state", pairs)
    swapped = lax.ppermute(swap, "state", pairs)
    mine = words(arrived, emit_kept, z_part, z_other)
    along_x = lax.all_to_all(
        mine, "seq", split_axis=0, concat_axis=0, tiled=True,
        axis_index_groups=[[0, 2, 4, 6], [1, 3, 5, 7]],
    )
    everything = lax.all_gather(
        along_x, "seq", axis=0, tiled=True, axis_index_groups=[[0, 1], [2, 3], [4, 5], [6, 7]]
    )
    panels, spare, trans_norm, emit_norm, full = pick(exps, swapped, everything)

    def exchange(value):
        return lax.all_to_all(value, ("state", "seq"), split_axis=0, concat_axis=0, tiled=True)

    got = exchange(panels)
    spare = lax.cond(full.reshape(()) > 0, exchange, lambda value: value, spare)
    token_loglik = chain(slots, full, got, spare)
    return (token_loglik.reshape(1), trans_norm.reshape(-1), emit_norm.reshape(-1))


def solution(mesh):
    placed = (
        P("state", None),
        P("state", None),
        P("state", None),
        P("state", None),
        P(),
        P(),
        P(),
        P(("state", "seq"), None),
    )
    return jax.shard_map(
        local,
        mesh=mesh,
        in_specs=placed,
        out_specs=(P(("state", "seq")), P("state"), P("state")),
        check_vma=False,
    )
```

```python
import jax
import jax.numpy as jnp
from jax import lax
from jax.experimental import pallas as pl
from jax.experimental.pallas import tpu as pltpu
from jax.sharding import PartitionSpec as P

BS = 256
PART = 32
KW = 64
LANES = 128
RANKS = 3
SHARDS = 64
SLOTS = 4
SENT = 3
ROWS = 16
SWAP = 528
XROWS = 208
f32 = jnp.float32
bf16 = jnp.bfloat16
i32 = jnp.int32


def iota(shape, axis):
    return lax.broadcasted_iota(i32, shape, axis)


def one_hot(mask):
    return jnp.where(mask, 1.0, 0.0).astype(bf16)


def ints(mask, value):
    return jnp.where(mask, value, 0)


def prep_kernel(
    parts_ref, token_ref, tokens_hbm, cluster_hbm, table_hbm, emit_hbm, out_hbm, in_hbm, word_hbm,
    msg_ref, out_kept, emit_kept, slot_ref,
    in_kept, slot_of, near, wide, counts_of, tokens_ref, cluster_ref, table_ref, word_ref, chosen, sems,
):
    me = lax.axis_index("state")
    share = lax.axis_index("seq")
    head = []
    for n, (src, dst) in enumerate(
        ((cluster_hbm, cluster_ref), (table_hbm, table_ref), (tokens_hbm, tokens_ref))
    ):
        head.append(pltpu.make_async_copy(src, dst, sems.at[n]))
        head[-1].start()
    word_copy = pltpu.make_async_copy(word_hbm, word_ref, sems.at[3])
    word_copy.start()
    kept = []
    for blk in range(2):
        for part in range(2):
            start = blk * BS + parts_ref[part, me * 2 + blk] * PART
            src = pl.ds(pl.multiple_of(start, PART), PART)
            at = (blk * 2 + part) * PART
            for which, (hbm, ref, to) in enumerate(
                ((in_hbm, in_kept, at), (out_hbm, out_kept, at), (emit_hbm, emit_kept, at))
            ):
                sem = sems.at[4 + (blk * 2 + part) * 3 + which]
                kept.append(pltpu.make_async_copy(hbm.at[src, :], ref.at[pl.ds(to, PART), :], sem))
                kept[-1].start()
    for copy in head:
        copy.wait()
    sub = iota((LANES, LANES), 0)
    lane = iota((LANES, LANES), 1)
    eye = sub == lane

    def column(row):
        return jnp.sum(ints(eye, row), axis=1, keepdims=True)

    def line(col):
        return jnp.sum(ints(eye, col), axis=0, keepdims=True)

    sums = jnp.concatenate([one_hot(sub < lane), jnp.ones((LANES, LANES), bf16)], axis=1)
    block_row = table_ref[...]
    block_col = column(block_row)
    block_col_f = block_col.astype(f32)
    carry = jnp.zeros((LANES, LANES), f32)
    chunks = 2048 // LANES
    own = pl.multiple_of(me * chunks, chunks)
    own_rows = cluster_ref[pl.ds(own, chunks), :]
    for c in range(chunks):
        hit = sub == own_rows[c : c + 1, :]
        found = jnp.dot(one_hot(hit), sums, preferred_element_type=f32)
        before = found[:, :LANES] + carry
        carry = carry + found[:, LANES:]
        rank = jnp.sum(jnp.where(hit, before, 0.0), axis=0, keepdims=True).astype(i32)
        block = jnp.sum(jnp.where(hit, block_col_f, 0.0), axis=0, keepdims=True).astype(i32)
        x = rank - RANKS * share
        slot = (block >> 1) * 8 + x * 2 + (block & 1)
        slot_of[c : c + 1, :] = jnp.where((x >= 0) & (x < RANKS), slot, -1)
    counts_of[...] = carry

    length = token_ref.shape[1]

    for t in range(length):
        near[t : t + 1, :] = cluster_ref[pl.ds(token_ref[0, t] >> 7, 1), :]
    token_col = column(tokens_ref[...])
    cluster_col = jnp.sum(ints(lane == (token_col & 127), near[...]), axis=1, keepdims=True)
    near[...] = jnp.broadcast_to(cluster_col, (LANES, LANES))
    place = iota((chunks, LANES), 0) * LANES + iota((chunks, LANES), 1)

    for t in range(length):
        token = token_ref[0, t]
        shard_rows = cluster_ref[pl.ds(pl.multiple_of((token >> 11) * chunks, chunks), chunks), :]
        earlier = (shard_rows == near[t : t + 1, :]) & (place < (token & 2047))
        wide[t : t + 1, :] = jnp.sum(ints(earlier, 1), axis=0, keepdims=True)
    rank_col = jnp.sum(wide[...], axis=1, keepdims=True)
    own_block_col = jnp.sum(ints(lane == cluster_col, block_row), axis=1, keepdims=True)
    own_block_row = line(own_block_col)
    same = (own_block_col >> 1) == (own_block_row >> 1)
    times_col = jnp.sum(ints(same & (lane < sub), 1), axis=1, keepdims=True)
    times_row = jnp.sum(ints(same & (sub < lane), 1), axis=0, keepdims=True)
    slot_ref[...] = times_row * 4096 + (own_block_row >> 1) * 64
    following = jnp.sum(ints(lane == sub + 1, own_block_row), axis=1, keepdims=True)
    following = jnp.where(iota((LANES, 1), 0) == length - 1, LANES, following)
    slots_col = (own_block_col >> 1) * SLOTS + times_col
    asked = jnp.zeros((SHARDS, LANES), f32)
    slot_line = iota((LANES, 2 * LANES), 1)
    at_slot = slot_line == slots_col
    owner = (iota((SHARDS, 2 * LANES), 1) >> 2) == iota((SHARDS, 2 * LANES), 0)
    slot_sub = iota((2 * LANES, LANES), 0) & 3
    slot_lane = iota((2 * LANES, LANES), 1)
    for field, values in enumerate((following, token_col >> 11, rank_col + 32 * (own_block_col & 1))):
        value_row = jnp.sum(ints(at_slot, values), axis=0, keepdims=True)
        spread = jnp.where(owner, value_row.astype(f32), 0.0).astype(bf16)
        asked += jnp.dot(
            spread, one_hot(slot_lane == field * 4 + slot_sub), preferred_element_type=f32
        )
    count_lane = jnp.where(lane == 12 + (block_col & 1), counts_of[...], 0.0).astype(bf16)
    count_owner = one_hot((block_row >> 1) == iota((SHARDS, LANES), 0))
    asked += jnp.dot(count_owner, count_lane, preferred_element_type=f32)
    full = jnp.max(times_row, axis=1, keepdims=True) >= SENT
    asked += jnp.where(full & (iota((SHARDS, LANES), 1) == 14), 1.0, 0.0)

    for copy in kept:
        copy.wait()
    row = iota((16, LANES), 0)
    want = ((row >> 2) & 1) * KW + ((row >> 3) * 4 + (row & 3)) * 8 + share
    targets = jnp.dot(
        one_hot(iota((16, LANES), 1) == want), in_kept[...], preferred_element_type=f32
    )
    for tile in range(4):
        for c in range(chunks):
            chosen[tile * LANES : (tile + 1) * LANES, c * LANES : (c + 1) * LANES] = one_hot(
                sub + tile * LANES == slot_of[c : c + 1, :]
            )
    word_copy.wait()
    request_row = iota((8, LANES), 0) == 6
    words = jnp.dot(chosen[...], word_ref[...], preferred_element_type=f32)
    for to in range(SHARDS):
        mine = words[to * 8 : to * 8 + 8, :]
        first = jnp.where(request_row, asked[to : to + 1, :], mine[:, :LANES])
        mine = jnp.concatenate([first, mine[:, LANES:]], axis=1)
        head = targets[(to & 1) * 8 : (to & 1) * 8 + 8, :]
        msg_ref[to] = jnp.concatenate([head, mine], axis=0).astype(bf16)


def prep(kept_parts, tokens, word_cluster, cluster_block, emit_states, trans_out, trans_in, word_emb):
    width = emit_states.shape[1]
    vmem = pl.BlockSpec(memory_space=pltpu.VMEM)
    smem = pl.BlockSpec(memory_space=pltpu.SMEM)
    clusters = word_cluster.reshape(-1, LANES)
    return pl.pallas_call(
        prep_kernel,
        out_shape=(
            jax.ShapeDtypeStruct((SHARDS, ROWS, width), bf16),
            jax.ShapeDtypeStruct((2 * KW, width), bf16),
            jax.ShapeDtypeStruct((2 * KW, width), bf16),
            jax.ShapeDtypeStruct((1, LANES), i32),
        ),
        in_specs=[smem, smem] + [pl.BlockSpec(memory_space=pltpu.HBM)] * 7,
        out_specs=(vmem,) * 4,
        scratch_shapes=[
            pltpu.VMEM((2 * KW, width), bf16),
            pltpu.VMEM((16, LANES), i32),
            pltpu.VMEM((LANES, LANES), i32),
            pltpu.VMEM((LANES, LANES), i32),
            pltpu.VMEM((LANES, LANES), f32),
            pltpu.VMEM((1, LANES), i32),
            pltpu.VMEM(clusters.shape, i32),
            pltpu.VMEM((1, LANES), i32),
            pltpu.VMEM(word_emb.shape, bf16),
            pltpu.VMEM((8 * SHARDS, word_emb.shape[0]), bf16),
            pltpu.SemaphoreType.DMA((16,)),
        ],
        compiler_params=pltpu.CompilerParams(vmem_limit_bytes=60 * 1024 * 1024),
        name="prep",
    )(
        kept_parts.T, tokens, tokens, clusters, cluster_block[None, :],
        emit_states, trans_out, trans_in, word_emb,
    )


def thirds(value):
    high = value.astype(bf16).astype(f32)
    mid = (value - high).astype(bf16).astype(f32)
    return [high, mid, value - high - mid]


def score_kernel(msg_ref, own_ref, other_ref, exps_ref, z_ref, swap_ref):
    states = jnp.concatenate([own_ref[...], other_ref[...]], axis=0)
    total = jnp.zeros((1, 2 * LANES), f32)
    for tile in range(4):
        got = msg_ref[tile * 16 : tile * 16 + 16].reshape(16 * ROWS, msg_ref.shape[2])
        res = lax.dot_general(
            got, states, (((1,), (1,)), ((), ())), preferred_element_type=f32
        ).reshape(16, ROWS, 2 * LANES)
        exps = jnp.exp(res[:, :8, :]).reshape(LANES, 2 * LANES)
        total = total + jnp.sum(exps, axis=0, keepdims=True)
        rows = slice(tile * LANES, (tile + 1) * LANES)
        exps_ref[rows, :] = exps[:, :LANES]
        swap_ref[rows, :] = jnp.minimum(exps[:, LANES:], 3.38e38).astype(bf16)
    z_ref[...] = jnp.broadcast_to(total[:, :LANES], (8, LANES))
    sums = thirds(total[:, LANES:]) + [jnp.zeros((13, LANES), f32)]
    swap_ref[512:SWAP, :] = jnp.concatenate(sums, axis=0).astype(bf16)


def words_kernel(msg_ref, emit_ref, z_ref, swap_ref, out_ref, words, raw):
    share = lax.axis_index("seq")
    sums = swap_ref[512:SWAP, :].astype(f32)
    total = z_ref[0:1, :] + (sums[0:1, :] + sums[1:2, :] + sums[2:3, :])
    for tile in range(4):
        got = msg_ref[tile * 16 : tile * 16 + 16].reshape(16 * ROWS, msg_ref.shape[2])
        res = lax.dot_general(
            got, emit_ref[...], (((1,), (1,)), ((), ())), preferred_element_type=f32
        ).reshape(16, ROWS, LANES)
        rows = slice(tile * LANES, (tile + 1) * LANES)
        words[rows, :] = res[:, 8:, :].reshape(LANES, LANES)
        some = got[:, :LANES].astype(f32).reshape(16, ROWS, LANES)
        raw[rows, :] = some[:, 8:, :].reshape(LANES, LANES)
    asked = raw[pl.ds(6, SHARDS, stride=8), :]
    spread = one_hot(iota((LANES, LANES), 0) == 12 + (iota((LANES, LANES), 1) >> 6))
    counts = jnp.dot(asked.astype(bf16), spread, preferred_element_type=f32)
    low = iota((SHARDS, LANES), 1) < KW
    scores, valid = [], []
    for x in range(RANKS):
        some = jnp.where(
            low,
            words[pl.ds(2 * x, SHARDS, stride=8), :],
            words[pl.ds(2 * x + 1, SHARDS, stride=8), :],
        )
        valid.append((RANKS * share + x).astype(f32) < counts)
        scores.append(jnp.where(valid[-1], some, -1e30))
    top = jnp.max(jnp.maximum(jnp.maximum(scores[0], scores[1]), scores[2]), axis=0, keepdims=True)
    top = top.astype(bf16).astype(f32)
    parts = [jnp.where(v, jnp.exp(s - top), 0.0) for s, v in zip(scores, valid)]
    mass = jnp.sum(parts[0] + parts[1] + parts[2], axis=0, keepdims=True)
    lane16 = iota((8, LANES), 1) >> 4
    packed = jnp.zeros((8, LANES), f32)
    for m in range(8):
        some = raw[pl.ds(m * 8 + 6, 8, stride=64), :]
        some = pltpu.roll(some, m * 16, 1) if m else some
        packed = jnp.where(lane16 == m, some, packed)
    sums = jnp.concatenate([top] + thirds(mass) + thirds(total) + [jnp.zeros_like(top)], axis=0)
    message = jnp.concatenate(parts + [packed, sums], axis=0).astype(bf16)
    for copy in range(4):
        out_ref[copy] = message


def call(kernel, name, outs, scratch, *args):
    vmem = pl.BlockSpec(memory_space=pltpu.VMEM)
    return pl.pallas_call(
        kernel,
        out_shape=tuple(jax.ShapeDtypeStruct(shape, kind) for shape, kind in outs),
        in_specs=[vmem] * len(args),
        out_specs=(vmem,) * len(outs),
        scratch_shapes=[pltpu.VMEM(shape, kind) for shape, kind in scratch],
        compiler_params=pltpu.CompilerParams(vmem_limit_bytes=40 * 1024 * 1024),
        name=name,
    )(*args)


def score(msg, own, other):
    outs = [((512, LANES), f32), ((8, LANES), f32), ((SWAP, LANES), bf16)]
    return call(score_kernel, "score", outs, [], msg, own, other)


def words(msg, emit_kept, z_part, swapped):
    outs = [((4, XROWS, LANES), bf16)]
    scratch = [((512, LANES), f32)] * 2
    return call(words_kernel, "words", outs, scratch, msg, emit_kept, z_part, swapped)[0]


def pick_slots(asked, share, first, count, outs, table, emits, next_rows, word_rows, stage):
    size = count * LANES
    row, lane = iota((size, LANES), 0), iota((size, LANES), 1)
    pick_row, pick_lane = iota((size, 64), 0), iota((size, 64), 1)
    mine = ((lane >> 4) == ((row >> 3) & 7)) & ((lane & 3) == (row >> 7) + first)
    next_at = mine & ((lane & 15) < 4)
    key_at = mine & ((lane & 15) >= 4) & ((lane & 15) < 12)
    ones = jnp.ones((LANES, LANES), bf16)
    weights = jnp.where((iota((LANES, LANES), 0) & 15) >= 8, 64.0, 1.0).astype(bf16)
    lane_f = lane.astype(f32)
    row_of = lane & (KW - 1)
    found = []
    for step in range(4):
        source = (pick_row & 7) * 8 + step * 2 + ((pick_row >> 6) & 1)
        spread = jnp.dot(one_hot(pick_lane == source), asked, preferred_element_type=f32)
        block = jnp.dot(
            jnp.where(next_at, spread, 0.0).astype(bf16), ones, preferred_element_type=f32
        )
        key = jnp.dot(
            jnp.where(key_at, spread, 0.0).astype(bf16), weights, preferred_element_type=f32
        )
        found.append((block, key))
    for step in range(4):
        rows = slice(step * size, (step + 1) * size)
        block, key = found[step]
        second = key >= 2048.0
        key = jnp.where(second, key - 2048.0, key)
        key = jnp.where(key >= 768.0, key - 768.0, key)
        hit = block == lane_f
        next_rows[rows, :LANES] = one_hot(hit & ~second)
        next_rows[rows, LANES:] = one_hot(hit & second)
        for n in range(6):
            word_rows[rows, n * LANES : (n + 1) * LANES] = one_hot(key == lane_f + float(n * LANES))
    for step in range(4):
        rows = slice(step * size, (step + 1) * size)
        got = jnp.dot(word_rows[rows, :], emits[...], preferred_element_type=f32)
        panels = jnp.dot(next_rows[rows, :], table[...], preferred_element_type=f32)
        block, key = found[step]
        second = key >= 2048.0
        late = jnp.where(second, key - 2048.0, key) >= 768.0
        emit = jnp.where(late, got[:, LANES:], got[:, :LANES])
        emit = jnp.where((lane_f < float(KW)) ^ second, emit, pltpu.roll(emit, KW, 1))
        last = block == float(LANES)
        base = step * 4 * size
        for pair in range(4):
            column = (pair * 2 + (lane >> 6)) * 8 + share
            panel = panels[:, pair * LANES : (pair + 1) * LANES]
            panel = jnp.where(last & (row_of == column), 1.0, panel) * emit
            for n in range(count):
                stage[pl.ds(base + n * 512 + pair, LANES, stride=4), :] = panel[
                    n * LANES : (n + 1) * LANES, :
                ]
        for n in range(count):
            block = stage[base + n * 512 : base + (n + 1) * 512, :]
            block = block.reshape(LANES, 4, LANES).astype(bf16)
            outs[0][step * LANES : (step + 1) * LANES, :, n * LANES : (n + 1) * LANES] = block


def pick_kernel(
    exps_ref, swap_ref, all_ref, panel_ref, spare_ref, trans_ref, emit_ref, full_ref,
    halves, table, emits, next_rows, word_rows, stage,
):
    share = lax.axis_index("seq")
    order = [(g & 1) * 4 + (g >> 1) for g in range(8)]
    sums = [all_ref[n, 200:208, :].astype(f32) for n in order]
    total = jnp.zeros((1, LANES), f32)
    top = sums[0][0:1, :]
    full = jnp.zeros((8, LANES), f32)
    for g in range(8):
        total = total + (sums[g][4:5, :] + sums[g][5:6, :] + sums[g][6:7, :])
        top = jnp.maximum(top, sums[g][0:1, :])
        full = jnp.maximum(full, all_ref[order[g], 192:200, :].astype(f32))
    mass = jnp.zeros((1, LANES), f32)
    for g in range(8):
        part = sums[g][1:2, :] + sums[g][2:3, :] + sums[g][3:4, :]
        mass = mass + part * jnp.exp(sums[g][0:1, :] - top)
    full = jnp.where((iota((8, LANES), 1) & 15) == 14, full, 0.0)
    full = jnp.max(jnp.max(full, axis=0, keepdims=True), axis=1, keepdims=True)
    full_ref[...] = full.astype(i32)
    trans_ref[...] = jnp.log(total)
    emit_norm = top + jnp.log(mass)
    emit_ref[...] = emit_norm
    for g in range(8):
        rows = slice((g & 3) * 192, (g & 3) * 192 + 192)
        lanes = slice((g >> 2) * LANES, (g >> 2) * LANES + LANES)
        scale = jnp.exp(sums[g][0:1, :] - emit_norm)
        emits[rows, lanes] = (all_ref[order[g], 0:192, :].astype(f32) * scale).astype(bf16)
    odd = lax.axis_index("state") & 1
    halves[pl.ds(pl.multiple_of(odd * 512, 512), 512), :] = exps_ref[...]
    halves[pl.ds(pl.multiple_of((1 - odd) * 512, 512), 512), :] = swap_ref[0:512, :].astype(f32)
    low = iota((LANES, LANES), 1) < KW
    for pair in range(4):
        start = (pair >> 1) * 512 + (pair & 1) * 2
        first = halves[pl.ds(start, LANES, stride=4), :] / total
        second = halves[pl.ds(start + 1, LANES, stride=4), :] / total
        lanes = slice(pair * LANES, (pair + 1) * LANES)
        table[0:LANES, lanes] = jnp.where(low, first, pltpu.roll(second, KW, 1)).astype(bf16)
        table[LANES:, lanes] = jnp.where(low, pltpu.roll(first, KW, 1), second).astype(bf16)
    asked = jnp.concatenate([all_ref[n, 192:200, :].astype(f32) for n in order], axis=0)
    asked = asked.astype(bf16)
    pick_slots(asked, share, 0, SENT, (panel_ref,), table, emits, next_rows, word_rows, stage)

    @pl.when(jnp.max(full) > 0.5)
    def _():
        pick_slots(
            asked, share, SENT, SLOTS - SENT, (spare_ref,), table, emits, next_rows, word_rows, stage
        )


def pick(exps, swapped, everything):
    vmem = pl.BlockSpec(memory_space=pltpu.VMEM)
    return pl.pallas_call(
        pick_kernel,
        out_shape=(
            jax.ShapeDtypeStruct((512, 4, SENT * LANES), bf16),
            jax.ShapeDtypeStruct((512, 4, LANES), bf16),
            jax.ShapeDtypeStruct((1, LANES), f32),
            jax.ShapeDtypeStruct((1, LANES), f32),
            jax.ShapeDtypeStruct((1, 1), i32),
        ),
        in_specs=[vmem] * 3,
        out_specs=(vmem,) * 5,
        scratch_shapes=[
            pltpu.VMEM((1024, LANES), f32),
            pltpu.VMEM((256, 512), bf16),
            pltpu.VMEM((768, 256), bf16),
            pltpu.VMEM((2048, 256), bf16),
            pltpu.VMEM((2048, 768), bf16),
            pltpu.VMEM((8192, LANES), f32),
        ],
        compiler_params=pltpu.CompilerParams(vmem_limit_bytes=40 * 1024 * 1024),
        name="pick",
    )(exps, swapped, everything)


def chain_kernel(slot_ref, panel_ref, spare_ref, out_ref, wide, ping, pong, logs, tops):
    length = slot_ref.shape[1]

    def widen(i, _):
        some = pl.ds(pl.multiple_of(i * 32, 32), 32)
        for n in range(SLOTS):
            if n < SENT:
                got = panel_ref[some, :, n * LANES : (n + 1) * LANES].astype(f32)
            else:
                got = spare_ref[some, :, :].astype(f32)
            rows = pl.ds(pl.multiple_of(n * 4096 + i * 256, 256), 256)
            wide[rows, :] = jnp.concatenate([got, got], axis=1).reshape(256, LANES)
        return 0

    lax.fori_loop(0, panel_ref.shape[0] // 32, widen, 0)
    low = iota((8, LANES), 1) < KW

    def build(i, _):
        for u in range(8):
            t = i * 8 + u
            start = slot_ref[0, t]
            parts = [wide[pl.ds(start + pair, 8, stride=8), :] for pair in range(4)]
            top = jnp.maximum(jnp.maximum(parts[0], parts[1]), jnp.maximum(parts[2], parts[3]))
            logs[pl.ds(t, 1), :] = jnp.max(top, axis=0, keepdims=True)
            move = []
            for part in parts:
                move += [jnp.where(low, part, 0.0), jnp.where(low, pltpu.roll(part, KW, 1), 0.0)]
            ping[t] = jnp.concatenate(move, axis=0).astype(bf16)
        return 0

    lax.fori_loop(0, length // 8, build, 0, unroll=4)
    peak = jnp.max(logs[0:length, :], axis=1, keepdims=True)
    tops[...] = jnp.broadcast_to((1.0 / peak).astype(bf16).astype(f32), (length, LANES))
    logs[0:length, :] = 1.0 / tops[...]
    logs[length:, :] = jnp.ones((length, LANES), f32)
    src, dst, count, base = ping, pong, length // 2, length
    while count > 1:
        unroll = min(count, 64)

        def level(i, _, src=src, dst=dst, unroll=unroll, base=base, first=src is ping and base == length):
            for u in range(unroll):
                n = i * unroll + u
                left, right = src[2 * n + 1][:, :KW], src[2 * n]
                if first:
                    left = left * tops[pl.ds(2 * n + 1, 1), :KW].astype(bf16)
                    right = right * tops[pl.ds(2 * n, 1), :].astype(bf16)
                prod = jnp.dot(left, right, preferred_element_type=f32)
                top = jnp.max(jnp.max(prod, axis=0, keepdims=True), axis=1, keepdims=True)
                logs[pl.ds(base + n, 1), :] = jnp.broadcast_to(top, (1, LANES))
                dst[n] = (prod * (1.0 / top)).astype(bf16)
            return 0

        lax.fori_loop(0, count // unroll, level, 0)
        src, dst, count, base = dst, src, count // 2, base + count
    prod = jnp.dot(src[1][:, :KW], src[0], preferred_element_type=f32)
    final = jnp.sum(jnp.sum(prod, axis=0, keepdims=True), axis=1, keepdims=True)
    scale = jnp.sum(jnp.log(logs[...]), axis=0, keepdims=True)
    total = jnp.log(final) + scale - jnp.log(jnp.full((1, LANES), 8192.0, f32))
    out_ref[...] = total[:, :1] / length


def chain(slots, panels, spare):
    length = slots.shape[1]
    vmem = pl.BlockSpec(memory_space=pltpu.VMEM)
    return pl.pallas_call(
        chain_kernel,
        out_shape=jax.ShapeDtypeStruct((1, 1), f32),
        in_specs=[pl.BlockSpec(memory_space=pltpu.SMEM), vmem, vmem],
        out_specs=vmem,
        scratch_shapes=[
            pltpu.VMEM((SLOTS * 4096, LANES), f32),
            pltpu.VMEM((length, KW, LANES), bf16),
            pltpu.VMEM((length // 2, KW, LANES), bf16),
            pltpu.VMEM((2 * length, LANES), f32),
            pltpu.VMEM((length, LANES), f32),
        ],
        compiler_params=pltpu.CompilerParams(vmem_limit_bytes=40 * 1024 * 1024),
        name="chain",
    )(slots, panels, spare)


def local(
    emit_states, trans_out, trans_in, word_emb, word_cluster, cluster_block, kept_parts, tokens
):
    msg, out_kept, emit_kept, slots = prep(
        kept_parts, tokens, word_cluster, cluster_block, emit_states, trans_out, trans_in, word_emb
    )
    pairs = [(i, i ^ 1) for i in range(SHARDS)]
    other = lax.ppermute(out_kept, "state", pairs)
    arrived = lax.all_to_all(msg, "state", split_axis=0, concat_axis=0, tiled=True)
    exps, z_part, swap = score(arrived, out_kept, other)
    swapped = lax.ppermute(swap, "state", pairs)
    mine = words(arrived, emit_kept, z_part, swapped)
    along_x = lax.all_to_all(
        mine, "seq", split_axis=0, concat_axis=0, tiled=True,
        axis_index_groups=[[0, 2, 4, 6], [1, 3, 5, 7]],
    )
    everything = lax.all_gather(
        along_x, "seq", axis=0, tiled=True, axis_index_groups=[[0, 1], [2, 3], [4, 5], [6, 7]]
    )
    panels, spare, trans_norm, emit_norm, full = pick(exps, swapped, everything)

    def exchange(value):
        return lax.all_to_all(value, ("state", "seq"), split_axis=0, concat_axis=0, tiled=True)

    got = exchange(panels)
    spare = lax.cond(full.reshape(()) > 0, exchange, lambda value: value, spare)
    token_loglik = chain(slots, got, spare)
    return (token_loglik.reshape(1), trans_norm.reshape(-1), emit_norm.reshape(-1))


def solution(mesh):
    placed = (
        P("state", None),
        P("state", None),
        P("state", None),
        P("state", None),
        P(),
        P(),
        P(),
        P(("state", "seq"), None),
    )
    return jax.shard_map(
        local,
        mesh=mesh,
        in_specs=placed,
        out_specs=(P(("state", "seq")), P("state"), P("state")),
        check_vma=False,
    )
```

```python
import jax
import jax.numpy as jnp
from jax import lax
from jax.experimental import pallas as pl
from jax.experimental.pallas import tpu as pltpu
from jax.sharding import PartitionSpec as P

BS = 256
PART = 32
KW = 64
LANES = 128
RANKS = 3
SHARDS = 64
SLOTS = 4
SENT = 3
ROWS = 16
SWAP = 528
XROWS = 208
f32 = jnp.float32
bf16 = jnp.bfloat16
i32 = jnp.int32


def iota(shape, axis):
    return lax.broadcasted_iota(i32, shape, axis)


def one_hot(mask):
    return jnp.where(mask, 1.0, 0.0).astype(bf16)


def ints(mask, value):
    return jnp.where(mask, value, 0)


def prep_kernel(
    parts_ref, token_ref, tokens_hbm, cluster_hbm, table_hbm, emit_hbm, out_hbm, in_hbm, word_hbm,
    msg_ref, out_kept, emit_kept, slot_ref,
    in_kept, slot_of, near, wide, counts_of, tokens_ref, cluster_ref, table_ref, word_ref, chosen, sems,
):
    me = lax.axis_index("state")
    share = lax.axis_index("seq")
    head = []
    for n, (src, dst) in enumerate(
        ((cluster_hbm, cluster_ref), (table_hbm, table_ref), (tokens_hbm, tokens_ref))
    ):
        head.append(pltpu.make_async_copy(src, dst, sems.at[n]))
        head[-1].start()
    word_copy = pltpu.make_async_copy(word_hbm, word_ref, sems.at[3])
    word_copy.start()
    kept = []
    for blk in range(2):
        for part in range(2):
            start = blk * BS + parts_ref[part, me * 2 + blk] * PART
            src = pl.ds(pl.multiple_of(start, PART), PART)
            at = (blk * 2 + part) * PART
            for which, (hbm, ref, to) in enumerate(
                ((in_hbm, in_kept, at), (out_hbm, out_kept, at), (emit_hbm, emit_kept, at))
            ):
                sem = sems.at[4 + (blk * 2 + part) * 3 + which]
                kept.append(pltpu.make_async_copy(hbm.at[src, :], ref.at[pl.ds(to, PART), :], sem))
                kept[-1].start()
    for copy in head:
        copy.wait()
    sub = iota((LANES, LANES), 0)
    lane = iota((LANES, LANES), 1)
    eye = sub == lane

    def column(row):
        return jnp.sum(ints(eye, row), axis=1, keepdims=True)

    def line(col):
        return jnp.sum(ints(eye, col), axis=0, keepdims=True)

    sums = jnp.concatenate([one_hot(sub < lane), jnp.ones((LANES, LANES), bf16)], axis=1)
    block_row = table_ref[...]
    block_col = column(block_row)
    block_col_f = block_col.astype(f32)
    carry = jnp.zeros((LANES, LANES), f32)
    chunks = 2048 // LANES
    own = pl.multiple_of(me * chunks, chunks)
    own_rows = cluster_ref[pl.ds(own, chunks), :]
    for c in range(chunks):
        hit = sub == own_rows[c : c + 1, :]
        found = jnp.dot(one_hot(hit), sums, preferred_element_type=f32)
        before = found[:, :LANES] + carry
        carry = carry + found[:, LANES:]
        rank = jnp.sum(jnp.where(hit, before, 0.0), axis=0, keepdims=True).astype(i32)
        block = jnp.sum(jnp.where(hit, block_col_f, 0.0), axis=0, keepdims=True).astype(i32)
        x = rank - RANKS * share
        slot = (block >> 1) * 8 + x * 2 + (block & 1)
        slot_of[c : c + 1, :] = jnp.where((x >= 0) & (x < RANKS), slot, -1)
    counts_of[...] = carry

    length = token_ref.shape[1]

    for t in range(length):
        near[t : t + 1, :] = cluster_ref[pl.ds(token_ref[0, t] >> 7, 1), :]
    token_col = column(tokens_ref[...])
    cluster_col = jnp.sum(ints(lane == (token_col & 127), near[...]), axis=1, keepdims=True)
    near[...] = jnp.broadcast_to(cluster_col, (LANES, LANES))
    place = iota((chunks, LANES), 0) * LANES + iota((chunks, LANES), 1)

    for t in range(length):
        token = token_ref[0, t]
        shard_rows = cluster_ref[pl.ds(pl.multiple_of((token >> 11) * chunks, chunks), chunks), :]
        earlier = (shard_rows == near[t : t + 1, :]) & (place < (token & 2047))
        wide[t : t + 1, :] = jnp.sum(ints(earlier, 1), axis=0, keepdims=True)
    rank_col = jnp.sum(wide[...], axis=1, keepdims=True)
    own_block_col = jnp.sum(ints(lane == cluster_col, block_row), axis=1, keepdims=True)
    own_block_row = line(own_block_col)
    same = (own_block_col >> 1) == (own_block_row >> 1)
    times_col = jnp.sum(ints(same & (lane < sub), 1), axis=1, keepdims=True)
    times_row = jnp.sum(ints(same & (sub < lane), 1), axis=0, keepdims=True)
    slot_ref[...] = times_row * 4096 + (own_block_row >> 1) * 64
    following = jnp.sum(ints(lane == sub + 1, own_block_row), axis=1, keepdims=True)
    following = jnp.where(iota((LANES, 1), 0) == length - 1, LANES, following)
    slots_col = (own_block_col >> 1) * SLOTS + times_col
    asked = jnp.zeros((SHARDS, LANES), f32)
    slot_line = iota((LANES, 2 * LANES), 1)
    at_slot = slot_line == slots_col
    owner = (iota((SHARDS, 2 * LANES), 1) >> 2) == iota((SHARDS, 2 * LANES), 0)
    slot_sub = iota((2 * LANES, LANES), 0) & 3
    slot_lane = iota((2 * LANES, LANES), 1)
    for field, values in enumerate((following, token_col >> 11, rank_col + 32 * (own_block_col & 1))):
        value_row = jnp.sum(ints(at_slot, values), axis=0, keepdims=True)
        spread = jnp.where(owner, value_row.astype(f32), 0.0).astype(bf16)
        asked += jnp.dot(
            spread, one_hot(slot_lane == field * 4 + slot_sub), preferred_element_type=f32
        )
    count_lane = jnp.where(lane == 12 + (block_col & 1), counts_of[...], 0.0).astype(bf16)
    count_owner = one_hot((block_row >> 1) == iota((SHARDS, LANES), 0))
    asked += jnp.dot(count_owner, count_lane, preferred_element_type=f32)
    full = jnp.max(times_row, axis=1, keepdims=True) >= SENT
    asked += jnp.where(full & (iota((SHARDS, LANES), 1) == 14), 1.0, 0.0)

    for copy in kept:
        copy.wait()
    row = iota((16, LANES), 0)
    want = ((row >> 2) & 1) * KW + ((row >> 3) * 4 + (row & 3)) * 8 + share
    targets = jnp.dot(
        one_hot(iota((16, LANES), 1) == want), in_kept[...], preferred_element_type=f32
    )
    for tile in range(4):
        for c in range(chunks):
            chosen[tile * LANES : (tile + 1) * LANES, c * LANES : (c + 1) * LANES] = one_hot(
                sub + tile * LANES == slot_of[c : c + 1, :]
            )
    word_copy.wait()
    request_row = iota((8, LANES), 0) == 6
    words = jnp.dot(chosen[...], word_ref[...], preferred_element_type=f32)
    for to in range(SHARDS):
        mine = words[to * 8 : to * 8 + 8, :]
        first = jnp.where(request_row, asked[to : to + 1, :], mine[:, :LANES])
        mine = jnp.concatenate([first, mine[:, LANES:]], axis=1)
        head = targets[(to & 1) * 8 : (to & 1) * 8 + 8, :]
        msg_ref[to] = jnp.concatenate([head, mine], axis=0).astype(bf16)


def prep(kept_parts, tokens, word_cluster, cluster_block, emit_states, trans_out, trans_in, word_emb):
    width = emit_states.shape[1]
    vmem = pl.BlockSpec(memory_space=pltpu.VMEM)
    smem = pl.BlockSpec(memory_space=pltpu.SMEM)
    clusters = word_cluster.reshape(-1, LANES)
    return pl.pallas_call(
        prep_kernel,
        out_shape=(
            jax.ShapeDtypeStruct((SHARDS, ROWS, width), bf16),
            jax.ShapeDtypeStruct((2 * KW, width), bf16),
            jax.ShapeDtypeStruct((2 * KW, width), bf16),
            jax.ShapeDtypeStruct((1, LANES), i32),
        ),
        in_specs=[smem, smem] + [pl.BlockSpec(memory_space=pltpu.HBM)] * 7,
        out_specs=(vmem,) * 4,
        scratch_shapes=[
            pltpu.VMEM((2 * KW, width), bf16),
            pltpu.VMEM((16, LANES), i32),
            pltpu.VMEM((LANES, LANES), i32),
            pltpu.VMEM((LANES, LANES), i32),
            pltpu.VMEM((LANES, LANES), f32),
            pltpu.VMEM((1, LANES), i32),
            pltpu.VMEM(clusters.shape, i32),
            pltpu.VMEM((1, LANES), i32),
            pltpu.VMEM(word_emb.shape, bf16),
            pltpu.VMEM((8 * SHARDS, word_emb.shape[0]), bf16),
            pltpu.SemaphoreType.DMA((16,)),
        ],
        compiler_params=pltpu.CompilerParams(vmem_limit_bytes=60 * 1024 * 1024),
        name="prep",
    )(
        kept_parts.T, tokens, tokens, clusters, cluster_block[None, :],
        emit_states, trans_out, trans_in, word_emb,
    )


def thirds(value):
    high = value.astype(bf16).astype(f32)
    mid = (value - high).astype(bf16).astype(f32)
    return [high, mid, value - high - mid]


def score_kernel(msg_ref, own_ref, other_ref, exps_ref, z_ref, swap_ref):
    states = jnp.concatenate([own_ref[...], other_ref[...]], axis=0)
    total = jnp.zeros((1, 2 * LANES), f32)
    for tile in range(4):
        got = msg_ref[tile * 16 : tile * 16 + 16].reshape(16 * ROWS, msg_ref.shape[2])
        res = lax.dot_general(
            got, states, (((1,), (1,)), ((), ())), preferred_element_type=f32
        ).reshape(16, ROWS, 2 * LANES)
        exps = jnp.exp(res[:, :8, :]).reshape(LANES, 2 * LANES)
        total = total + jnp.sum(exps, axis=0, keepdims=True)
        rows = slice(tile * LANES, (tile + 1) * LANES)
        exps_ref[rows, :] = exps[:, :LANES]
        swap_ref[rows, :] = jnp.minimum(exps[:, LANES:], 3.38e38).astype(bf16)
    z_ref[...] = jnp.broadcast_to(total[:, :LANES], (8, LANES))
    sums = thirds(total[:, LANES:]) + [jnp.zeros((13, LANES), f32)]
    swap_ref[512:SWAP, :] = jnp.concatenate(sums, axis=0).astype(bf16)


def words_kernel(msg_ref, emit_ref, z_ref, swap_ref, out_ref, words, raw):
    share = lax.axis_index("seq")
    sums = swap_ref[512:SWAP, :].astype(f32)
    total = z_ref[0:1, :] + (sums[0:1, :] + sums[1:2, :] + sums[2:3, :])
    for tile in range(4):
        got = msg_ref[tile * 16 : tile * 16 + 16].reshape(16 * ROWS, msg_ref.shape[2])
        res = lax.dot_general(
            got, emit_ref[...], (((1,), (1,)), ((), ())), preferred_element_type=f32
        ).reshape(16, ROWS, LANES)
        rows = slice(tile * LANES, (tile + 1) * LANES)
        words[rows, :] = res[:, 8:, :].reshape(LANES, LANES)
        some = got[:, :LANES].astype(f32).reshape(16, ROWS, LANES)
        raw[rows, :] = some[:, 8:, :].reshape(LANES, LANES)
    asked = raw[pl.ds(6, SHARDS, stride=8), :]
    spread = one_hot(iota((LANES, LANES), 0) == 12 + (iota((LANES, LANES), 1) >> 6))
    counts = jnp.dot(asked.astype(bf16), spread, preferred_element_type=f32)
    low = iota((SHARDS, LANES), 1) < KW
    scores, valid = [], []
    for x in range(RANKS):
        some = jnp.where(
            low,
            words[pl.ds(2 * x, SHARDS, stride=8), :],
            words[pl.ds(2 * x + 1, SHARDS, stride=8), :],
        )
        valid.append((RANKS * share + x).astype(f32) < counts)
        scores.append(jnp.where(valid[-1], some, -1e30))
    top = jnp.max(jnp.maximum(jnp.maximum(scores[0], scores[1]), scores[2]), axis=0, keepdims=True)
    top = top.astype(bf16).astype(f32)
    parts = [jnp.where(v, jnp.exp(s - top), 0.0) for s, v in zip(scores, valid)]
    mass = jnp.sum(parts[0] + parts[1] + parts[2], axis=0, keepdims=True)
    lane16 = iota((8, LANES), 1) >> 4
    packed = jnp.zeros((8, LANES), f32)
    for m in range(8):
        some = raw[pl.ds(m * 8 + 6, 8, stride=64), :]
        some = pltpu.roll(some, m * 16, 1) if m else some
        packed = jnp.where(lane16 == m, some, packed)
    sums = jnp.concatenate([top] + thirds(mass) + thirds(total) + [jnp.zeros_like(top)], axis=0)
    message = jnp.concatenate(parts + [packed, sums], axis=0).astype(bf16)
    for copy in range(4):
        out_ref[copy] = message


def call(kernel, name, outs, scratch, *args):
    vmem = pl.BlockSpec(memory_space=pltpu.VMEM)
    return pl.pallas_call(
        kernel,
        out_shape=tuple(jax.ShapeDtypeStruct(shape, kind) for shape, kind in outs),
        in_specs=[vmem] * len(args),
        out_specs=(vmem,) * len(outs),
        scratch_shapes=[pltpu.VMEM(shape, kind) for shape, kind in scratch],
        compiler_params=pltpu.CompilerParams(vmem_limit_bytes=40 * 1024 * 1024),
        name=name,
    )(*args)


def score(msg, own, other):
    outs = [((512, LANES), f32), ((8, LANES), f32), ((SWAP, LANES), bf16)]
    return call(score_kernel, "score", outs, [], msg, own, other)


def words(msg, emit_kept, z_part, swapped):
    outs = [((4, XROWS, LANES), bf16)]
    scratch = [((576, LANES), f32)] * 2
    return call(words_kernel, "words", outs, scratch, msg, emit_kept, z_part, swapped)[0]


def pick_slots(asked, share, first, count, outs, table, emits, next_rows, word_rows, stage):
    size = count * LANES
    row, lane = iota((size, LANES), 0), iota((size, LANES), 1)
    pick_row, pick_lane = iota((size, 64), 0), iota((size, 64), 1)
    mine = ((lane >> 4) == ((row >> 3) & 7)) & ((lane & 3) == (row >> 7) + first)
    next_at = mine & ((lane & 15) < 4)
    key_at = mine & ((lane & 15) >= 4) & ((lane & 15) < 12)
    ones = jnp.ones((LANES, LANES), bf16)
    weights = jnp.where((iota((LANES, LANES), 0) & 15) >= 8, 64.0, 1.0).astype(bf16)
    lane_f = lane.astype(f32)
    row_of = lane & (KW - 1)
    found = []
    for step in range(4):
        source = (pick_row & 7) * 8 + step * 2 + ((pick_row >> 6) & 1)
        spread = jnp.dot(one_hot(pick_lane == source), asked, preferred_element_type=f32)
        block = jnp.dot(
            jnp.where(next_at, spread, 0.0).astype(bf16), ones, preferred_element_type=f32
        )
        key = jnp.dot(
            jnp.where(key_at, spread, 0.0).astype(bf16), weights, preferred_element_type=f32
        )
        found.append((block, key))
    for step in range(4):
        rows = slice(step * size, (step + 1) * size)
        block, key = found[step]
        second = key >= 2048.0
        key = jnp.where(second, key - 2048.0, key)
        key = jnp.where(key >= 768.0, key - 768.0, key)
        hit = block == lane_f
        next_rows[rows, :LANES] = one_hot(hit & ~second)
        next_rows[rows, LANES:] = one_hot(hit & second)
        for n in range(6):
            word_rows[rows, n * LANES : (n + 1) * LANES] = one_hot(key == lane_f + float(n * LANES))
    for step in range(4):
        rows = slice(step * size, (step + 1) * size)
        got = jnp.dot(word_rows[rows, :], emits[...], preferred_element_type=f32)
        panels = jnp.dot(next_rows[rows, :], table[...], preferred_element_type=f32)
        block, key = found[step]
        second = key >= 2048.0
        late = jnp.where(second, key - 2048.0, key) >= 768.0
        emit = jnp.where(late, got[:, LANES:], got[:, :LANES])
        emit = jnp.where((lane_f < float(KW)) ^ second, emit, pltpu.roll(emit, KW, 1))
        last = block == float(LANES)
        base = step * 4 * size
        for pair in range(4):
            column = (pair * 2 + (lane >> 6)) * 8 + share
            panel = panels[:, pair * LANES : (pair + 1) * LANES]
            panel = jnp.where(last & (row_of == column), 1.0, panel) * emit
            for n in range(count):
                stage[pl.ds(base + n * 512 + pair, LANES, stride=4), :] = panel[
                    n * LANES : (n + 1) * LANES, :
                ]
        for n in range(count):
            block = stage[base + n * 512 : base + (n + 1) * 512, :]
            block = block.reshape(LANES, 4, LANES).astype(bf16)
            outs[0][step * LANES : (step + 1) * LANES, :, n * LANES : (n + 1) * LANES] = block


def pick_kernel(
    exps_ref, swap_ref, all_ref, panel_ref, spare_ref, trans_ref, emit_ref, full_ref,
    halves, table, emits, next_rows, word_rows, stage,
):
    share = lax.axis_index("seq")
    order = [(g & 1) * 4 + (g >> 1) for g in range(8)]
    sums = [all_ref[n, 200:208, :].astype(f32) for n in order]
    total = jnp.zeros((1, LANES), f32)
    top = sums[0][0:1, :]
    full = jnp.zeros((8, LANES), f32)
    for g in range(8):
        total = total + (sums[g][4:5, :] + sums[g][5:6, :] + sums[g][6:7, :])
        top = jnp.maximum(top, sums[g][0:1, :])
        full = jnp.maximum(full, all_ref[order[g], 192:200, :].astype(f32))
    mass = jnp.zeros((1, LANES), f32)
    for g in range(8):
        part = sums[g][1:2, :] + sums[g][2:3, :] + sums[g][3:4, :]
        mass = mass + part * jnp.exp(sums[g][0:1, :] - top)
    full = jnp.where((iota((8, LANES), 1) & 15) == 14, full, 0.0)
    full = jnp.max(jnp.max(full, axis=0, keepdims=True), axis=1, keepdims=True)
    full_ref[...] = full.astype(i32)
    trans_ref[...] = jnp.log(total)
    emit_norm = top + jnp.log(mass)
    emit_ref[...] = emit_norm
    for g in range(8):
        rows = slice((g & 3) * 192, (g & 3) * 192 + 192)
        lanes = slice((g >> 2) * LANES, (g >> 2) * LANES + LANES)
        scale = jnp.exp(sums[g][0:1, :] - emit_norm)
        emits[rows, lanes] = (all_ref[order[g], 0:192, :].astype(f32) * scale).astype(bf16)
    odd = lax.axis_index("state") & 1
    halves[pl.ds(pl.multiple_of(odd * 512, 512), 512), :] = exps_ref[...]
    halves[pl.ds(pl.multiple_of((1 - odd) * 512, 512), 512), :] = swap_ref[0:512, :].astype(f32)
    low = iota((LANES, LANES), 1) < KW
    for pair in range(4):
        start = (pair >> 1) * 512 + (pair & 1) * 2
        first = halves[pl.ds(start, LANES, stride=4), :] / total
        second = halves[pl.ds(start + 1, LANES, stride=4), :] / total
        lanes = slice(pair * LANES, (pair + 1) * LANES)
        table[0:LANES, lanes] = jnp.where(low, first, pltpu.roll(second, KW, 1)).astype(bf16)
        table[LANES:, lanes] = jnp.where(low, pltpu.roll(first, KW, 1), second).astype(bf16)
    asked = jnp.concatenate([all_ref[n, 192:200, :].astype(f32) for n in order], axis=0)
    asked = asked.astype(bf16)
    pick_slots(asked, share, 0, SENT, (panel_ref,), table, emits, next_rows, word_rows, stage)

    @pl.when(jnp.max(full) > 0.5)
    def _():
        pick_slots(
            asked, share, SENT, SLOTS - SENT, (spare_ref,), table, emits, next_rows, word_rows, stage
        )


def pick(exps, swapped, everything):
    vmem = pl.BlockSpec(memory_space=pltpu.VMEM)
    return pl.pallas_call(
        pick_kernel,
        out_shape=(
            jax.ShapeDtypeStruct((512, 4, SENT * LANES), bf16),
            jax.ShapeDtypeStruct((512, 4, LANES), bf16),
            jax.ShapeDtypeStruct((1, LANES), f32),
            jax.ShapeDtypeStruct((1, LANES), f32),
            jax.ShapeDtypeStruct((1, 1), i32),
        ),
        in_specs=[vmem] * 3,
        out_specs=(vmem,) * 5,
        scratch_shapes=[
            pltpu.VMEM((1032, LANES), f32),
            pltpu.VMEM((256, 512), bf16),
            pltpu.VMEM((768, 256), bf16),
            pltpu.VMEM((2048, 256), bf16),
            pltpu.VMEM((2048, 768), bf16),
            pltpu.VMEM((8200, LANES), f32),
        ],
        compiler_params=pltpu.CompilerParams(vmem_limit_bytes=40 * 1024 * 1024),
        name="pick",
    )(exps, swapped, everything)


def chain_kernel(slot_ref, panel_ref, spare_ref, out_ref, wide, ping, pong, logs, tops):
    length = slot_ref.shape[1]

    def widen(i, _):
        some = pl.ds(pl.multiple_of(i * 32, 32), 32)
        for n in range(SLOTS):
            if n < SENT:
                got = panel_ref[some, :, n * LANES : (n + 1) * LANES].astype(f32)
            else:
                got = spare_ref[some, :, :].astype(f32)
            rows = pl.ds(pl.multiple_of(n * 4096 + i * 256, 256), 256)
            wide[rows, :] = jnp.concatenate([got, got], axis=1).reshape(256, LANES)
        return 0

    lax.fori_loop(0, panel_ref.shape[0] // 32, widen, 0)
    low = iota((8, LANES), 1) < KW

    def build(i, _):
        for u in range(8):
            t = i * 8 + u
            start = slot_ref[0, t]
            parts = [wide[pl.ds(start + pair, 8, stride=8), :] for pair in range(4)]
            top = jnp.maximum(jnp.maximum(parts[0], parts[1]), jnp.maximum(parts[2], parts[3]))
            logs[pl.ds(t, 1), :] = jnp.max(top, axis=0, keepdims=True)
            move = []
            for part in parts:
                move += [jnp.where(low, part, 0.0), jnp.where(low, pltpu.roll(part, KW, 1), 0.0)]
            ping[t] = jnp.concatenate(move, axis=0).astype(bf16)
        return 0

    lax.fori_loop(0, length // 8, build, 0, unroll=4)
    peak = jnp.max(logs[0:length, :], axis=1, keepdims=True)
    tops[...] = jnp.broadcast_to((1.0 / peak).astype(bf16).astype(f32), (length, LANES))
    logs[0:length, :] = 1.0 / tops[...]
    logs[length:, :] = jnp.ones((length, LANES), f32)
    src, dst, count, base = ping, pong, length // 2, length
    while count > 1:
        unroll = min(count, 64)

        def level(i, _, src=src, dst=dst, unroll=unroll, base=base, first=src is ping and base == length):
            for u in range(unroll):
                n = i * unroll + u
                left, right = src[2 * n + 1][:, :KW], src[2 * n]
                if first:
                    left = left * tops[pl.ds(2 * n + 1, 1), :KW].astype(bf16)
                    right = right * tops[pl.ds(2 * n, 1), :].astype(bf16)
                prod = jnp.dot(left, right, preferred_element_type=f32)
                top = jnp.max(jnp.max(prod, axis=0, keepdims=True), axis=1, keepdims=True)
                logs[pl.ds(base + n, 1), :] = jnp.broadcast_to(top, (1, LANES))
                dst[n] = (prod * (1.0 / top)).astype(bf16)
            return 0

        lax.fori_loop(0, count // unroll, level, 0)
        src, dst, count, base = dst, src, count // 2, base + count
    prod = jnp.dot(src[1][:, :KW], src[0], preferred_element_type=f32)
    final = jnp.sum(jnp.sum(prod, axis=0, keepdims=True), axis=1, keepdims=True)
    scale = jnp.sum(jnp.log(logs[...]), axis=0, keepdims=True)
    total = jnp.log(final) + scale - jnp.log(jnp.full((1, LANES), 8192.0, f32))
    out_ref[...] = total[:, :1] / length


def chain(slots, panels, spare):
    length = slots.shape[1]
    vmem = pl.BlockSpec(memory_space=pltpu.VMEM)
    return pl.pallas_call(
        chain_kernel,
        out_shape=jax.ShapeDtypeStruct((1, 1), f32),
        in_specs=[pl.BlockSpec(memory_space=pltpu.SMEM), vmem, vmem],
        out_specs=vmem,
        scratch_shapes=[
            pltpu.VMEM((SLOTS * 4096 + 64, LANES), f32),
            pltpu.VMEM((length, KW, LANES), bf16),
            pltpu.VMEM((length // 2, KW, LANES), bf16),
            pltpu.VMEM((2 * length, LANES), f32),
            pltpu.VMEM((length, LANES), f32),
        ],
        compiler_params=pltpu.CompilerParams(vmem_limit_bytes=40 * 1024 * 1024),
        name="chain",
    )(slots, panels, spare)


def local(
    emit_states, trans_out, trans_in, word_emb, word_cluster, cluster_block, kept_parts, tokens
):
    msg, out_kept, emit_kept, slots = prep(
        kept_parts, tokens, word_cluster, cluster_block, emit_states, trans_out, trans_in, word_emb
    )
    pairs = [(i, i ^ 1) for i in range(SHARDS)]
    other = lax.ppermute(out_kept, "state", pairs)
    arrived = lax.all_to_all(msg, "state", split_axis=0, concat_axis=0, tiled=True)
    exps, z_part, swap = score(arrived, out_kept, other)
    swapped = lax.ppermute(swap, "state", pairs)
    mine = words(arrived, emit_kept, z_part, swapped)
    along_x = lax.all_to_all(
        mine, "seq", split_axis=0, concat_axis=0, tiled=True,
        axis_index_groups=[[0, 2, 4, 6], [1, 3, 5, 7]],
    )
    everything = lax.all_gather(
        along_x, "seq", axis=0, tiled=True, axis_index_groups=[[0, 1], [2, 3], [4, 5], [6, 7]]
    )
    panels, spare, trans_norm, emit_norm, full = pick(exps, swapped, everything)

    def exchange(value):
        return lax.all_to_all(value, ("state", "seq"), split_axis=0, concat_axis=0, tiled=True)

    got = exchange(panels)
    spare = lax.cond(full.reshape(()) > 0, exchange, lambda value: value, spare)
    token_loglik = chain(slots, got, spare)
    return (token_loglik.reshape(1), trans_norm.reshape(-1), emit_norm.reshape(-1))


def solution(mesh):
    placed = (
        P("state", None),
        P("state", None),
        P("state", None),
        P("state", None),
        P(),
        P(),
        P(),
        P(("state", "seq"), None),
    )
    return jax.shard_map(
        local,
        mesh=mesh,
        in_specs=placed,
        out_specs=(P(("state", "seq")), P("state"), P("state")),
        check_vma=False,
    )
```
